32 devices in a mesh: dp: 8 (over y, x, core), mp: 4 (over z).
Axes of the slice: x: 2, y: 2, z: 4, core: 2. Of those that a mesh axis runs over, the one named last changes fastest.
Arguments:
- tokens: bfloat16 [8192, 768], P('dp'), may hold values from -6 to 6
- segment_ids: int32 [16, 512], P('dp'), may hold values from 0 to 3, never falling along the last dimension, each value on 1 to 256 neighbouring positions
- buckets: int32 [512, 512], replicated, may hold values from 0 to 319
- qkv_weight: bfloat16 [3, 768, 768], P(None, None, 'mp'), may hold values from -0.21875 to 0.21875
- qv_bias: float32 [2, 768], P(None, 'mp'), may hold values from -3 to 3
- rel_table: float32 [320, 12], P(None, 'mp'), may hold values from -3 to 3
- gate_weight: bfloat16 [64, 8], replicated, may hold values from -0.375 to 0.375
- gate_bias: float32 [8], replicated, may hold values from -2 to 2
- gate_scale: float32 [12], P('mp'), may hold values from 0.5 to 2.5
- out_weight: bfloat16 [768, 768], P('mp'), may hold values from -1.25 to 1.25
- out_bias: float32 [768], replicated, may hold values from -3 to 3
- ln1_gain: float32 [768], replicated, may hold values from 0.1 to 1.9
- ln1_bias: float32 [768], replicated, may hold values from -3 to 3
- fc1_weight: bfloat16 [768, 3072], P(None, 'mp'), may hold values from -0.21875 to 0.21875
- fc1_bias: float32 [3072], P('mp'), may hold values from -3 to 3
- fc2_weight: bfloat16 [3072, 768], P('mp'), may hold values from -0.21875 to 0.21875
- fc2_bias: float32 [768], replicated, may hold values from -3 to 3
- ln2_gain: float32 [768], replicated, may hold values from 0.1 to 1.9
- ln2_bias: float32 [768], replicated, may hold values from -3 to 3
- grad_out: bfloat16 [8192, 768], P('dp'), may hold values from -6 to 6
Outputs:
- output: float32 [8192, 768], P('dp')
- input_grad: float32 [8192, 768], P('dp')
- grad_qkv_weight: float32 [3, 768, 768], P(None, None, 'mp')
- grad_qv_bias: float32 [2, 768], P(None, 'mp')
- grad_rel_table: float32 [320, 12], P(None, 'mp')
- grad_gate_weight: float32 [64, 8], replicated
- grad_gate_bias: float32 [8], replicated
- grad_gate_scale: float32 [12], P('mp')
- grad_out_weight: float32 [768, 768], P('mp')
- grad_out_bias: float32 [768], replicated
- grad_ln1_gain: float32 [768], replicated
- grad_ln1_bias: float32 [768], replicated
- grad_fc1_weight: float32 [768, 3072], P(None, 'mp')
- grad_fc1_bias: float32 [3072], P('mp')
- grad_fc2_weight: float32 [3072, 768], P('mp')
- grad_fc2_bias: float32 [768], replicated
- grad_ln2_gain: float32 [768], replicated
- grad_ln2_bias: float32 [768], replicated
The draws below stay inside these ranges and needn't reach their ends.
Inputs may be any that keep to these rules, and one draw needn't show every extreme that they name: `segment_ids`: segment numbers never fall along a row of 512 patches, and a segment holds at most 256 patches. `buckets`: one bucket for each pair of positions, the same for every row.
All inputs are finite; a program needn't handle non-finite values.
Results may differ from the reference program's by a relative error of at most 0.02.
Values may be sent and summed in bfloat16 or wider, within the bound.
No kernel may reach another device: no remote copies, remote signals or barrier semaphores. Data moves between devices by JAX's collectives and lax.ppermute only.
A program may use at most 320 MiB of HBM per device.

```python
import math
from functools import partial
import jax
import jax.numpy as jnp
import numpy as np
from jax import lax

D = 768
H = 12
HD = 64
FF = 3072
NB = 320
GATE = 8
SEQ = 512
TOKENS = 8192
SEQS = 16


def plant(values, key, least, top_value):
    extent = values.shape
    spot = [jax.random.randint(jax.random.fold_in(key, axis), (), 0, extent[axis]) for axis in range(len(extent))]
    values = values.at[tuple(spot)].set(least)
    longest = extent.index(max(extent))
    spot[longest] = (spot[longest] + 1) % extent[longest]
    return values.at[tuple(spot)].set(top_value)


def block_scale(stream_key, extent, cuts, least, high):
    level = 1.0
    for position, parts in cuts:
        steps = jax.random.uniform(jax.random.fold_in(jax.random.fold_in(stream_key, 6), position), (parts,), jnp.float32, least / len(cuts), high / len(cuts))
        level = level * jnp.repeat(jnp.exp(steps), extent[position] // parts).reshape((-1,) + (1,) * (len(extent) - 1 - position))
    return level


def profile(amount, total, reach, slope):
    loads = [(1 << 20) // math.isqrt(rank ** slope) + 1 for rank in range(2, amount + 1)]
    surplus, holding = total - reach - (amount - 1), [1] * (amount - 1)
    while surplus > 0:
        candidates = [i for i in range(amount - 1) if holding[i] < reach]
        mass, remaining = sum([loads[i] for i in candidates]), surplus
        for i in candidates:
            addition = min(reach - holding[i], max(1, remaining * loads[i] // mass), surplus)
            holding[i] = holding[i] + addition
            surplus = surplus - addition
    return np.array([reach] + holding)


def ragged(stream_key, amount, total, limit, skew):
    if amount == 2:
        one = jax.random.randint(stream_key, (), max(1, total - limit), min(limit, total - 1) + 1)
        return jnp.stack([one, total - one])
    tallies = jnp.asarray(profile(amount, total, limit, skew), jnp.int32)
    twos = (amount - 1) // 2
    source_of, receiver = tallies[1:1 + 2 * twos:2], tallies[2:2 + 2 * twos:2]
    room = jnp.minimum(source_of - 1, limit - receiver)
    shifted = jax.random.randint(jax.random.fold_in(stream_key, 1), (twos,), 0, 1 << 20) % (room + 1)
    tallies = tallies.at[1:1 + 2 * twos:2].set(source_of - shifted).at[2:2 + 2 * twos:2].set(receiver + shifted)
    return tallies[jax.random.permutation(jax.random.fold_in(stream_key, 2), amount)]


def bell_draw(key, shape, deviation, bound, shards=(), dtype=jnp.bfloat16):
    entries = deviation * jax.random.normal(key, shape, jnp.float32)
    if shards:
        entries = entries * block_scale(key, shape, shards, -0.22, 0.18)
    return jnp.clip(entries, -bound, bound).astype(dtype)


def setup_inputs(seed: int = 0) -> dict:
    key_of = jax.random.split(jax.random.key(seed), 21)
    return {
        "tokens": bell_draw(key_of[0], (TOKENS, D), 1.0, 6.0, ((0, 8),)),
        "segment_ids": jax.vmap(lambda own: jnp.searchsorted(jnp.cumsum(ragged(own, 4, SEQ, SEQ // 2, 2)), jnp.arange(SEQ), side="right"))(jax.random.split(key_of[1], SEQS)).reshape((SEQS, SEQ)).astype(jnp.int32),
        "buckets": plant(jax.random.randint(key_of[2], (SEQ, SEQ), 0, NB), jax.random.fold_in(key_of[2], 1), 0, NB - 1).astype(jnp.int32),
        "qkv_weight": bell_draw(key_of[3], (3, D, D), D ** -0.5, 0.21875, ((2, 4),)),
        "qv_bias": bell_draw(key_of[4], (2, D), 0.5, 3.0, ((1, 4),), jnp.float32),
        "rel_table": bell_draw(key_of[5], (NB, H), 0.5, 3.0, ((1, 4),), jnp.float32),
        "gate_weight": bell_draw(key_of[6], (HD, GATE), (HD * 4) ** -0.5, 0.375),
        "gate_bias": bell_draw(key_of[7], (GATE,), 0.3, 2.0, (), jnp.float32),
        "gate_scale": jnp.clip(0.5 + 2.0 * jax.random.uniform(key_of[8], (H,), jnp.float32) ** block_scale(key_of[8], (H,), ((0, 4),), -0.2, 0.2), 0.5, 2.5),
        "out_weight": bell_draw(key_of[9], (D, D), (D // 32) ** -0.5, 1.25, ((0, 4),)),
        "out_bias": bell_draw(key_of[10], (D,), 0.5, 3.0, (), jnp.float32),
        "ln1_gain": jnp.clip(1.0 + 0.18 * jax.random.normal(key_of[11], (D,), jnp.float32), 0.1, 1.9),
        "ln1_bias": bell_draw(key_of[12], (D,), 0.5, 3.0, (), jnp.float32),
        "fc1_weight": bell_draw(key_of[13], (D, FF), D ** -0.5, 0.21875, ((1, 4),)),
        "fc1_bias": bell_draw(key_of[14], (FF,), 0.5, 3.0, ((0, 4),), jnp.float32),
        "fc2_weight": bell_draw(key_of[15], (FF, D), (FF // 4) ** -0.5, 0.21875, ((0, 4),)),
        "fc2_bias": bell_draw(key_of[16], (D,), 0.5, 3.0, (), jnp.float32),
        "ln2_gain": jnp.clip(1.0 + 0.18 * jax.random.normal(key_of[17], (D,), jnp.float32), 0.1, 1.9),
        "ln2_bias": bell_draw(key_of[18], (D,), 0.5, 3.0, (), jnp.float32),
        "grad_out": bell_draw(key_of[19], (TOKENS, D), 1.0, 6.0, ((0, 8),)),
    }


highest = lax.Precision.HIGHEST
norm_eps = 1e-05
deep_alpha = 24.0 ** 0.25
masked_score = -1e+30

@jax.custom_vjp
def low(v):
    return lax.optimization_barrier(v.astype(jnp.bfloat16)).astype(jnp.float32)

@jax.custom_vjp
def low_back(v):
    return v

def low_keep(v):
    return (low(v), None)

def low_pass(kept, grad):
    return (grad,)

def back_keep(v):
    return (v, None)

def back_low(kept, grad):
    return (low(grad),)
low.defvjp(low_keep, low_pass)
low_back.defvjp(back_keep, back_low)

def layer_norm(values_in, gain, shift):
    mean_row = lax.optimization_barrier(jnp.mean(values_in, axis=-1, keepdims=True))
    centred = values_in - mean_row
    spread = lax.optimization_barrier(jnp.mean(centred * centred, axis=-1, keepdims=True))
    return centred * lax.rsqrt(spread + norm_eps) * gain + shift

def gate_values(heads_in, gate_weight, gate_bias, gate_scale):
    gate_lin = jnp.einsum('thc,cg->thg', heads_in, gate_weight, precision=highest) + gate_bias
    half = gate_lin.shape[-1] // 2
    first_gate = jax.nn.sigmoid(lax.optimization_barrier(jnp.sum(gate_lin[..., :half], axis=-1)))
    second_gate = jax.nn.sigmoid(lax.optimization_barrier(jnp.sum(gate_lin[..., half:], axis=-1)))
    return first_gate * (second_gate * gate_scale - 1.0) + 2.0

def attend_one(queries, keys_all, values_all, segment, gate, pos_bias):
    scores = jnp.einsum('qhd,khd->hqk', queries, keys_all, precision=highest) * HD ** (-0.5)
    scores = low_back(scores + jnp.swapaxes(gate, 0, 1)[:, :, None] * pos_bias)
    same = segment[:, None] == segment[None, :]
    scores = jnp.where(same[None], scores, masked_score)
    probs = low(jax.nn.softmax(scores, axis=-1))
    return jnp.einsum('hqk,khd->qhd', probs, values_all, precision=highest)

def reference(tokens, segment_ids, buckets, qkv_weight, qv_bias, rel_table, gate_weight, gate_bias, gate_scale, out_weight, out_bias, ln1_gain, ln1_bias, fc1_weight, fc1_bias, fc2_weight, fc2_bias, ln2_gain, ln2_bias, grad_out):
    group = math.gcd(SEQS, 8)
    blocks = SEQS // group

    def forward(tokens, qkv_weight, qv_bias, rel_table, gate_weight, gate_bias, gate_scale, out_weight, out_bias, ln1_gain, ln1_bias, fc1_weight, fc1_bias, fc2_weight, fc2_bias, ln2_gain, ln2_bias):
        projected = jnp.einsum('td,cde->cte', tokens, qkv_weight, precision=highest)
        queries = low(low_back(projected[0] + qv_bias[0]))
        keys_all = low(low_back(projected[1]))
        values_all = low(low_back(projected[2] + qv_bias[1]))
        gate = gate_values(tokens.reshape(TOKENS, H, HD), gate_weight, gate_bias, gate_scale)
        pos_bias = jnp.moveaxis(rel_table[buckets], 2, 0)

        def attend_group(block):
            return jax.vmap(partial(attend_one, pos_bias=pos_bias))(*block)
        shaped = tuple((member.reshape(blocks, group, SEQ, H, HD) for member in (queries, keys_all, values_all)))
        context = lax.map(jax.checkpoint(attend_group), shaped + (segment_ids.reshape(blocks, group, SEQ), gate.reshape(blocks, group, SEQ, H)))
        context = low(low_back(context.reshape(TOKENS, D)))
        attended = low_back(jnp.dot(context, out_weight, precision=highest)) + out_bias
        hidden = layer_norm(deep_alpha * tokens + attended, ln1_gain, ln1_bias)
        pre = low_back(jnp.dot(low(hidden), fc1_weight, precision=highest)) + fc1_bias
        active = low(jax.nn.gelu(pre, approximate=False))
        feed = low_back(jnp.dot(active, fc2_weight, precision=highest)) + fc2_bias
        return layer_norm(deep_alpha * hidden + feed, ln2_gain, ln2_bias)
    floats = tuple((member.astype(jnp.float32) for member in (tokens, qkv_weight, qv_bias, rel_table, gate_weight, gate_bias, gate_scale, out_weight, out_bias, ln1_gain, ln1_bias, fc1_weight, fc1_bias, fc2_weight, fc2_bias, ln2_gain, ln2_bias)))
    output, pullback = jax.vjp(forward, *floats)
    grads = pullback(grad_out.astype(jnp.float32))
    return (output, grads[0], grads[1], grads[2], grads[3], grads[4], grads[5], grads[6], grads[7], grads[8], grads[9], grads[10], grads[11], grads[12], grads[13], grads[14], grads[15], grads[16])
```

```python
import functools

import jax
import jax.numpy as jnp
from jax import lax
from jax.experimental import pallas as pl
from jax.experimental.pallas import tpu as pltpu
from jax.sharding import PartitionSpec as P

norm_eps = 1e-05
deep_alpha = 24.0**0.25
masked_score = -1e30
bf = jnp.bfloat16
f32 = jnp.float32
LANES = 128


def nn(a, b):
    return lax.dot_general(a, b, (((1,), (0,)), ((), ())), preferred_element_type=f32)


def nt(a, b):
    return lax.dot_general(a, b, (((1,), (1,)), ((), ())), preferred_element_type=f32)


def params(mib):
    return pltpu.CompilerParams(vmem_limit_bytes=mib * 1024 * 1024)


def bias_kernel(heads, chunks, buckets_ref, table_ref, out_ref):
    rows, cols = buckets_ref.shape

    def group(g, carry):
        at = pl.ds(pl.multiple_of(g * 8, 8), 8)
        for c in range(cols // LANES):
            lanes = pl.ds(c * LANES, LANES)
            idx = buckets_ref[at, lanes]
            low = idx & (LANES - 1)
            high = idx >> 7
            for h in range(heads):
                got = None
                for k in range(chunks):
                    line = jnp.broadcast_to(table_ref[h, pl.ds(k, 1), :], (8, LANES))
                    part = jnp.take_along_axis(line, low, axis=1, mode="promise_in_bounds")
                    got = part if got is None else jnp.where(high == k, part, got)
                out_ref[h, at, lanes] = got
        return carry

    lax.fori_loop(0, rows // 8, group, 0)


def bias_of(buckets_t, table):
    heads, chunks, _ = table.shape
    seq = buckets_t.shape[0]
    rows = 64
    return pl.pallas_call(
        functools.partial(bias_kernel, heads, chunks),
        grid=(seq // rows,),
        in_specs=[
            pl.BlockSpec((rows, seq), lambda i: (i, 0)),
            pl.BlockSpec((heads, chunks, LANES), lambda i: (0, 0, 0)),
        ],
        out_specs=pl.BlockSpec((heads, rows, seq), lambda i: (0, i, 0)),
        out_shape=jax.ShapeDtypeStruct((heads, seq, seq), f32),
        name="pos_bias",
    )(buckets_t, table)


def attend_kernel(
    heads, hd, gates, idx_ref, x_ref, w_ref, gb_ref, qvb_ref, pos_ref, segq_ref, segk_ref, gbias_ref, gscale_ref,
    qkv_ref, ctx_ref, out_t_ref, lse_ref, gate_ref, mask, sc, pr,
):
    r = pl.program_id(0)
    width = heads * hd
    seq = x_ref.shape[0]
    x = x_ref[...]
    wide = nt(w_ref[0], x) + qvb_ref[0]
    qkv_ref[0, 0, pl.ds(0, width), :] = wide[:width].astype(bf) * bf(hd**-0.5)
    qkv_ref[0, 0, pl.ds(width, 2 * width), :] = wide[width:].astype(bf)
    lin = nt(gb_ref[0], x)
    half = gates // 2
    for c in range(seq // LANES):
        lanes = pl.ds(c * LANES, LANES)
        mask[:, lanes] = jnp.where(segk_ref[0] == segq_ref[0, :, lanes], 0.0, masked_score)
    for h in range(heads):
        at = pl.ds(h * hd, hd)
        q_t = qkv_ref[0, 0, at, :]
        k_t = qkv_ref[0, 0, pl.ds(width + h * hd, hd), :]
        v_t = qkv_ref[0, 0, pl.ds(2 * width + h * hd, hd), :]
        first = jax.nn.sigmoid(jnp.sum(lin[h * gates : h * gates + half], axis=0, keepdims=True) + gbias_ref[0])
        second = jax.nn.sigmoid(
            jnp.sum(lin[h * gates + half : (h + 1) * gates], axis=0, keepdims=True) + gbias_ref[1]
        )
        gate = first * (second * gscale_ref[idx_ref[r], h] - 1.0) + 2.0
        gate_ref[0, 0, pl.ds(h, 1), :] = first
        gate_ref[0, 0, pl.ds(heads + h, 1), :] = second
        sc[h % 2] = nn(k_t.T, q_t)
        for c in range(seq // LANES):
            lanes = pl.ds(c * LANES, LANES)
            s = sc[h % 2, :, lanes] + pos_ref[0, h, :, lanes] * gate[:, c * LANES : (c + 1) * LANES] + mask[:, lanes]
            top = jnp.max(s, axis=0, keepdims=True)
            p = jnp.exp(s - top)
            total = jnp.sum(p, axis=0, keepdims=True)
            pr[h % 2, :, lanes] = p.astype(bf)
            lse_ref[0, 0, pl.ds(h, 1), lanes] = top + jnp.log(total)
            lse_ref[0, 0, pl.ds(heads + h, 1), lanes] = 1.0 / total
        out_t_ref[0, 0, at, :] = nn(v_t, pr[h % 2]) * lse_ref[0, 0, pl.ds(heads + h, 1), :]
    ctx_ref[0] = out_t_ref[0, 0].T.astype(bf)


def attend_back_kernel(
    heads, hd, idx_ref, x_ref, w_ref, gsum_ref, pos_ref, segq_ref, segk_ref, gscale_ref, qkv_ref, out_t_ref, lse_ref,
    gate_ref, dctx_ref, first_ref,
    grad_ref, dw_ref, dqv_ref, dgw_ref, dgate_ref, table_ref, mask, sc, dp, pr, ds, wide,
):
    r = pl.program_id(0)
    row = pl.program_id(1)
    width = heads * hd
    seq = x_ref.shape[0]
    for c in range(seq // LANES):
        lanes = pl.ds(c * LANES, LANES)
        mask[:, lanes] = jnp.where(segk_ref[0] == segq_ref[0, :, lanes], 0.0, masked_score)
    wide[...] = jnp.zeros_like(wide)
    dgate_ref[0, 0] = jnp.zeros_like(dgate_ref[0, 0])
    for h in range(heads):
        at = pl.ds(h * hd, hd)
        q_t = qkv_ref[0, 0, at, :]
        k_t = qkv_ref[0, 0, pl.ds(width + h * hd, hd), :]
        v_t = qkv_ref[0, 0, pl.ds(2 * width + h * hd, hd), :]
        g_t = dctx_ref[0, at, :]
        b = h % 2
        sc[b] = nn(k_t.T, q_t)
        dp[b] = nn(v_t.T, g_t)
        first = gate_ref[0, 0, pl.ds(h, 1), :]
        second = gate_ref[0, 0, pl.ds(heads + h, 1), :]
        scale = gscale_ref[idx_ref[r], h]
        gate = first * (second * scale - 1.0) + 2.0
        centre = jnp.sum(g_t.astype(f32) * out_t_ref[0, 0, at, :], axis=0, keepdims=True)
        lse = lse_ref[0, 0, pl.ds(h, 1), :]
        parts = []
        for c in range(seq // LANES):
            lanes = pl.ds(c * LANES, LANES)
            cut = slice(c * LANES, (c + 1) * LANES)
            pos = pos_ref[0, h, :, lanes]
            p = jnp.exp(sc[b, :, lanes] + (pos * gate[:, cut] - lse[:, cut]) + mask[:, lanes])
            pr[b, :, lanes] = p.astype(bf)
            d = p * (dp[b, :, lanes] - centre[:, cut])
            ds[b, :, lanes] = d.astype(bf)
            parts.append(jnp.sum(d * pos, axis=0, keepdims=True))
        dgate = jnp.concatenate(parts, axis=1)

        @pl.when(r == 0)
        def _():
            @pl.when(row == 0)
            def _():
                table_ref[h] = gate * ds[b].astype(f32)

            @pl.when(row != 0)
            def _():
                table_ref[h] += gate * ds[b].astype(f32)

        wide[at, :] = (nn(k_t, ds[b]) * hd**-0.5).astype(bf)
        wide[pl.ds(width + h * hd, hd), :] = nt(q_t, ds[b]).astype(bf)
        wide[pl.ds(2 * width + h * hd, hd), :] = nt(g_t, pr[b]).astype(bf)
        dfirst = dgate * (second * scale - 1.0) * first * (1.0 - first)
        dsecond = dgate * first * scale * second * (1.0 - second)
        dgate_ref[0, 0, pl.ds(h, 1), :] = dfirst
        dgate_ref[0, 0, pl.ds(heads + h, 1), :] = dsecond
        dgate_ref[0, 0, pl.ds(8 + h, 1), :] = dgate * first * second
    x = x_ref[...]
    low_gate = dgate_ref[0, 0].astype(bf)
    wide[pl.ds(3 * width, 16), :] = low_gate

    @pl.when(row == 0)
    def _():
        dgw_ref[0] = nn(low_gate, x)

    @pl.when(row != 0)
    def _():
        dgw_ref[0] += nn(low_gate, x)

    lines = pl.ds(pl.multiple_of(row * seq, seq), seq)
    part = nn(wide[pl.ds(0, 3 * width), :].T, w_ref[0]) + nn(wide[pl.ds(3 * width, 16), :].T, gsum_ref[0])

    @pl.when(r == 0)
    def _():
        grad_ref[lines, :] = deep_alpha * first_ref[lines, :] + part
        dqv_ref[0] = wide[pl.ds(0, 3 * width), :]

        @pl.when(row == 0)
        def _():
            dw_ref[...] = nn(wide[pl.ds(0, 3 * width), :], x)

        @pl.when(row != 0)
        def _():
            dw_ref[...] += nn(wide[pl.ds(0, 3 * width), :], x)

    @pl.when(r != 0)
    def _():
        grad_ref[lines, :] += part


def norm_stats(v):
    mean = jnp.mean(v, axis=-1, keepdims=True)
    cen = v - mean
    rs = lax.rsqrt(jnp.mean(cen * cen, axis=-1, keepdims=True) + norm_eps)
    return cen * rs, rs


def norm_back(g, n, rs, gain):
    gn = g * gain
    return rs * (gn - jnp.mean(gn, axis=-1, keepdims=True) - n * jnp.mean(gn * n, axis=-1, keepdims=True))


def gelu_pair(x):
    e = jnp.exp(x * x * -0.5)
    t = 1.0 / (1.0 + (0.3275911 * 0.5**0.5) * jnp.abs(x))
    poly = t * (0.5 * 0.254829592 + t * (0.5 * -0.284496736 + t * (0.5 * 1.421413741 + t * (0.5 * -1.453152027 + t * (0.5 * 1.061405429)))))
    tail = poly * e
    cdf = jnp.where(x > 0.0, 1.0 - tail, tail)
    return x * cdf, cdf + x * e * 0.3989422804014327


def layer_kernel(
    idx_ref, ctx_ref, x_ref, go_ref, ow_ref, w1_ref, b1_ref, w2_ref, vec_ref,
    out_ref, first_ref, dctx_ref, hid_low_ref, mix_low_ref, first_low_ref, act_ref, pre_low_ref, sums_ref,
    act, slope, plow,
):
    step = pl.program_id(0)
    parts, units, feats = w1_ref.shape
    rows = x_ref.shape[0]
    own = idx_ref[0]
    vec = vec_ref[...]
    out_bias, gain1, bias1, bias2, gain2, beta2 = (vec[i : i + 1] for i in range(6))
    total = deep_alpha * x_ref[...].astype(f32) + out_bias
    for c in range(parts):
        total = total + nn(ctx_ref[c], ow_ref[c])
    n1, rs1 = norm_stats(total)
    hidden = n1 * gain1 + bias1
    hid_low = hidden.astype(bf)
    hid_low_ref[...] = hid_low
    block = 256
    for c in range(parts):
        for u in range(0, units, block):
            pre = nt(hid_low, w1_ref[c, pl.ds(u, block), :]) + b1_ref[c, :, pl.ds(u, block)]
            a, s = gelu_pair(pre)
            act[c, :, pl.ds(u, block)] = a.astype(bf)
            slope[c, :, pl.ds(u, block)] = s.astype(bf)
    mixed = deep_alpha * hidden + bias2
    for c in range(parts):
        mixed = mixed + nn(act[c], w2_ref[c])
    act_ref[...] = act[own]
    n2, rs2 = norm_stats(mixed)
    out_ref[...] = n2 * gain2 + beta2
    g = go_ref[...].astype(f32)
    grad_mixed = norm_back(g, n2, rs2, gain2)
    mix_low = grad_mixed.astype(bf)
    mix_low_ref[...] = mix_low
    bias_sums = []
    for c in range(parts):
        line = []
        for u in range(0, units, block):
            d = nt(mix_low, w2_ref[c, pl.ds(u, block), :]) * slope[c, :, pl.ds(u, block)].astype(f32)
            line.append(jnp.sum(d, axis=0, keepdims=True))
            plow[c, :, pl.ds(u, block)] = d.astype(bf)
        bias_sums.append(jnp.concatenate(line, axis=1))
    grad_hidden = deep_alpha * grad_mixed
    for c in range(parts):
        grad_hidden = grad_hidden + nn(plow[c], w1_ref[c])
    pre_low_ref[...] = plow[own]
    b1_sum = bias_sums[0]
    for c in range(1, parts):
        b1_sum = jnp.where(own == c, bias_sums[c], b1_sum)
    grad_first = norm_back(grad_hidden, n1, rs1, gain1)
    first_ref[...] = grad_first
    first_low = grad_first.astype(bf)
    first_low_ref[...] = first_low
    for c in range(parts):
        dctx_ref[c] = nt(ow_ref[c], first_low).astype(bf)

    def col(v):
        return jnp.sum(v, axis=0, keepdims=True)

    sums = jnp.concatenate(
        [
            col(g * n2), col(g), col(grad_mixed), col(grad_hidden * n1), col(grad_hidden), col(grad_first), b1_sum,
            jnp.zeros_like(b1_sum),
        ],
        axis=0,
    )

    @pl.when(step == 0)
    def _():
        sums_ref[...] = sums

    @pl.when(step != 0)
    def _():
        sums_ref[...] += sums


def table_kernel(heads, tops, lows, buckets_ref, val_ref, out_ref):
    rows, cols = buckets_ref.shape

    @pl.when(pl.program_id(0) == 0)
    def _():
        out_ref[...] = jnp.zeros_like(out_ref)

    top_id = lax.broadcasted_iota(jnp.int32, (tops, cols), 0)
    low_id = lax.broadcasted_iota(jnp.int32, (lows, cols), 0)

    def group(g, acc):
        at = pl.ds(pl.multiple_of(g * 8, 8), 8)
        idx = buckets_ref[at, :]
        high = idx >> 4
        low = idx & 15
        vals = [val_ref[h, at, :] for h in range(heads)]
        for i in range(8):
            a = (high[i : i + 1] == top_id).astype(f32).astype(bf)
            hit = low[i : i + 1] == low_id
            b = jnp.concatenate([jnp.where(hit, v[i : i + 1], 0.0) for v in vals], axis=0).astype(bf)
            acc = acc + nt(a, b)
        return acc

    out_ref[...] += lax.fori_loop(0, rows // 8, group, jnp.zeros(out_ref.shape, f32))


def table_grad(buckets_t, values, size):
    heads, seq, _ = values.shape
    lows = 16
    tops = -(-size // lows // 8) * 8
    rows = 64
    out = pl.pallas_call(
        functools.partial(table_kernel, heads, tops, lows),
        grid=(seq // rows,),
        in_specs=[
            pl.BlockSpec((rows, seq), lambda i: (i, 0)),
            pl.BlockSpec((heads, rows, seq), lambda i: (0, i, 0)),
        ],
        out_specs=pl.BlockSpec((tops, heads * lows), lambda i: (0, 0)),
        out_shape=jax.ShapeDtypeStruct((tops, heads * lows), f32),
        name="table_grad",
    )(buckets_t, values)
    return out.reshape(tops, heads, lows).transpose(0, 2, 1).reshape(tops * lows, heads)[:size]


def body(
    n_dp, n_mp,
    tokens, segment_ids, buckets, qkv_weight, qv_bias, rel_table, gate_weight, gate_bias, gate_scale, out_weight,
    out_bias, ln1_gain, ln1_bias, fc1_weight, fc1_bias, fc2_weight, fc2_bias, ln2_gain, ln2_bias, grad_out,
):
    rows, feats = tokens.shape
    seqs, seq = segment_ids.shape
    size, heads = rel_table.shape
    hd, gates = gate_weight.shape
    width = heads * hd
    units = fc1_weight.shape[1]
    me = lax.axis_index("mp")
    dp = lax.axis_index("dp")
    order = (me + jnp.arange(n_mp)) % n_mp
    idx = order.astype(jnp.int32)

    small = jnp.concatenate([rel_table.T.reshape(-1), fc1_bias, qv_bias.reshape(-1), gate_scale])
    small = lax.all_gather(small, "mp")
    cuts = [size * heads, units, 2 * width, heads]
    ends = [sum(cuts[:i]) for i in range(len(cuts) + 1)]
    tables, b1, qvb, scales = (small[:, ends[i] : ends[i + 1]] for i in range(4))
    chunks = -(-size // LANES)
    tables = jnp.pad(tables.reshape(n_mp * heads, size), ((0, 0), (0, chunks * LANES - size)))
    tables = tables.reshape(n_mp * heads, chunks, LANES)
    b1 = b1.reshape(n_mp, 1, units)
    qvb = qvb.reshape(n_mp, 2, width)
    qvb = jnp.concatenate([qvb[:, 0], jnp.zeros_like(qvb[:, 0]), qvb[:, 1]], axis=1)[:, :, None]

    def gathered(w):
        per = w.shape[0] // n_dp
        mine = lax.dynamic_slice_in_dim(w, dp * per, per, 0)
        return lax.all_gather(mine, ("mp", "dp"), tiled=True).reshape(n_mp, w.shape[0], w.shape[1])

    wqkv = gathered(qkv_weight.transpose(0, 2, 1).reshape(3 * width, feats))
    ow = gathered(out_weight)
    w1 = gathered(fc1_weight.T)
    w2 = gathered(fc2_weight)

    eye = jnp.eye(n_mp * heads, dtype=bf).reshape(n_mp, heads, 1, n_mp * heads, 1)
    gb = (eye * gate_weight.T.reshape(1, 1, gates, 1, hd)).reshape(n_mp, heads * gates, feats)
    gb = jnp.pad(gb, ((0, 0), (0, 32 - heads * gates), (0, 0)))
    gw = gate_weight.astype(f32).T
    halves = jnp.stack([gw[: gates // 2].sum(0), gw[gates // 2 :].sum(0)]).astype(bf)
    gsum = (eye.reshape(n_mp, 1, heads, n_mp * heads, 1) * halves.reshape(1, 2, 1, 1, hd)).reshape(n_mp, 2 * heads, feats)
    gsum = jnp.pad(gsum, ((0, 0), (0, 16 - 2 * heads), (0, 0)))
    gbias = jnp.stack([gate_bias[: gates // 2].sum(), gate_bias[gates // 2 :].sum()])

    buckets_t = buckets.T
    pos = bias_of(buckets_t, tables).reshape(n_mp, heads, seq, seq)
    segq = segment_ids[:, None, :]
    segk = segment_ids[:, :, None]

    whole = lambda *shape: pl.BlockSpec(shape, lambda *_: (0,) * len(shape))
    smem = pl.BlockSpec(memory_space=pltpu.SMEM)
    by_r = lambda *shape: pl.BlockSpec((1,) + shape, lambda r, s, ix: (ix[r],) + (0,) * len(shape))
    by_rs = lambda *shape: pl.BlockSpec((1, 1) + shape, lambda r, s, ix: (ix[r], s) + (0,) * len(shape))
    x_spec = pl.BlockSpec((seq, feats), lambda r, s, ix: (s, 0))
    segq_spec = pl.BlockSpec((1, 1, seq), lambda r, s, ix: (s, 0, 0))
    segk_spec = pl.BlockSpec((1, seq, 1), lambda r, s, ix: (s, 0, 0))
    sds = jax.ShapeDtypeStruct

    qkv_t, ctx, out_t, lse, gate = pl.pallas_call(
        functools.partial(attend_kernel, heads, hd, gates),
        grid_spec=pltpu.PrefetchScalarGridSpec(
            num_scalar_prefetch=1,
            grid=(n_mp, seqs),
            in_specs=[
                x_spec, by_r(3 * width, feats), by_r(32, feats), by_r(3 * width, 1), by_r(heads, seq, seq), segq_spec,
                segk_spec, smem, smem,
            ],
            out_specs=[
                by_rs(3 * width, seq),
                pl.BlockSpec((1, seq, width), lambda r, s, ix: (ix[r], s, 0)),
                by_rs(width, seq), by_rs(8, seq), by_rs(8, seq),
            ],
            scratch_shapes=[
                pltpu.VMEM((seq, seq), f32), pltpu.VMEM((2, seq, seq), f32), pltpu.VMEM((2, seq, seq), bf),
            ],
        ),
        out_shape=[
            sds((n_mp, seqs, 3 * width, seq), bf), sds((n_mp, rows, width), bf), sds((n_mp, seqs, width, seq), f32),
            sds((n_mp, seqs, 8, seq), f32), sds((n_mp, seqs, 8, seq), f32),
        ],
        compiler_params=params(56),
        name="attend",
    )(idx, tokens, wqkv, gb, qvb, pos, segq, segk, gbias, scales)

    vec = jnp.stack([out_bias, ln1_gain, ln1_bias, fc2_bias, ln2_gain, ln2_bias, out_bias, out_bias])
    tile = 256
    row = lambda n: pl.BlockSpec((tile, n), lambda i, ix: (i, 0))
    once = lambda *shape: pl.BlockSpec(shape, lambda *_: (0,) * len(shape), pipeline_mode=pl.Buffered(1))
    (normed, grad_first, dctx, hid_low, mix_low, first_low, act_own, pre_own, sums) = pl.pallas_call(
        layer_kernel,
        grid_spec=pltpu.PrefetchScalarGridSpec(
            num_scalar_prefetch=1,
            grid=(rows // tile,),
            in_specs=[
                pl.BlockSpec((n_mp, tile, width), lambda i, ix: (0, i, 0)), row(feats), row(feats),
                once(n_mp, width, feats), once(n_mp, units, feats), once(n_mp, 1, units), once(n_mp, units, feats),
                once(8, feats),
            ],
            out_specs=[
                row(feats), row(feats), pl.BlockSpec((n_mp, width, tile), lambda i, ix: (0, 0, i)), row(feats), row(feats),
                row(feats), row(units), row(units), whole(8, feats),
            ],
            scratch_shapes=[pltpu.VMEM((n_mp, tile, units), bf) for _ in range(3)],
        ),
        out_shape=[
            sds((rows, feats), f32), sds((rows, feats), f32), sds((n_mp, width, rows), bf), sds((rows, feats), bf),
            sds((rows, feats), bf), sds((rows, feats), bf), sds((rows, units), bf), sds((rows, units), bf),
            sds((8, feats), f32),
        ],
        compiler_params=params(60),
        name="layer",
    )(idx, ctx, tokens, grad_out, ow, w1, b1, w2, vec)

    grad_fc2 = lax.dot_general(act_own, mix_low, (((0,), (0,)), ((), ())), preferred_element_type=f32)
    grad_fc1 = lax.dot_general(hid_low, pre_own, (((0,), (0,)), ((), ())), preferred_element_type=f32)
    ctx_own = lax.dynamic_index_in_dim(ctx, me, 0, keepdims=False)
    grad_ow = lax.dot_general(ctx_own, first_low, (((0,), (0,)), ((), ())), preferred_element_type=f32)

    input_grad, dw, dqv, dgw, dgate, acc = pl.pallas_call(
        functools.partial(attend_back_kernel, heads, hd),
        grid_spec=pltpu.PrefetchScalarGridSpec(
            num_scalar_prefetch=1,
            grid=(n_mp, seqs),
            in_specs=[
                x_spec, by_r(3 * width, feats), by_r(16, feats), by_r(heads, seq, seq), segq_spec, segk_spec, smem,
                by_rs(3 * width, seq), by_rs(width, seq), by_rs(8, seq), by_rs(8, seq),
                pl.BlockSpec((1, width, seq), lambda r, s, ix: (ix[r], 0, s)), once(rows, feats),
            ],
            out_specs=[
                whole(rows, feats), whole(3 * width, feats),
                pl.BlockSpec((1, 3 * width, seq), lambda r, s, ix: (jnp.where(r == 0, s, seqs - 1), 0, 0)),
                by_r(16, feats), by_rs(16, seq), whole(heads, seq, seq),
            ],
            scratch_shapes=[
                pltpu.VMEM((seq, seq), f32), pltpu.VMEM((2, seq, seq), f32), pltpu.VMEM((2, seq, seq), f32),
                pltpu.VMEM((2, seq, seq), bf), pltpu.VMEM((2, seq, seq), bf), pltpu.VMEM((3 * width + 16, seq), bf),
            ],
        ),
        out_shape=[
            sds((rows, feats), f32), sds((3 * width, feats), f32), sds((seqs, 3 * width, seq), bf),
            sds((n_mp, 16, feats), f32), sds((n_mp, seqs, 16, seq), f32), sds((heads, seq, seq), f32),
        ],
        compiler_params=params(60),
        name="attend_back",
    )(idx, tokens, wqkv, gsum, pos, segq, segk, scales, qkv_t, out_t, lse, gate, dctx, grad_first)

    grad_table = table_grad(buckets_t, acc, size)

    by_head = dgw[:, : 2 * heads].reshape(n_mp, 2, heads, n_mp, heads, hd)
    picked = jnp.einsum("cihcht->it", by_head)
    gate_sums = dgate.sum(axis=(1, 3))
    dbias = gate_sums[:, : 2 * heads].reshape(n_mp, 2, heads).sum(axis=(0, 2))
    dscale = lax.dynamic_index_in_dim(gate_sums, me, 0, keepdims=False)[8 : 8 + heads]
    dqv_sum = dqv.astype(f32).sum(axis=(0, 2))
    little = jnp.concatenate(
        [
            sums[:7].reshape(-1), dqv_sum[:width], dqv_sum[2 * width :], grad_table.reshape(-1), picked.reshape(-1), dbias,
            dscale,
        ]
    )
    little = lax.psum(little, "dp")
    sums = little[: 7 * feats].reshape(7, feats)
    rest = little[7 * feats :]
    dqv_bias = rest[: 2 * width].reshape(2, width)
    rest = rest[2 * width :]
    grad_table = rest[: size * heads].reshape(size, heads)
    rest = rest[size * heads :]
    grad_gate_weight = jnp.repeat(rest[: 2 * hd].reshape(2, hd), gates // 2, axis=0).T
    rest = rest[2 * hd :]
    grad_gate_bias = jnp.repeat(rest[:2], gates // 2)
    grad_gate_scale = rest[2:]

    big = jnp.concatenate([dw, grad_ow, grad_fc1, grad_fc2], axis=0).astype(bf)
    big = lax.psum(big, "dp").astype(f32)
    dw = big[: 3 * width].reshape(3, width, feats).transpose(0, 2, 1)
    grad_ow = big[3 * width : 4 * width]
    grad_fc1 = big[4 * width : 4 * width + feats]
    grad_fc2 = big[4 * width + feats :]
    return (
        normed, input_grad, dw, dqv_bias, grad_table, grad_gate_weight, grad_gate_bias, grad_gate_scale, grad_ow, sums[5],
        sums[3], sums[4], grad_fc1, sums[6], grad_fc2, sums[2], sums[0], sums[1],
    )


def solution(mesh):
    in_specs = (
        P("dp", None), P("dp", None), P(), P(None, None, "mp"), P(None, "mp"), P(None, "mp"), P(), P(), P("mp"),
        P("mp", None), P(), P(), P(), P(None, "mp"), P("mp"), P("mp", None), P(), P(), P(), P("dp", None),
    )
    out_specs = (
        P("dp", None), P("dp", None), P(None, None, "mp"), P(None, "mp"), P(None, "mp"), P(), P(), P("mp"),
        P("mp", None), P(), P(), P(), P(None, "mp"), P("mp"), P("mp", None), P(), P(), P(),
    )
    fn = functools.partial(body, mesh.shape["dp"], mesh.shape["mp"])
    return jax.shard_map(fn, mesh=mesh, in_specs=in_specs, out_specs=out_specs, check_vma=False)
```

```python
import functools

import jax
import jax.numpy as jnp
from jax import lax
from jax.experimental import pallas as pl
from jax.experimental.pallas import tpu as pltpu
from jax.sharding import PartitionSpec as P

norm_eps = 1e-05
deep_alpha = 24.0**0.25
masked_score = -1e30
bf = jnp.bfloat16
f32 = jnp.float32
LANES = 128
LIMIT = 60
COST = 3_000_000_000


def nn(a, b):
    return lax.dot_general(a, b, (((1,), (0,)), ((), ())), preferred_element_type=f32)


def nt(a, b):
    return lax.dot_general(a, b, (((1,), (1,)), ((), ())), preferred_element_type=f32)


def params(mib):
    return pltpu.CompilerParams(vmem_limit_bytes=mib * 1024 * 1024)


def lines_kernel(table_ref, b1_ref, qv_ref, scale_ref, out_ref, cut_ref):
    heads, size = table_ref.shape
    feats = out_ref.shape[1]
    width = qv_ref.shape[1]
    out_ref[...] = jnp.zeros_like(out_ref)
    per = -(-size // LANES) * LANES
    for h in range(heads):
        out_ref[pl.ds(h * per // feats, 1), pl.ds(h * per % feats, size)] = table_ref[pl.ds(h, 1), :]
    out_ref[pl.ds(2, 1), :] = b1_ref[...]
    out_ref[pl.ds(3, 1), pl.ds(0, width)] = qv_ref[pl.ds(0, 1), :]
    out_ref[pl.ds(3, 1), pl.ds(256, width)] = qv_ref[pl.ds(1, 1), :]
    out_ref[pl.ds(3, 1), pl.ds(512, heads)] = scale_ref[...]
    rest = out_ref[...]
    cuts = []
    for _ in range(3):
        cut = rest.astype(bf).astype(f32)
        cuts.append(cut)
        rest = rest - cut
    cut_ref[...] = jnp.concatenate(cuts + [jnp.zeros_like(rest)], axis=0).astype(bf)


def lines_of(table, b1, qv, scale):
    feats = b1.shape[1]
    return pl.pallas_call(
        lines_kernel,
        out_shape=[jax.ShapeDtypeStruct((4, feats), f32), jax.ShapeDtypeStruct((16, feats), bf)],
        compiler_params=params(LIMIT),
        name="lines",
    )(table, b1, qv, scale)


def bias_kernel(heads, chunks, buckets_ref, small_ref, out_ref):
    rows, cols = buckets_ref.shape
    groups, _, feats = small_ref.shape
    for r in range(0, rows, 8):
        at = pl.ds(r, 8)
        for c in range(cols // LANES):
            lanes = pl.ds(c * LANES, LANES)
            idx = buckets_ref[at, lanes]
            low = idx & (LANES - 1)
            high = idx >> 7
            for h in range(heads):
                got = None
                for k in range(chunks):
                    spot = ((h % 3) * chunks + k) * LANES
                    line = jnp.broadcast_to(
                        small_ref[h // 3, pl.ds(spot // feats, 1), pl.ds(spot % feats, LANES)], (8, LANES)
                    )
                    part = jnp.take_along_axis(line, low, axis=1, mode="promise_in_bounds")
                    got = part if got is None else jnp.where(high == k, part, got)
                out_ref[h, at, lanes] = got


def bias_of(buckets_t, small, heads, size):
    groups, _, feats = small.shape
    seq = buckets_t.shape[0]
    rows = 64
    cost = pl.CostEstimate(flops=COST, bytes_accessed=1 << 20, transcendentals=0)
    return pl.pallas_call(
        functools.partial(bias_kernel, heads * groups, -(-size // LANES)),
        grid=(seq // rows,),
        in_specs=[
            pl.BlockSpec((rows, seq), lambda i: (i, 0)),
            pl.BlockSpec((groups, 4, feats), lambda i: (0, 0, 0)),
        ],
        out_specs=pl.BlockSpec((heads * groups, rows, seq), lambda i: (0, i, 0)),
        out_shape=jax.ShapeDtypeStruct((heads * groups, seq, seq), f32),
        compiler_params=params(LIMIT),
        cost_estimate=cost,
        name="pos_bias",
    )(buckets_t, small)


def head_lanes(shape, head, hd):
    return lax.broadcasted_iota(jnp.int32, shape, 1) // hd == head


def fill_mask(mask, segq_ref, segk_ref, row):
    seq = mask.shape[0]
    for c in range(seq // LANES):
        lanes = pl.ds(c * LANES, LANES)
        mask[:, lanes] = jnp.where(segk_ref[row] == segq_ref[row, :, lanes], 0.0, masked_score)


def attend_kernel(
    heads, hd, group, x_hbm, wt_hbm, wl_hbm, pos_hbm, gw_ref, small_ref, segq_ref, segk_ref, gbias_ref, at_ref,
    qkv_hbm, ctx_hbm, out_hbm, lse_ref, gate_ref,
    x_v, w_v, pos_v, qkv_v, ctx_v, out_v, mask, sc, pr, sem,
):
    width = heads * hd
    seqs, _, seq = segq_ref.shape
    gates = gw_ref.shape[0]
    half = gates // 2
    cut = wt_hbm.shape[1]

    def line(row):
        return pl.ds(row * seq, seq)

    copy = pltpu.make_async_copy
    x_in = [copy(x_hbm.at[line(r)], x_v.at[r], sem.at[r]) for r in range(seqs)]
    w_in = [
        copy(wt_hbm.at[group], w_v.at[pl.ds(0, cut)], sem.at[seqs]),
        copy(wl_hbm.at[group, pl.ds(0, 3 * width - cut)], w_v.at[pl.ds(cut, 3 * width - cut)], sem.at[seqs + 1]),
    ]
    pos_in = [copy(pos_hbm.at[group * heads + h], pos_v.at[h], sem.at[seqs + 2 + h]) for h in range(heads)]
    base = seqs + 2 + heads
    out_copies = [
        [copy(qkv_v.at[r], qkv_hbm.at[r], sem.at[base + 3 * r]), copy(ctx_v.at[line(r)], ctx_hbm.at[line(r)], sem.at[base + 3 * r + 1]),
         copy(out_v.at[r], out_hbm.at[r], sem.at[base + 3 * r + 2])]
        for r in range(seqs)
    ]
    for c in [x_in[0]] + w_in + [pos_in[0]] + x_in[1:] + pos_in[1:]:
        c.start()

    cols = jnp.broadcast_to(small_ref[group, pl.ds(3, 1), pl.ds(0, 512)], (8, 512)).T[:, :1]
    gw = gw_ref[...].astype(f32)
    mine = [jnp.where(head_lanes(gw.shape, at_ref[0] * heads + h, hd), gw, 0.0) for h in range(heads)]
    mine = jnp.concatenate(mine, axis=0).astype(bf)
    bias_a = gbias_ref[0] + gbias_ref[1] + gbias_ref[2] + gbias_ref[3]
    bias_b = gbias_ref[4] + gbias_ref[5] + gbias_ref[6] + gbias_ref[7]
    lins = {}

    def project(row):
        x_in[row].wait()
        if row == 0:
            for c in w_in:
                c.wait()
        x = x_v[row]
        both = nt(w_v[...], x)
        qkv_v[row, pl.ds(0, width), :] = (both[:width] + cols[:width]).astype(bf) * bf(hd**-0.5)
        qkv_v[row, pl.ds(width, width), :] = both[width : 2 * width].astype(bf)
        qkv_v[row, pl.ds(2 * width, width), :] = (both[2 * width :] + cols[256 : 256 + width]).astype(bf)
        lins[row] = nt(mine, x)
        fill_mask(mask.at[row], segq_ref, segk_ref, row)
        out_copies[row][0].start()

    def score(i):
        row, h = divmod(i, heads)
        k_t = qkv_v[row, pl.ds(width + h * hd, hd), :]
        sc[i % 2] = nn(k_t.T, qkv_v[row, pl.ds(h * hd, hd), :])

    def weigh(i):
        row, h = divmod(i, heads)
        if row == 0:
            pos_in[h].wait()
        lin = lins[row]
        first = jax.nn.sigmoid(jnp.sum(lin[h * gates : h * gates + half], axis=0, keepdims=True) + bias_a)
        second = jax.nn.sigmoid(jnp.sum(lin[h * gates + half : (h + 1) * gates], axis=0, keepdims=True) + bias_b)
        gate = first * (second * small_ref[group, pl.ds(3, 1), pl.ds(512 + h, 1)] - 1.0) + 2.0
        gate_ref[row, pl.ds(h, 1), :] = first
        gate_ref[row, pl.ds(heads + h, 1), :] = second
        for c in range(seq // LANES):
            lanes = pl.ds(c * LANES, LANES)
            s = sc[i % 2, :, lanes] + pos_v[h, :, lanes] * gate[:, c * LANES : (c + 1) * LANES] + mask[row, :, lanes]
            top = jnp.max(s, axis=0, keepdims=True)
            p = jnp.exp(s - top)
            total = jnp.sum(p, axis=0, keepdims=True)
            pr[i % 2, :, lanes] = p.astype(bf)
            lse_ref[row, pl.ds(h, 1), lanes] = top + jnp.log(total)
            lse_ref[row, pl.ds(heads + h, 1), lanes] = 1.0 / total

    def gather(i):
        row, h = divmod(i, heads)
        v_t = qkv_v[row, pl.ds(2 * width + h * hd, hd), :]
        out_v[row, pl.ds(h * hd, hd), :] = nn(v_t, pr[i % 2]) * lse_ref[row, pl.ds(heads + h, 1), :]
        if h == heads - 1:
            out_copies[row][2].start()
            ctx_v[line(row), :] = out_v[row].T.astype(bf)
            out_copies[row][1].start()

    count = seqs * heads
    project(0)
    score(0)
    for i in range(count):
        if i + 1 < count:
            if (i + 1) % heads == 0:
                project((i + 1) // heads)
            score(i + 1)
        weigh(i)
        if i:
            gather(i - 1)
    gather(count - 1)
    for row in out_copies:
        for c in row:
            c.wait()


def attend_back_kernel(
    heads, hd, which, wt_hbm, wl_hbm, pos_hbm, qkv_hbm, out_hbm, dctx_hbm, base_hbm, x_hbm,
    gw_ref, small_ref, segq_ref, segk_ref, at_ref, lse_ref, gate_ref, *rest,
):
    own, group = which == 0, max(which - 1, 0)
    if own:
        grad_hbm, dw_hbm, tiny_ref, table_hbm = rest[:4]
        dw_v, x_v, parts, table_v, table_sem = rest[-5:]
        rest = rest[4:-5]
    else:
        grad_hbm = rest[0]
        rest = rest[1:]
    w_v, pos_v, qkv_v, out_v, dctx_v, base_v, mask, sc, dp, pr, ds, wide, sem = rest
    width = heads * hd
    seqs, _, seq = segq_ref.shape
    feats = w_v.shape[1]
    cut = wt_hbm.shape[1]

    def line(row):
        return pl.ds(row * seq, seq)

    copy = pltpu.make_async_copy
    w_in = [
        copy(wt_hbm.at[group], w_v.at[pl.ds(0, cut)], sem.at[0]),
        copy(wl_hbm.at[group, pl.ds(0, 3 * width - cut)], w_v.at[pl.ds(cut, 3 * width - cut)], sem.at[1]),
    ]
    pos_in = [copy(pos_hbm.at[group * heads + h], pos_v.at[h], sem.at[2 + h]) for h in range(heads)]
    spot = 2 + heads
    row_in, base_in, grad_out = [], [], []
    for r in range(seqs):
        row_in.append([
            copy(qkv_hbm.at[r], qkv_v.at[r], sem.at[spot]), copy(dctx_hbm.at[which, r], dctx_v.at[r], sem.at[spot + 1]),
            copy(out_hbm.at[r], out_v.at[r], sem.at[spot + 2]),
        ])
        base_in.append(copy(base_hbm.at[line(r)], base_v.at[r], sem.at[spot + 3]))
        grad_out.append(copy(base_v.at[r], grad_hbm.at[line(r)], sem.at[spot + 4]))
        spot += 5
    for c in row_in[0] + [pos_in[0]] + row_in[1] + pos_in[1:] + w_in + base_in:
        c.start()
    if own:
        x_in = [copy(x_hbm.at[line(r)], x_v.at[r], table_sem.at[heads + 1 + r]) for r in range(seqs)]
        table_out = [copy(table_v.at[h], table_hbm.at[h], table_sem.at[h]) for h in range(heads)]
        dw_out = copy(dw_v, dw_hbm, table_sem.at[heads])
        for c in x_in:
            c.start()

    gw = gw_ref[...].astype(f32)
    half = gw.shape[0] // 2
    sums = [jnp.sum(gw[:half], axis=0, keepdims=True), jnp.sum(gw[half:], axis=0, keepdims=True)]
    lanes_of = [head_lanes((1, feats), at_ref[0] * heads + h, hd) for h in range(heads)]
    gsum = [jnp.where(lanes_of[h], part, 0.0) for part in sums for h in range(heads)]
    w_v[pl.ds(3 * width, 16), :] = jnp.concatenate(gsum + [jnp.zeros((16 - 2 * heads, feats), f32)], axis=0).astype(bf)
    gate_parts = {}

    def score(i):
        row, h = divmod(i, heads)
        if h == 0:
            for c in row_in[row]:
                c.wait()
            fill_mask(mask.at[row], segq_ref, segk_ref, row)
        k_t = qkv_v[row, pl.ds(width + h * hd, hd), :]
        v_t = qkv_v[row, pl.ds(2 * width + h * hd, hd), :]
        sc[i % 2] = nn(k_t.T, qkv_v[row, pl.ds(h * hd, hd), :])
        dp[i % 2] = nn(v_t.T, dctx_v[row, pl.ds(h * hd, hd), :])

    def weigh(i):
        row, h = divmod(i, heads)
        if row == 0:
            pos_in[h].wait()
        b = i % 2
        g_t = dctx_v[row, pl.ds(h * hd, hd), :]
        first = gate_ref[row, pl.ds(h, 1), :]
        second = gate_ref[row, pl.ds(heads + h, 1), :]
        scale = small_ref[group, pl.ds(3, 1), pl.ds(512 + h, 1)]
        gate = first * (second * scale - 1.0) + 2.0
        centre = jnp.sum(g_t.astype(f32) * out_v[row, pl.ds(h * hd, hd), :], axis=0, keepdims=True)
        lse = lse_ref[row, pl.ds(h, 1), :]
        sums_of = []
        for c in range(seq // LANES):
            lanes = pl.ds(c * LANES, LANES)
            at = slice(c * LANES, (c + 1) * LANES)
            pos = pos_v[h, :, lanes]
            p = jnp.exp(sc[b, :, lanes] + (pos * gate[:, at] - lse[:, at]) + mask[row, :, lanes])
            pr[b, :, lanes] = p.astype(bf)
            d = p * (dp[b, :, lanes] - centre[:, at])
            ds[b, :, lanes] = d.astype(bf)
            sums_of.append(jnp.sum(d * pos, axis=0, keepdims=True))
            if own:
                tab = gate[:, at] * d
                if row == 0:
                    table_v[h, :, lanes] = tab
                else:
                    table_v[h, :, lanes] += tab
        if own and row == seqs - 1:
            table_out[h].start()
        dgate = jnp.concatenate(sums_of, axis=1)
        dfirst = dgate * (second * scale - 1.0) * first * (1.0 - first)
        dsecond = dgate * first * scale * second * (1.0 - second)
        gate_parts[i] = (dfirst, dsecond, dgate * first * second)

    def gather(i):
        row, h = divmod(i, heads)
        b = i % 2
        q_t = qkv_v[row, pl.ds(h * hd, hd), :]
        k_t = qkv_v[row, pl.ds(width + h * hd, hd), :]
        g_t = dctx_v[row, pl.ds(h * hd, hd), :]
        for j, d in enumerate((nn(k_t, ds[b]) * hd**-0.5, nt(q_t, ds[b]), nt(g_t, pr[b]))):
            hi = d.astype(bf)
            wide[row, pl.ds(j * width + h * hd, hd), :] = hi
            if own:
                parts[row, pl.ds(j * width + h * hd, hd), :] = (d - hi.astype(f32)).astype(bf)
        if h < heads - 1:
            return
        lines = [gate_parts[row * heads + j][k] for k in (0, 1) for j in range(heads)]
        low = jnp.concatenate(lines + [jnp.zeros((16 - 2 * heads, seq), f32)], axis=0).astype(bf)
        wide[row, pl.ds(3 * width, 16), :] = low
        if row == 0:
            for c in w_in:
                c.wait()
        part = nn(wide[row].T, w_v[...])
        base_in[row].wait()
        base_v[row] = deep_alpha * base_v[row] + part if own else base_v[row] + part
        grad_out[row].start()
        if not own:
            return
        x_in[row].wait()
        x = x_v[row]
        main = wide[row, pl.ds(0, 3 * width), :]
        dw_here = nn(main, x) + nn(parts[row], x)
        dgw = nn(low, x)
        one = sum(jnp.where(lanes_of[j], dgw[j : j + 1], 0.0) for j in range(heads))
        two = sum(jnp.where(lanes_of[j], dgw[heads + j : heads + j + 1], 0.0) for j in range(heads))
        qv = nt(jnp.ones((8, seq), bf), main)[:1]
        lane = lax.broadcasted_iota(jnp.int32, (1, feats), 1)

        def spot_of(k, v):
            return jnp.where(lane == k, jnp.sum(v, axis=1, keepdims=True), 0.0)

        biases = spot_of(0, sum(lines[:heads])) + spot_of(1, sum(lines[heads:]))
        gains = sum(spot_of(j, gate_parts[row * heads + j][2]) for j in range(heads))
        none = jnp.zeros((1, feats), f32)
        qv = jnp.concatenate([qv, none[:, : feats - qv.shape[1]]], axis=1)
        here = jnp.concatenate([one, two, biases, none, qv, gains, none, none], axis=0)
        if row == 0:
            dw_v[...] = dw_here
            tiny_ref[...] = here
        else:
            dw_v[...] += dw_here
            tiny_ref[...] += here
        if row == seqs - 1:
            dw_out.start()

    count = seqs * heads
    score(0)
    for i in range(count):
        if i + 1 < count:
            score(i + 1)
        weigh(i)
        if i:
            gather(i - 1)
    gather(count - 1)
    for c in grad_out:
        c.wait()
    if own:
        for c in table_out + [dw_out]:
            c.wait()


def norm_stats(v):
    mean = jnp.mean(v, axis=-1, keepdims=True)
    cen = v - mean
    rs = lax.rsqrt(jnp.mean(cen * cen, axis=-1, keepdims=True) + norm_eps)
    return cen * rs, rs


def norm_back(g, n, rs, gain):
    gn = g * gain
    return rs * (gn - jnp.mean(gn, axis=-1, keepdims=True) - n * jnp.mean(gn * n, axis=-1, keepdims=True))


def gelu_pair(x):
    cdf = 0.5 + 0.5 * lax.erf(x * 0.5**0.5)
    return x * cdf, cdf + x * jnp.exp(x * x * -0.5) * 0.3989422804014327


def layer_kernel(
    ctx0_ref, ctx1_ref, ctx2_ref, ctx3_ref, x_ref, go_ref, ow0_hbm, ow_hbm, w10_hbm, w1a_hbm, w1b_hbm, small_ref, b1a_ref, b1b_ref,
    w20_hbm, w2a_hbm, w2b_hbm, vec_ref, at_ref,
    out_ref, first_ref, dctx_ref, hid_low_ref, mix_low_ref, first_low_ref, act_ref, pre_low_ref, sums_ref,
    ow_v, w1_v, w2_v, act, slope, plow, sem,
):
    step = pl.program_id(0)
    ctxs = (ctx0_ref, ctx1_ref, ctx2_ref, ctx3_ref)
    width = ow0_hbm.shape[0]
    own = w10_hbm.shape[0]
    half = w1a_hbm.shape[0]
    part = w2a_hbm.shape[1]
    copy = pltpu.make_async_copy
    ow_in = [copy(ow0_hbm, ow_v.at[pl.ds(0, width)], sem.at[0])]
    for i in range(1, len(ctxs)):
        ow_in.append(copy(ow_hbm.at[i - 1, pl.ds(ow_hbm.shape[1] - width, width)], ow_v.at[pl.ds(i * width, width)], sem.at[i]))
    w1_in = [
        copy(w10_hbm, w1_v.at[pl.ds(0, own)], sem.at[4]),
        copy(w1a_hbm, w1_v.at[pl.ds(own, half)], sem.at[5]),
        copy(w1b_hbm, w1_v.at[pl.ds(own + half, half)], sem.at[6]),
    ]
    w2_in = [copy(w20_hbm, w2_v.at[pl.ds(0, own)], sem.at[7])]
    for i in range(1, len(ctxs)):
        for k, src in enumerate((w2a_hbm, w2b_hbm)):
            spot = pl.ds(own + k * half + (i - 1) * part, part)
            w2_in.append(copy(src.at[at_ref[i]], w2_v.at[spot], sem.at[6 + 2 * i + k]))

    @pl.when(step == 0)
    def _():
        for c in ow_in + w1_in + w2_in:
            c.start()
        for c in ow_in:
            c.wait()

    vec = vec_ref[...]
    out_bias, gain1, bias1, bias2, gain2, beta2 = (vec[i : i + 1] for i in range(6))
    total = deep_alpha * x_ref[...].astype(f32) + out_bias
    for i, c in enumerate(ctxs):
        total = total + nn(c[...], ow_v[pl.ds(i * width, width), :])
    n1, rs1 = norm_stats(total)
    hidden = n1 * gain1 + bias1
    hid_low = hidden.astype(bf)
    hid_low_ref[...] = hid_low

    @pl.when(step == 0)
    def _():
        for c in w1_in:
            c.wait()

    block = 256
    b1 = jnp.concatenate(
        [small_ref[pl.ds(2, 1), :]] + [ref[pl.ds(i, 1), :] for ref in (b1a_ref, b1b_ref) for i in range(len(ctxs) - 1)], axis=1
    )
    blocks = [pl.ds(u, block) for u in range(0, w1_v.shape[0], block)]
    for at in blocks:
        pre = nt(hid_low, w1_v[at, :]) + b1[:, at.start : at.start + block]
        a, s = gelu_pair(pre)
        act[:, at] = a.astype(bf)
        slope[:, at] = s

    @pl.when(step == 0)
    def _():
        for c in w2_in:
            c.wait()

    mixed = deep_alpha * hidden + bias2 + nn(act[...], w2_v[...])
    act_ref[...] = act[:, pl.ds(0, own)]
    n2, rs2 = norm_stats(mixed)
    out_ref[...] = n2 * gain2 + beta2
    g = go_ref[...].astype(f32)
    grad_mixed = norm_back(g, n2, rs2, gain2)
    mix_low = grad_mixed.astype(bf)
    mix_low_ref[...] = mix_low
    line = []
    for at in blocks:
        d = nt(mix_low, w2_v[at, :]) * slope[:, at]
        if at.start < own:
            line.append(jnp.sum(d, axis=0, keepdims=True))
        plow[:, at] = d.astype(bf)
    b1_sum = jnp.concatenate(line, axis=1)
    grad_hidden = deep_alpha * grad_mixed + nn(plow[...], w1_v[...])
    pre_low_ref[...] = plow[:, pl.ds(0, own)]
    grad_first = norm_back(grad_hidden, n1, rs1, gain1)
    first_ref[...] = grad_first
    first_low = grad_first.astype(bf)
    first_low_ref[...] = first_low
    first_rest = (grad_first - first_low.astype(f32)).astype(bf)
    dctx = (nt(ow_v[...], first_low) + nt(ow_v[...], first_rest)).astype(bf)
    for i in range(len(ctxs)):
        dctx_ref[i, 0] = dctx[i * width : (i + 1) * width]

    def col(v):
        return jnp.sum(v, axis=0, keepdims=True)

    sums = jnp.concatenate(
        [
            col(g * n2), col(g), col(grad_mixed), col(grad_hidden * n1), col(grad_hidden), col(grad_first), b1_sum,
            jnp.zeros_like(b1_sum),
        ],
        axis=0,
    )

    @pl.when(step == 0)
    def _():
        sums_ref[...] = sums

    @pl.when(step != 0)
    def _():
        sums_ref[...] += sums


def table_kernel(heads, tops, lows, buckets_ref, val_ref, out_ref):
    rows, cols = buckets_ref.shape
    top_id = lax.broadcasted_iota(jnp.int32, (tops, cols), 0)
    low_id = lax.broadcasted_iota(jnp.int32, (lows, cols), 0)
    unroll = 32

    def group(g, acc):
        for u in range(0, unroll, 8):
            at = pl.ds(pl.multiple_of(g * unroll, unroll) + u, 8)
            idx = buckets_ref[at, :]
            high = idx >> 4
            low = idx & 15
            vals = [val_ref[h, at, :] for h in range(heads)]
            for i in range(8):
                a = jnp.where(high[i : i + 1] == top_id, 1.0, 0.0).astype(bf)
                hit = low[i : i + 1] == low_id
                b = jnp.concatenate([jnp.where(hit, v[i : i + 1], 0.0).astype(bf) for v in vals], axis=0)
                acc = acc + nt(a, b)
        return acc

    out_ref[...] = lax.fori_loop(0, rows // unroll, group, jnp.zeros(out_ref.shape, f32))


def table_grad(buckets_t, values, size):
    heads, seq, _ = values.shape
    lows = 16
    tops = -(-size // lows // 8) * 8
    return pl.pallas_call(
        functools.partial(table_kernel, heads, tops, lows),
        out_shape=jax.ShapeDtypeStruct((tops, heads * lows), f32),
        compiler_params=params(LIMIT),
        cost_estimate=pl.CostEstimate(flops=COST, bytes_accessed=1 << 20, transcendentals=0),
        name="table_grad",
    )(buckets_t, values)


def rotate(x, by, n):
    return lax.ppermute(x, "mp", [(i, (i + by) % n) for i in range(n)])


def swap(x, bit, n, axis="dp"):
    return lax.ppermute(x, axis, [(i, i ^ bit) for i in range(n)])


def after(x, *earlier):
    return lax.optimization_barrier((x,) + earlier)[0]


def joined(pieces, got, bit, index, have):
    at = 1 + sum(b > bit for b in have)
    mine = (index & bit) != 0
    return jnp.stack([jnp.where(mine, got, pieces), jnp.where(mine, pieces, got)], axis=at)


def body(
    n_dp, n_mp,
    tokens, segment_ids, buckets, qkv_weight, qv_bias, rel_table, gate_weight, gate_bias, gate_scale, out_weight,
    out_bias, ln1_gain, ln1_bias, fc1_weight, fc1_bias, fc2_weight, fc2_bias, ln2_gain, ln2_bias, grad_out,
):
    rows, feats = tokens.shape
    seqs, seq = segment_ids.shape
    size, heads = rel_table.shape
    hd, gates = gate_weight.shape
    width = heads * hd
    units = fc1_weight.shape[1]
    me = lax.axis_index("mp")
    dp = lax.axis_index("dp")
    order = ((me - jnp.arange(n_mp)) % n_mp).astype(jnp.int32)
    bits = [1 << i for i in range(n_dp.bit_length() - 1)]
    plane = bits[1:]
    others = n_mp - 1
    core = dp & 1
    sds = jax.ShapeDtypeStruct

    hbm = pl.BlockSpec(memory_space=pl.ANY)
    smem = pl.BlockSpec(memory_space=pltpu.SMEM)
    full = pl.BlockSpec()
    square = pltpu.VMEM((seqs, seq, seq), f32)
    pair = pltpu.VMEM((2, seq, seq), f32)
    low_pair = pltpu.VMEM((2, seq, seq), bf)
    segq = segment_ids[:, None, :]
    segk = segment_ids[:, :, None]
    gw = jnp.tile(gate_weight.T, (1, n_mp * heads))
    lines_t = pltpu.VMEM((seqs, 3 * width, seq), bf)
    outs_t = pltpu.VMEM((seqs, width, seq), f32)
    tables_t = pltpu.VMEM((heads, seq, seq), f32)

    def attend(i, sources, *deps):
        wt, wl, sm, pos = sources
        return pl.pallas_call(
            functools.partial(attend_kernel, heads, hd, max(i - 1, 0)),
            in_specs=[hbm] * 4 + [full] * 4 + [smem] * 2,
            out_specs=[hbm] * 3 + [full] * 2,
            scratch_shapes=[
                pltpu.VMEM((seqs, seq, feats), bf), pltpu.VMEM((3 * width, feats), bf), tables_t, lines_t,
                pltpu.VMEM((rows, width), bf), outs_t, square, pair, low_pair,
                pltpu.SemaphoreType.DMA((4 * seqs + 2 + heads,)),
            ],
            out_shape=[
                sds((seqs, 3 * width, seq), bf), sds((rows, width), bf), sds((seqs, width, seq), f32),
                sds((seqs, 8, seq), f32), sds((seqs, 8, seq), f32),
            ],
            compiler_params=params(LIMIT),
            cost_estimate=pl.CostEstimate(flops=COST, bytes_accessed=1 << 20, transcendentals=0),
            name="attend",
        )(tokens, wt, wl, pos, gw, sm, segq, segk, gate_bias, after(order[i : i + 1], *deps))

    def attend_back(i, sources, front, dctx, base, *deps):
        wt, wl, sm, pos = sources
        qkv_t, _, out_t, lse, gate = front
        own = i == 0
        out_shape = [sds((rows, feats), f32)]
        out_specs = [hbm]
        scratch = [
            pltpu.VMEM((3 * width + 16, feats), bf), tables_t, lines_t, outs_t, pltpu.VMEM((seqs, width, seq), bf),
            pltpu.VMEM((seqs, seq, feats), f32), square, pair, pair, low_pair, low_pair,
            pltpu.VMEM((seqs, 3 * width + 16, seq), bf), pltpu.SemaphoreType.DMA((5 * seqs + 2 + heads,)),
        ]
        if own:
            out_shape += [sds((3 * width, feats), f32), sds((8, feats), f32), sds((heads, seq, seq), f32)]
            out_specs += [hbm, full, hbm]
            scratch += [
                pltpu.VMEM((3 * width, feats), f32), pltpu.VMEM((seqs, seq, feats), bf), lines_t, tables_t,
                pltpu.SemaphoreType.DMA((heads + 1 + seqs,)),
            ]
        return pl.pallas_call(
            functools.partial(attend_back_kernel, heads, hd, i),
            in_specs=[hbm] * 8 + [full] * 4 + [smem] + [full] * 2,
            out_specs=out_specs,
            scratch_shapes=scratch,
            out_shape=out_shape,
            compiler_params=params(LIMIT),
            cost_estimate=pl.CostEstimate(flops=COST, bytes_accessed=1 << 20, transcendentals=0),
            name="attend_back",
        )(
            wt, wl, pos, qkv_t, out_t, dctx, base, tokens, gw, sm, segq, segk, after(order[i : i + 1], *deps), lse, gate
        )

    def piece(w, parts=1):
        per = w.shape[0] // n_dp // parts
        w = w.reshape(parts, n_dp, per, w.shape[1])
        return lax.dynamic_index_in_dim(w, dp, 1, False).reshape(parts * per, -1)

    alike = [[m * n_dp + d for m in range(n_mp) for d in range(n_dp) if d % 2 == c] for c in range(2)]
    yx = dp // 2
    per2 = units // n_dp
    piece2 = lax.dynamic_slice_in_dim(fc2_weight, core * (units // 2) + yx * per2, per2, 0)
    half2 = lax.all_gather(piece2, ("mp", "dp"), axis_index_groups=alike)

    small, cuts = lines_of(after(rel_table.T, piece2), fc1_bias[None], qv_bias, gate_scale[None])
    w0 = jnp.concatenate([qkv_weight.transpose(0, 2, 1).reshape(3 * width, feats), out_weight], axis=0)
    piece0 = jnp.concatenate([piece(w0, 2), cuts], axis=0)
    w0 = w0.reshape(2, 2 * width, feats)
    z0 = [rotate(piece0, r, n_mp) for r in range(1, n_mp)]
    buckets_t = buckets.T
    pos_own = bias_of(after(buckets_t, piece0), small[None], heads, size)
    z0, pos_own = lax.optimization_barrier((z0, pos_own))
    z0 = jnp.stack(z0)

    mid = 2 * width // n_dp
    got = z0[:, 2 * mid :].astype(f32)
    smalls = (got[:, 0:4] + got[:, 4:8]) + got[:, 8:12]
    w1_rows = fc1_weight.T
    mid1 = units // n_dp // 2
    piece1 = lax.dynamic_slice(w1_rows.reshape(2, 2, n_dp // 2, mid1, feats), (core, 0, yx, 0, 0), (1, 2, 1, mid1, feats))
    piece1 = after(piece1.reshape(2 * mid1, feats), z0)
    own_sources = (w0, w0[1:], small[None], pos_own)
    spreads = [z0[:, :mid], z0[:, mid : 2 * mid]]
    routes = [plane[::-1], plane]
    covers = [lambda *deps: bias_of(after(buckets_t, *deps), smalls, heads, size), lambda *deps: attend(0, own_sources, *deps)]
    done = []
    for step in range(len(plane)):
        gots = [swap(v, route[step], n_dp) for v, route in zip(spreads, routes)]
        if step == 0:
            z1 = [rotate(piece1, r, n_mp) for r in range(1, n_mp)]
        if step < len(covers):
            result = covers[step](*spreads)
            gots, result = lax.optimization_barrier((gots, result))
            done.append(result)
        spreads = [joined(v, g, route[step], dp, route[:step]) for v, g, route in zip(spreads, gots, routes)]
    for step in range(len(plane), len(covers)):
        done.append(covers[step]())
    pos_rest, front = done
    fronts = [front]
    spreads, z1 = lax.optimization_barrier((spreads, z1))
    gots = [swap(v, 1, n_dp) for v in spreads]
    top, low = (joined(v, g, 1, dp, plane).reshape(others, 2 * width, feats) for v, g in zip(spreads, gots))
    rest_sources = (top, low, smalls, pos_rest)

    z1 = jnp.stack(z1)
    spreads = [z1[:, :mid1], z1[:, mid1:]]
    for step in range(len(plane)):
        gots = [swap(v, route[step], n_dp) for v, route in zip(spreads, routes)]
        if step + 1 < n_mp:
            result = attend(step + 1, rest_sources, *spreads)
            gots, result = lax.optimization_barrier((gots, result))
            fronts.append(result)
        spreads = [joined(v, g, route[step], dp, route[:step]) for v, g, route in zip(spreads, gots, routes)]
    half = others * units // 2
    w1a = jnp.stack(spreads, axis=1).reshape(half, feats)
    w1b = swap(w1a, 1, n_dp)
    w2a = half2.reshape(n_mp, units // 2, feats)
    w2b = swap(w2a, 1, n_dp)
    for i in range(len(fronts), n_mp):
        fronts.append(attend(i, rest_sources, w1a, w2a))
    ctxs = [f[1] for f in fronts]
    b1o = smalls[:, 2]
    b1a = jnp.where(core == 1, b1o[:, units // 2 :], b1o[:, : units // 2])
    b1b = jnp.where(core == 1, b1o[:, : units // 2], b1o[:, units // 2 :])

    vec = jnp.concatenate([out_bias, ln1_gain, ln1_bias, fc2_bias, ln2_gain, ln2_bias]).reshape(6, feats)
    tile = 256

    def row(n):
        return pl.BlockSpec((tile, n), lambda i: (i, 0))

    outs = pl.pallas_call(
        layer_kernel,
        grid=(rows // tile,),
        in_specs=[row(width)] * n_mp
        + [row(feats), row(feats)]
        + [hbm] * 5
        + [full] * 3
        + [hbm] * 3
        + [full, smem],
        out_specs=[
            row(feats), row(feats), pl.BlockSpec((n_mp, 1, width, tile), lambda i: (0, i * tile // seq, 0, i % (seq // tile))),
            row(feats), row(feats), row(feats), row(units), row(units), pl.BlockSpec((8, feats), lambda i: (0, 0)),
        ],
        scratch_shapes=[
            pltpu.VMEM((n_mp * width, feats), bf), pltpu.VMEM((n_mp * units, feats), bf), pltpu.VMEM((n_mp * units, feats), bf),
            pltpu.VMEM((tile, n_mp * units), bf), pltpu.VMEM((tile, n_mp * units), f32), pltpu.VMEM((tile, n_mp * units), bf),
            pltpu.SemaphoreType.DMA((8 + 2 * others,)),
        ],
        out_shape=[
            sds((rows, feats), f32), sds((rows, feats), f32), sds((n_mp, seqs, width, seq), bf), sds((rows, feats), bf),
            sds((rows, feats), bf), sds((rows, feats), bf), sds((rows, units), bf), sds((rows, units), bf), sds((8, feats), f32),
        ],
        compiler_params=params(LIMIT),
        cost_estimate=pl.CostEstimate(flops=4 * COST, bytes_accessed=1 << 24, transcendentals=0),
        name="layer",
    )(*ctxs, tokens, grad_out, out_weight, low, w1_rows, w1a, w1b, small, b1a, b1b, fc2_weight, w2a, w2b, vec, order)
    normed, grad_first = outs[:2]
    dctx = outs[2]
    hid_low, mix_low, first_low, act_own, pre_own, sums = outs[3:]

    def outer(a, b):
        return lax.dot_general(a, b, (((0,), (0,)), ((), ())), preferred_element_type=f32)

    big = jnp.concatenate([outer(ctxs[0], first_low), outer(hid_low, pre_own), outer(act_own, mix_low)], axis=0).astype(bf)
    back, dw, tiny, acc = attend_back(0, own_sources, front, dctx, grad_first, big)
    big = lax.psum_scatter(big, "dp", scatter_dimension=0, tiled=True)

    shared = tiny[:3]
    turned = [rotate(shared, r, n_mp) for r in range(1, n_mp)]
    table = table_grad(after(buckets_t, shared), acc, size)
    table, turned, big = lax.optimization_barrier((table, turned, big))
    big = lax.all_gather(big, "dp", tiled=True)
    turned = [shared] + list(turned)
    while len(turned) > 1:
        turned = [a + b for a, b in zip(turned[: len(turned) // 2], turned[len(turned) // 2 :])]
    table = jnp.pad(table, ((0, 0), (0, feats - table.shape[1])))
    extra = jnp.concatenate([sums, turned[0], tiny[3:], table], axis=0)
    count = extra.shape[0] // 2

    def parted(flip):
        def pick(v):
            v = v.reshape(2, -1, feats)
            return jnp.where((core == 1) != flip, v[1], v[0])

        return jnp.concatenate([pick(dw), pick(extra)])

    total = parted(False) + swap(parted(True), 1, n_dp)
    cut = dw.shape[0] // 2
    i = 1
    for bit in plane:
        low_part = lax.reduce_precision(total[cut:], 8, 7)
        sent = jnp.concatenate([total[:cut], low_part, total[cut:] - low_part])
        sent = lax.reduce_precision(sent, 8, 7).astype(bf)
        got = swap(sent, bit, n_dp)
        if i < n_mp:
            back = attend_back(i, rest_sources, fronts[i], dctx, back, sent)[0]
            got, back = lax.optimization_barrier((got, back))
            if i == n_mp - 2:
                big, back = lax.optimization_barrier((big, back))
            i += 1
        both = sent.astype(f32) + got.astype(f32)
        total = jnp.concatenate([both[:cut], both[cut : cut + count] + both[cut + count :]])
    got = swap(total, 1, n_dp)
    while i < n_mp:
        back = attend_back(i, rest_sources, fronts[i], dctx, back, total)[0]
        i += 1
    input_grad, got, big = lax.optimization_barrier((back, got, big))
    first = jnp.where(core == 1, got, total)
    second = jnp.where(core == 1, total, got)
    dw = jnp.concatenate([first[:cut], second[:cut]]).reshape(3, width, feats).transpose(0, 2, 1)
    extra = jnp.concatenate([first[cut:], second[cut:]])

    sums = extra[:8]
    halves = extra[8:10].reshape(2, n_mp * heads, hd).sum(axis=1)
    grad_gate_weight = jnp.repeat(halves, gates // 2, axis=0).T
    grad_gate_bias = jnp.repeat(extra[10, :2], gates // 2)
    dqv_bias = jnp.stack([extra[12, :width], extra[12, 2 * width : 3 * width]])
    grad_gate_scale = extra[13, :heads]
    lows = 16
    grad_table = extra[16:, : heads * lows].reshape(-1, heads, lows).transpose(0, 2, 1).reshape(-1, heads)[:size]
    big = big.astype(f32)
    grad_ow = big[:width]
    grad_fc1 = big[width : width + feats]
    grad_fc2 = big[width + feats :]
    return (
        normed, input_grad, dw, dqv_bias, grad_table, grad_gate_weight, grad_gate_bias, grad_gate_scale, grad_ow, sums[5],
        sums[3], sums[4], grad_fc1, sums[6], grad_fc2, sums[2], sums[0], sums[1],
    )


def solution(mesh):
    in_specs = (
        P("dp", None), P("dp", None), P(), P(None, None, "mp"), P(None, "mp"), P(None, "mp"), P(), P(), P("mp"),
        P("mp", None), P(), P(), P(), P(None, "mp"), P("mp"), P("mp", None), P(), P(), P(), P("dp", None),
    )
    out_specs = (
        P("dp", None), P("dp", None), P(None, None, "mp"), P(None, "mp"), P(None, "mp"), P(), P(), P("mp"),
        P("mp", None), P(), P(), P(), P(None, "mp"), P("mp"), P("mp", None), P(), P(), P(),
    )
    fn = functools.partial(body, mesh.shape["dp"], mesh.shape["mp"])
    return jax.shard_map(fn, mesh=mesh, in_specs=in_specs, out_specs=out_specs, check_vma=False)
```

```python
import functools

import jax
import jax.numpy as jnp
from jax import lax
from jax.experimental import pallas as pl
from jax.experimental.pallas import tpu as pltpu
from jax.sharding import PartitionSpec as P

norm_eps = 1e-05
deep_alpha = 24.0**0.25
masked_score = -1e30
bf = jnp.bfloat16
f32 = jnp.float32
LANES = 128
LIMIT = 60
COST = 3_000_000_000


def nn(a, b):
    return lax.dot_general(a, b, (((1,), (0,)), ((), ())), preferred_element_type=f32)


def nt(a, b):
    return lax.dot_general(a, b, (((1,), (1,)), ((), ())), preferred_element_type=f32)


def params(mib):
    return pltpu.CompilerParams(vmem_limit_bytes=mib * 1024 * 1024)


def lines_kernel(table_ref, b1_ref, qv_ref, scale_ref, out_ref, cut_ref):
    heads, size = table_ref.shape
    feats = out_ref.shape[1]
    width = qv_ref.shape[1]
    out_ref[...] = jnp.zeros_like(out_ref)
    per = -(-size // LANES) * LANES
    for h in range(heads):
        out_ref[pl.ds(h * per // feats, 1), pl.ds(h * per % feats, size)] = table_ref[pl.ds(h, 1), :]
    out_ref[pl.ds(2, 1), :] = b1_ref[...]
    out_ref[pl.ds(3, 1), pl.ds(0, width)] = qv_ref[pl.ds(0, 1), :]
    out_ref[pl.ds(3, 1), pl.ds(256, width)] = qv_ref[pl.ds(1, 1), :]
    out_ref[pl.ds(3, 1), pl.ds(512, heads)] = scale_ref[...]
    rest = out_ref[...]
    cuts = []
    for _ in range(3):
        cut = rest.astype(bf).astype(f32)
        cuts.append(cut)
        rest = rest - cut
    cut_ref[...] = jnp.concatenate(cuts + [jnp.zeros_like(rest)], axis=0).astype(bf)


def lines_of(table, b1, qv, scale):
    feats = b1.shape[1]
    return pl.pallas_call(
        lines_kernel,
        out_shape=[jax.ShapeDtypeStruct((4, feats), f32), jax.ShapeDtypeStruct((16, feats), bf)],
        compiler_params=params(LIMIT),
        name="lines",
    )(table, b1, qv, scale)


def bias_kernel(heads, chunks, buckets_ref, small_ref, out_ref):
    rows, cols = buckets_ref.shape
    groups, _, feats = small_ref.shape
    for r in range(0, rows, 8):
        at = pl.ds(r, 8)
        for c in range(cols // LANES):
            lanes = pl.ds(c * LANES, LANES)
            idx = buckets_ref[at, lanes]
            low = idx & (LANES - 1)
            high = idx >> 7
            for h in range(heads):
                got = None
                for k in range(chunks):
                    spot = ((h % 3) * chunks + k) * LANES
                    line = jnp.broadcast_to(
                        small_ref[h // 3, pl.ds(spot // feats, 1), pl.ds(spot % feats, LANES)], (8, LANES)
                    )
                    part = jnp.take_along_axis(line, low, axis=1, mode="promise_in_bounds")
                    got = part if got is None else jnp.where(high == k, part, got)
                out_ref[h, at, lanes] = got


def bias_of(buckets_t, small, heads, size):
    groups, _, feats = small.shape
    seq = buckets_t.shape[0]
    rows = 64
    cost = pl.CostEstimate(flops=COST, bytes_accessed=1 << 20, transcendentals=0)
    return pl.pallas_call(
        functools.partial(bias_kernel, heads * groups, -(-size // LANES)),
        grid=(seq // rows,),
        in_specs=[
            pl.BlockSpec((rows, seq), lambda i: (i, 0)),
            pl.BlockSpec((groups, 4, feats), lambda i: (0, 0, 0)),
        ],
        out_specs=pl.BlockSpec((heads * groups, rows, seq), lambda i: (0, i, 0)),
        out_shape=jax.ShapeDtypeStruct((heads * groups, seq, seq), f32),
        compiler_params=params(LIMIT),
        cost_estimate=cost,
        name="pos_bias",
    )(buckets_t, small)


def head_lanes(shape, head, hd):
    return lax.broadcasted_iota(jnp.int32, shape, 1) // hd == head


def fill_mask(mask, segq_ref, segk_ref, row):
    seq = mask.shape[0]
    for c in range(seq // LANES):
        lanes = pl.ds(c * LANES, LANES)
        mask[:, lanes] = jnp.where(segk_ref[row] == segq_ref[row, :, lanes], 0.0, masked_score)


def attend_kernel(
    heads, hd, x_ref, wt_ref, wl_ref, pos_ref, gw_ref, small_ref, segq_ref, segk_ref, gbias_ref, at_ref,
    qkv_ref, ctx_ref, lse_ref, gate_ref, mask, sc, pr, ctx_t,
):
    group = pl.program_id(0)
    width = heads * hd
    seqs, _, seq = segq_ref.shape
    gates = gw_ref.shape[0]
    half = gates // 2
    cut = wt_ref.shape[1]
    strips = [pl.ds(c, LANES) for c in range(0, seq, LANES)]

    def line(row):
        return pl.ds(row * seq, seq)

    cols = jnp.broadcast_to(small_ref[0, pl.ds(3, 1), pl.ds(0, 512)], (8, 512)).T[:, :1]
    gw = gw_ref[...].astype(f32)
    mine = [jnp.where(head_lanes(gw.shape, at_ref[group] * heads + h, hd), gw, 0.0) for h in range(heads)]
    mine = jnp.concatenate(mine, axis=0).astype(bf)
    bias_a = gbias_ref[0] + gbias_ref[1] + gbias_ref[2] + gbias_ref[3]
    bias_b = gbias_ref[4] + gbias_ref[5] + gbias_ref[6] + gbias_ref[7]
    lins = {}

    def project(row):
        x = x_ref[line(row), :]
        upper = nt(wt_ref[0], x)
        lower = nt(wl_ref[0], x)
        qkv_ref[0, row, pl.ds(0, width), :] = (upper[:width] + cols[:width]).astype(bf) * bf(hd**-0.5)
        qkv_ref[0, row, pl.ds(width, width), :] = upper[width:cut].astype(bf)
        qkv_ref[0, row, pl.ds(2 * width, width), :] = (lower + cols[256 : 256 + width]).astype(bf)
        lins[row] = nt(mine, x)
        fill_mask(mask.at[row], segq_ref, segk_ref, row)

    def score(i):
        row, h = divmod(i, heads)
        k_t = qkv_ref[0, row, pl.ds(width + h * hd, hd), :]
        sc[i % 2] = nn(k_t.T, qkv_ref[0, row, pl.ds(h * hd, hd), :])

    def weigh(i):
        row, h = divmod(i, heads)
        lin = lins[row]
        first = jax.nn.sigmoid(jnp.sum(lin[h * gates : h * gates + half], axis=0, keepdims=True) + bias_a)
        second = jax.nn.sigmoid(jnp.sum(lin[h * gates + half : (h + 1) * gates], axis=0, keepdims=True) + bias_b)
        gate = first * (second * small_ref[0, pl.ds(3, 1), pl.ds(512 + h, 1)] - 1.0) + 2.0
        gate_ref[0, row, pl.ds(h, 1), :] = first
        gate_ref[0, row, pl.ds(heads + h, 1), :] = second
        for at in strips:
            s = sc[i % 2, :, at] + pos_ref[h, :, at] * gate[:, at.start : at.start + LANES] + mask[row, :, at]
            top = jnp.max(s, axis=0, keepdims=True)
            p = jnp.exp(s - top)
            total = jnp.sum(p, axis=0, keepdims=True)
            pr[i % 2, :, at] = (p * (1.0 / total)).astype(bf)
            lse_ref[0, row, pl.ds(h, 1), at] = top + jnp.log(total)

    def gather(i):
        row, h = divmod(i, heads)
        v_t = qkv_ref[0, row, pl.ds(2 * width + h * hd, hd), :]
        ctx_t[pl.ds(h * hd, hd), :] = nn(v_t, pr[i % 2])
        if h == heads - 1:
            ctx_ref[0, line(row), :] = ctx_t[...].T.astype(bf)

    count = seqs * heads
    project(0)
    score(0)
    for i in range(count):
        if i + 1 < count:
            if (i + 1) % heads == 0:
                project((i + 1) // heads)
            score(i + 1)
        weigh(i)
        if i:
            gather(i - 1)
    gather(count - 1)


def back_group(
    heads, hd, own, x_of, w_v, pos_of, gw_ref, small, segq_ref, segk_ref, head0, qkv_of, lse_of, gate_of, dctx_of, add,
    table_v, finish, mask, sc, dp, pr, ds, wide, ready,
):
    width = heads * hd
    seqs, _, seq = segq_ref.shape
    feats = w_v.shape[1]
    strips = [pl.ds(c, LANES) for c in range(0, seq, LANES)]
    gw = gw_ref[...].astype(f32)
    half = gw.shape[0] // 2
    sums = [jnp.sum(gw[:half], axis=0, keepdims=True), jnp.sum(gw[half:], axis=0, keepdims=True)]
    lanes_of = [head_lanes((1, feats), head0 + h, hd) for h in range(heads)]
    gsum = [jnp.where(lanes_of[h], part, 0.0) for part in sums for h in range(heads)]
    w_v[pl.ds(3 * width, 16), :] = jnp.concatenate(gsum + [jnp.zeros((16 - 2 * heads, feats), f32)], axis=0).astype(bf)
    gate_parts = {}

    def score(i):
        row, h = divmod(i, heads)
        if h == 0:
            ready("row", row)
            fill_mask(mask.at[row], segq_ref, segk_ref, row)
        k_t = qkv_of(row, width + h * hd, hd)
        v_t = qkv_of(row, 2 * width + h * hd, hd)
        sc[i % 2] = nn(k_t.T, qkv_of(row, h * hd, hd))
        dp[i % 2] = nn(v_t.T, dctx_of(row, h * hd, hd))

    def weigh(i):
        row, h = divmod(i, heads)
        if row == 0:
            ready("pos", h)
        b = i % 2
        first = gate_of(row, h)
        second = gate_of(row, heads + h)
        scale = small[pl.ds(3, 1), pl.ds(512 + h, 1)]
        gate = first * (second * scale - 1.0) + 2.0
        lse = lse_of(row, h)
        sums_of = []
        for at in strips:
            here = slice(at.start, at.start + LANES)
            pos = pos_of(h, at)
            p = jnp.exp(sc[b, :, at] + (pos * gate[:, here] - lse[:, here]) + mask[row, :, at])
            pr[b, :, at] = p.astype(bf)
            g = dp[b, :, at]
            centre = jnp.sum(p * g, axis=0, keepdims=True)
            low = (p * (g - centre)).astype(bf)
            ds[b, :, at] = low
            d = low.astype(f32)
            sums_of.append(jnp.sum(d * pos, axis=0, keepdims=True))
            if own:
                tab = gate[:, here] * d
                if row == 0:
                    table_v[h, :, at] = tab
                else:
                    table_v[h, :, at] += tab
        if own and row == seqs - 1:
            finish("table", h)
        dgate = jnp.concatenate(sums_of, axis=1)
        dfirst = dgate * (second * scale - 1.0) * first * (1.0 - first)
        dsecond = dgate * first * scale * second * (1.0 - second)
        gate_parts[i] = (dfirst, dsecond, dgate * first * second)

    def gather(i):
        row, h = divmod(i, heads)
        b = i % 2
        q_t = qkv_of(row, h * hd, hd)
        k_t = qkv_of(row, width + h * hd, hd)
        g_t = dctx_of(row, h * hd, hd)
        for j, d in enumerate((nn(k_t, ds[b]) * hd**-0.5, nt(q_t, ds[b]), nt(g_t, pr[b]))):
            wide[row, pl.ds(j * width + h * hd, hd), :] = d.astype(bf)
        if h < heads - 1:
            return
        lines = [gate_parts[row * heads + j][k] for k in (0, 1) for j in range(heads)]
        low = jnp.concatenate(lines + [jnp.zeros((16 - 2 * heads, seq), f32)], axis=0).astype(bf)
        wide[row, pl.ds(3 * width, 16), :] = low
        if row == 0:
            ready("w", 0)
        add(row, nn(wide[row].T, w_v[...]))
        if not own:
            return
        ready("x", row)
        x = x_of(row)
        main = wide[row, pl.ds(0, 3 * width), :]
        dw_here = nn(main, x)
        rest = jnp.concatenate(lines, axis=0) - low[: 2 * heads].astype(f32)
        dgw = nn(low, x)[: 2 * heads] + nn(jnp.concatenate([rest.astype(bf)] * 3, axis=0)[:16], x)[: 2 * heads]
        one = sum(jnp.where(lanes_of[j], dgw[j : j + 1], 0.0) for j in range(heads))
        two = sum(jnp.where(lanes_of[j], dgw[heads + j : heads + j + 1], 0.0) for j in range(heads))
        qv = nt(jnp.ones((8, seq), bf), main)[:1]
        lane = lax.broadcasted_iota(jnp.int32, (1, feats), 1)

        def spot_of(k, v):
            return jnp.where(lane == k, jnp.sum(v, axis=1, keepdims=True), 0.0)

        biases = spot_of(0, sum(lines[:heads])) + spot_of(1, sum(lines[heads:]))
        gains = sum(spot_of(j, gate_parts[row * heads + j][2]) for j in range(heads))
        none = jnp.zeros((1, feats), f32)
        qv = jnp.concatenate([qv, none[:, : feats - qv.shape[1]]], axis=1)
        finish("row", row, dw_here, jnp.concatenate([one, two, biases, none, qv, gains, none, none], axis=0))

    count = seqs * heads
    score(0)
    for i in range(count):
        if i + 1 < count:
            score(i + 1)
        weigh(i)
        if i:
            gather(i - 1)
    gather(count - 1)


def back_own_kernel(
    heads, hd, wt_hbm, wl_hbm, pos_hbm, qkv_hbm, dctx_hbm, base_hbm, x_hbm,
    gw_ref, small_ref, segq_ref, segk_ref, at_ref, lse_ref, gate_ref,
    grad_hbm, dw_hbm, tiny_ref, table_hbm,
    w_v, pos_v, qkv_v, dctx_v, base_v, mask, sc, dp, pr, ds, wide, dw_v, x_v, table_v, sem,
):
    width = heads * hd
    seqs, _, seq = segq_ref.shape
    cut = wt_hbm.shape[1]
    count = iter(range(64))

    def line(row):
        return pl.ds(row * seq, seq)

    def copy(src, dst):
        return pltpu.make_async_copy(src, dst, sem.at[next(count)])

    w_in = [
        copy(wt_hbm.at[0], w_v.at[pl.ds(0, cut)]),
        copy(wl_hbm.at[0, pl.ds(0, 3 * width - cut)], w_v.at[pl.ds(cut, 3 * width - cut)]),
    ]
    pos_in = [copy(pos_hbm.at[h], pos_v.at[h]) for h in range(heads)]
    row_in = [[copy(qkv_hbm.at[0, r], qkv_v.at[r]), copy(dctx_hbm.at[0, r], dctx_v.at[r])] for r in range(seqs)]
    base_in = [copy(base_hbm.at[line(r)], base_v.at[r]) for r in range(seqs)]
    grad_out = [copy(base_v.at[r], grad_hbm.at[line(r)]) for r in range(seqs)]
    x_in = [copy(x_hbm.at[line(r)], x_v.at[r]) for r in range(seqs)]
    table_out = [copy(table_v.at[h], table_hbm.at[h]) for h in range(heads)]
    dw_out = copy(dw_v, dw_hbm)
    for c in row_in[0] + [pos_in[0]] + [c for r in row_in[1:] for c in r] + pos_in[1:] + w_in + base_in + x_in:
        c.start()

    def ready(what, i):
        for c in {"row": lambda: row_in[i], "pos": lambda: [pos_in[i]], "w": lambda: w_in, "x": lambda: [x_in[i]]}[what]():
            c.wait()

    def add(row, part):
        base_in[row].wait()
        base_v[row] = deep_alpha * base_v[row] + part
        grad_out[row].start()

    def finish(what, i, *values):
        if what == "table":
            table_out[i].start()
        elif i == 0:
            dw_v[...], tiny_ref[...] = values
        else:
            dw_v[...] += values[0]
            tiny_ref[...] += values[1]
            if i == seqs - 1:
                dw_out.start()

    back_group(
        heads, hd, True, lambda r: x_v[r], w_v, lambda h, at: pos_v[h, :, at], gw_ref, small_ref.at[0], segq_ref, segk_ref,
        at_ref[0] * heads, lambda r, i, n: qkv_v[r, pl.ds(i, n), :], lambda r, h: lse_ref[0, r, pl.ds(h, 1), :],
        lambda r, h: gate_ref[0, r, pl.ds(h, 1), :], lambda r, i, n: dctx_v[r, pl.ds(i, n), :], add, table_v, finish,
        mask, sc, dp, pr, ds, wide, ready,
    )
    for c in grad_out + table_out + [dw_out]:
        c.wait()


def back_rest_kernel(
    heads, hd, first, wt_ref, wl_ref, pos_ref, qkv_ref, dctx_ref, base_hbm,
    gw_ref, small_ref, segq_ref, segk_ref, at_ref, lse_ref, gate_ref,
    grad_hbm,
    w_v, base_v, mask, sc, dp, pr, ds, wide, sem,
):
    step = pl.program_id(0)
    last = pl.num_programs(0) - 1
    width = heads * hd
    seqs, _, seq = segq_ref.shape
    cut = wt_ref.shape[1]

    def line(row):
        return pl.ds(row * seq, seq)

    base_in = [pltpu.make_async_copy(base_hbm.at[line(r)], base_v.at[r], sem.at[r]) for r in range(seqs)]
    grad_out = [pltpu.make_async_copy(base_v.at[r], grad_hbm.at[line(r)], sem.at[seqs + r]) for r in range(seqs)]

    @pl.when(step == 0)
    def _():
        for c in base_in:
            c.start()

    w_v[pl.ds(0, cut), :] = wt_ref[0]
    w_v[pl.ds(cut, 3 * width - cut), :] = wl_ref[0]

    def add(row, part):
        @pl.when(step == 0)
        def _():
            base_in[row].wait()

        base_v[row] += part

        @pl.when(step == last)
        def _():
            grad_out[row].start()

    back_group(
        heads, hd, False, None, w_v, lambda h, at: pos_ref[h, :, at], gw_ref, small_ref.at[0], segq_ref, segk_ref,
        at_ref[first + step] * heads, lambda r, i, n: qkv_ref[0, r, pl.ds(i, n), :], lambda r, h: lse_ref[0, r, pl.ds(h, 1), :],
        lambda r, h: gate_ref[0, r, pl.ds(h, 1), :], lambda r, i, n: dctx_ref[0, r, pl.ds(i, n), :], add, None, None,
        mask, sc, dp, pr, ds, wide, lambda what, i: None,
    )

    @pl.when(step == last)
    def _():
        for c in grad_out:
            c.wait()


def norm_stats(v):
    mean = jnp.mean(v, axis=-1, keepdims=True)
    cen = v - mean
    rs = lax.rsqrt(jnp.mean(cen * cen, axis=-1, keepdims=True) + norm_eps)
    return cen * rs, rs


def norm_back(g, n, rs, gain):
    gn = g * gain
    return rs * (gn - jnp.mean(gn, axis=-1, keepdims=True) - n * jnp.mean(gn * n, axis=-1, keepdims=True))


def gelu_pair(x):
    cdf = 0.5 + 0.5 * lax.erf(x * 0.5**0.5)
    return x * cdf, cdf + x * jnp.exp(x * x * -0.5) * 0.3989422804014327


def layer_kernel(
    ctx0_ref, ctx_ref, x_ref, go_ref, ow0_hbm, ow_hbm, w10_hbm, small_ref, smalls_ref,
    w20_hbm, all_hbm, vec_ref, at_ref,
    out_ref, first_ref, dctx_ref, hid_low_ref, mix_low_ref, first_low_ref, act_ref, pre_low_ref, sums_ref,
    ow_v, w1_v, w2_v, act, slope, plow, sem,
):
    step = pl.program_id(0)
    ctxs = [ctx0_ref.at[0]] + [ctx_ref.at[i] for i in range(ctx_ref.shape[0])]
    width = ow0_hbm.shape[0]
    own = w10_hbm.shape[0]
    count = iter(range(128))
    _, pieces, _, per, feats = all_hbm.shape

    def copy(src, dst):
        return pltpu.make_async_copy(src, dst, sem.at[next(count)])

    ow_in = [copy(ow0_hbm, ow_v.at[pl.ds(0, width)])]
    for i in range(1, len(ctxs)):
        ow_in.append(copy(ow_hbm.at[i - 1, pl.ds(ow_hbm.shape[1] - width, width)], ow_v.at[pl.ds(i * width, width)]))
    w_in = []
    for k, (mine, all_v) in enumerate(((w10_hbm, w1_v), (w20_hbm, w2_v))):
        w_in.append([copy(mine, all_v.at[pl.ds(0, own)])])
        parted = all_v.reshape(len(ctxs) * pieces, per, feats)
        for i in range(1, len(ctxs)):
            w_in[k].append(copy(all_hbm.at[at_ref[i], :, k], parted.at[pl.ds(i * pieces, pieces)]))
    w1_in, w2_in = w_in

    @pl.when(step == 0)
    def _():
        for c in ow_in + w1_in + w2_in:
            c.start()
        for c in ow_in:
            c.wait()

    vec = vec_ref[...]
    out_bias, gain1, bias1, bias2, gain2, beta2 = (vec[i : i + 1] for i in range(6))
    total = deep_alpha * x_ref[...].astype(f32) + out_bias
    for i, c in enumerate(ctxs):
        total = total + nn(c[...], ow_v[pl.ds(i * width, width), :])
    n1, rs1 = norm_stats(total)
    hidden = n1 * gain1 + bias1
    hid_low = hidden.astype(bf)
    hid_low_ref[...] = hid_low

    @pl.when(step == 0)
    def _():
        for c in w1_in:
            c.wait()

    block = 256
    b1 = [small_ref[pl.ds(2, 1), :]] + [smalls_ref[i, pl.ds(2, 1), :] for i in range(len(ctxs) - 1)]
    b1 = jnp.concatenate(b1, axis=1)
    blocks = [pl.ds(u, block) for u in range(0, w1_v.shape[0], block)]
    for at in blocks:
        pre = nt(hid_low, w1_v[at, :]) + b1[:, at.start : at.start + block]
        a, s = gelu_pair(pre)
        act[:, at] = a.astype(bf)
        slope[:, at] = s

    @pl.when(step == 0)
    def _():
        for c in w2_in:
            c.wait()

    mixed = deep_alpha * hidden + bias2 + nn(act[...], w2_v[...])
    act_ref[...] = act[:, pl.ds(0, own)]
    n2, rs2 = norm_stats(mixed)
    out_ref[...] = n2 * gain2 + beta2
    g = go_ref[...].astype(f32)
    grad_mixed = norm_back(g, n2, rs2, gain2)
    mix_low = grad_mixed.astype(bf)
    mix_low_ref[...] = mix_low
    line = []
    for at in blocks:
        d = nt(mix_low, w2_v[at, :]) * slope[:, at]
        if at.start < own:
            line.append(jnp.sum(d, axis=0, keepdims=True))
        plow[:, at] = d.astype(bf)
    b1_sum = jnp.concatenate(line, axis=1)
    grad_hidden = deep_alpha * grad_mixed + nn(plow[...], w1_v[...])
    pre_low_ref[...] = plow[:, pl.ds(0, own)]
    grad_first = norm_back(grad_hidden, n1, rs1, gain1)
    first_ref[...] = grad_first
    first_low = grad_first.astype(bf)
    first_low_ref[...] = first_low
    dctx = nt(ow_v[...], first_low).astype(bf)
    for i in range(len(ctxs)):
        dctx_ref[i, 0] = dctx[i * width : (i + 1) * width]

    def col(v):
        return jnp.sum(v, axis=0, keepdims=True)

    sums = jnp.concatenate(
        [
            col(g * n2), col(g), col(grad_mixed), col(grad_hidden * n1), col(grad_hidden), col(grad_first), b1_sum,
            jnp.zeros_like(b1_sum),
        ],
        axis=0,
    )

    @pl.when(step == 0)
    def _():
        sums_ref[...] = sums

    @pl.when(step != 0)
    def _():
        sums_ref[...] += sums


def table_kernel(heads, tops, lows, buckets_ref, val_ref, out_ref):
    rows, cols = buckets_ref.shape
    top_id = lax.broadcasted_iota(jnp.int32, (tops, cols), 0)
    low_id = lax.broadcasted_iota(jnp.int32, (lows, cols), 0)
    unroll = 32

    def group(g, acc):
        for u in range(0, unroll, 8):
            at = pl.ds(pl.multiple_of(g * unroll, unroll) + u, 8)
            idx = buckets_ref[at, :]
            high = idx >> 4
            low = idx & 15
            vals = [val_ref[h, at, :] for h in range(heads)]
            for i in range(8):
                a = jnp.where(high[i : i + 1] == top_id, 1.0, 0.0).astype(bf)
                hit = low[i : i + 1] == low_id
                b = jnp.concatenate([jnp.where(hit, v[i : i + 1], 0.0).astype(bf) for v in vals], axis=0)
                acc = acc + nt(a, b)
        return acc

    out_ref[...] = lax.fori_loop(0, rows // unroll, group, jnp.zeros(out_ref.shape, f32))


def table_grad(buckets_t, values, size):
    heads, seq, _ = values.shape
    lows = 16
    tops = -(-size // lows // 8) * 8
    return pl.pallas_call(
        functools.partial(table_kernel, heads, tops, lows),
        out_shape=jax.ShapeDtypeStruct((tops, heads * lows), f32),
        compiler_params=params(LIMIT),
        cost_estimate=pl.CostEstimate(flops=COST, bytes_accessed=1 << 20, transcendentals=0),
        name="table_grad",
    )(buckets_t, values)


def finish_kernel(
    heads, hd, size, core_ref, total_ref, got_ref, big_ref, big_got_ref,
    dw_ref, ow_ref, fc1_ref, fc2_ref, table_ref, gate_ref, qv_ref, gate_bias_ref, scale_ref, *sum_refs,
):
    later = core_ref[0] == 1
    total, got = total_ref[...], got_ref[...]
    first = jnp.where(later, got, total)
    second = jnp.where(later, total, got)
    cut = dw_ref.shape[0] // 2
    dw_ref[pl.ds(0, cut), :] = first[:cut]
    dw_ref[pl.ds(cut, cut), :] = second[:cut]
    extra = jnp.concatenate([first[cut:], second[cut:]], axis=0)
    feats = extra.shape[1]
    half = big_ref.shape[0]
    width, units = ow_ref.shape[0], fc2_ref.shape[0]
    inner = half - width
    for mine in (False, True):
        part = jnp.where(later == mine, big_ref[...], big_got_ref[...]).astype(f32)
        if not mine:
            ow_ref[...] = part[:width]
            fc1_ref[pl.ds(0, inner), :] = part[width:]
        else:
            fc1_ref[pl.ds(inner, feats - inner), :] = part[: feats - inner]
            fc2_ref[...] = part[feats - inner :]
    for i, ref in enumerate(sum_refs):
        ref[...] = extra[i]
    halves = sum(extra[8:10, c : c + LANES] for c in range(0, feats, LANES))
    halves = sum(halves[:, c : c + hd] for c in range(0, LANES, hd))
    gates = gate_ref.shape[0]
    gate_ref[...] = jnp.concatenate([halves[i : i + 1] for i in range(2) for _ in range(gates // 2)], axis=0)
    qv_ref[pl.ds(0, 1), :] = extra[12:13, :width]
    qv_ref[pl.ds(1, 1), :] = extra[12:13, 2 * width : 3 * width]
    lane = lax.broadcasted_iota(jnp.int32, (1, LANES), 1)
    pair = jnp.where(lane < gates // 2, extra[10:11, 0:1], extra[10:11, 1:2])
    gate_bias_ref[...] = pair[:, :gates]
    scale_ref[...] = extra[13:14, :heads]
    lows = 16
    tops = extra.shape[0] - 16
    wide = tops * lows
    spread = lax.broadcasted_iota(jnp.int32, (lows, wide), 1) % lows == lax.broadcasted_iota(jnp.int32, (lows, wide), 0)
    spread = jnp.where(spread, 1.0, 0.0).astype(bf)
    keep = lax.broadcasted_iota(jnp.int32, (tops, wide), 1) // lows == lax.broadcasted_iota(jnp.int32, (tops, wide), 0)
    for h in range(heads):
        rest = extra[16:, h * lows : (h + 1) * lows]
        line = jnp.zeros((tops, wide), f32)
        for _ in range(3):
            part = rest.astype(bf)
            line = line + nn(part, spread)
            rest = rest - part.astype(f32)
        line = jnp.sum(jnp.where(keep, line, 0.0), axis=0, keepdims=True)
        table_ref[pl.ds(h, 1), :] = line[:, :size]


def finish(heads, hd, gates, size, width, units, core, total, got, big, big_got):
    feats = total.shape[1]
    sds = jax.ShapeDtypeStruct
    vector = sds((feats,), f32)
    outs = pl.pallas_call(
        functools.partial(finish_kernel, heads, hd, size),
        in_specs=[pl.BlockSpec(memory_space=pltpu.SMEM)] + [pl.BlockSpec()] * 4,
        out_shape=[
            sds((3 * width, feats), f32), sds((width, feats), f32), sds((feats, units), f32), sds((units, feats), f32),
            sds((heads, size), f32), sds((gates, hd), f32), sds((2, width), f32), sds((1, gates), f32), sds((1, heads), f32),
        ]
        + [vector] * 7,
        compiler_params=params(LIMIT),
        name="finish",
    )(core, total, got, big, big_got)
    outs = list(outs)
    outs[7], outs[8] = outs[7][0], outs[8][0]
    return outs


def rotate(x, by, n):
    return lax.ppermute(x, "mp", [(i, (i + by) % n) for i in range(n)])


def swap(x, bit, n, axis="dp"):
    return lax.ppermute(x, axis, [(i, i ^ bit) for i in range(n)])


def after(x, *earlier):
    return lax.optimization_barrier((x,) + earlier)[0]


def joined(pieces, got, bit, index, have):
    at = 1 + sum(b > bit for b in have)
    mine = (index & bit) != 0
    return jnp.stack([jnp.where(mine, got, pieces), jnp.where(mine, pieces, got)], axis=at)


def body(
    n_dp, n_mp,
    tokens, segment_ids, buckets, qkv_weight, qv_bias, rel_table, gate_weight, gate_bias, gate_scale, out_weight,
    out_bias, ln1_gain, ln1_bias, fc1_weight, fc1_bias, fc2_weight, fc2_bias, ln2_gain, ln2_bias, grad_out,
):
    rows, feats = tokens.shape
    seqs, seq = segment_ids.shape
    size, heads = rel_table.shape
    hd, gates = gate_weight.shape
    width = heads * hd
    units = fc1_weight.shape[1]
    me = lax.axis_index("mp")
    dp = lax.axis_index("dp")
    order = ((me - jnp.arange(n_mp)) % n_mp).astype(jnp.int32)
    bits = [1 << i for i in range(n_dp.bit_length() - 1)]
    plane = bits[1:]
    others = n_mp - 1
    core = dp & 1
    sds = jax.ShapeDtypeStruct

    hbm = pl.BlockSpec(memory_space=pl.ANY)
    smem = pl.BlockSpec(memory_space=pltpu.SMEM)
    full = pl.BlockSpec()
    square = pltpu.VMEM((seqs, seq, seq), f32)
    pair = pltpu.VMEM((2, seq, seq), f32)
    low_pair = pltpu.VMEM((2, seq, seq), bf)
    segq = segment_ids[:, None, :]
    segk = segment_ids[:, :, None]
    gw = jnp.tile(gate_weight.T, (1, n_mp * heads))
    lines_t = pltpu.VMEM((seqs, 3 * width, seq), bf)
    outs_t = pltpu.VMEM((seqs, width, seq), f32)
    tables_t = pltpu.VMEM((heads, seq, seq), f32)

    def one(*shape):
        return pl.BlockSpec((1,) + shape, lambda s: (s,) + (0,) * len(shape))

    def whole(*shape):
        return pl.BlockSpec(shape, lambda s: (0,) * len(shape))

    def attend(n, sources, *deps):
        wt, wl, sm, pos = sources
        return pl.pallas_call(
            functools.partial(attend_kernel, heads, hd),
            grid=(n,),
            in_specs=[
                whole(rows, feats), one(2 * width, feats), one(width, feats),
                pl.BlockSpec((heads, seq, seq), lambda s: (s, 0, 0)), whole(gates, feats), one(4, feats),
                whole(seqs, 1, seq), whole(seqs, seq, 1), smem, smem,
            ],
            out_specs=[one(seqs, 3 * width, seq), one(rows, width), one(seqs, 8, seq), one(seqs, 8, seq)],
            scratch_shapes=[square, pair, low_pair, pltpu.VMEM((width, seq), f32)],
            out_shape=[
                sds((n, seqs, 3 * width, seq), bf), sds((n, rows, width), bf), sds((n, seqs, 8, seq), f32),
                sds((n, seqs, 8, seq), f32),
            ],
            compiler_params=params(LIMIT),
            cost_estimate=pl.CostEstimate(flops=n * COST, bytes_accessed=1 << 20, transcendentals=0),
            name="attend",
        )(tokens, wt, wl, pos, gw, sm, segq, segk, gate_bias, after(order[:1] if n == 1 else order[1:], *deps))

    back_scratch = [
        square, pair, pair, low_pair, low_pair, pltpu.VMEM((seqs, 3 * width + 16, seq), bf),
    ]
    w_t = pltpu.VMEM((3 * width + 16, feats), bf)
    base_t = pltpu.VMEM((seqs, seq, feats), f32)

    def back_own(sources, front, dctx, base, *deps):
        wt, wl, sm, pos = sources
        qkv_t, _, lse, gate = front
        return pl.pallas_call(
            functools.partial(back_own_kernel, heads, hd),
            in_specs=[hbm] * 7 + [full] * 4 + [smem] + [full] * 2,
            out_specs=[hbm, hbm, full, hbm],
            scratch_shapes=[w_t, tables_t, lines_t, pltpu.VMEM((seqs, width, seq), bf), base_t]
            + back_scratch
            + [
                pltpu.VMEM((3 * width, feats), f32), pltpu.VMEM((seqs, seq, feats), bf), tables_t,
                pltpu.SemaphoreType.DMA((3 + 2 * heads + 5 * seqs,)),
            ],
            out_shape=[
                sds((rows, feats), f32), sds((3 * width, feats), f32), sds((8, feats), f32), sds((heads, seq, seq), f32),
            ],
            compiler_params=params(LIMIT),
            cost_estimate=pl.CostEstimate(flops=COST, bytes_accessed=1 << 20, transcendentals=0),
            name="attend_back",
        )(wt, wl, pos, qkv_t, dctx, base, tokens, gw, sm, segq, segk, after(order[:1], *deps), lse, gate)

    def back_rest(first, n, sources, front, dctx, base, *deps):
        wt, wl, sm, pos = sources
        qkv_t, _, lse, gate = front

        def off(by, *shape):
            return pl.BlockSpec((1,) + shape, lambda s: (s + by,) + (0,) * len(shape))

        return pl.pallas_call(
            functools.partial(back_rest_kernel, heads, hd, first),
            grid=(n,),
            in_specs=[
                off(first, 2 * width, feats), off(first, width, feats),
                pl.BlockSpec((heads, seq, seq), lambda s: (s + first, 0, 0)), off(first, seqs, 3 * width, seq),
                off(first + 1, seqs, width, seq), hbm, whole(gates, feats), off(first, 4, feats), whole(seqs, 1, seq),
                whole(seqs, seq, 1), smem, off(first, seqs, 8, seq), off(first, seqs, 8, seq),
            ],
            out_specs=hbm,
            scratch_shapes=[w_t, base_t] + back_scratch + [pltpu.SemaphoreType.DMA((2 * seqs,))],
            out_shape=sds((rows, feats), f32),
            compiler_params=params(LIMIT),
            cost_estimate=pl.CostEstimate(flops=n * COST, bytes_accessed=1 << 20, transcendentals=0),
            name="attend_back",
        )(wt, wl, pos, qkv_t, dctx, base, gw, sm, segq, segk, after(order[1:], *deps), lse, gate)

    def piece(w, parts=1):
        per = w.shape[0] // n_dp // parts
        w = w.reshape(parts, n_dp, per, w.shape[1])
        return lax.dynamic_index_in_dim(w, dp, 1, False).reshape(parts * per, -1)

    w1_rows = fc1_weight.T
    mine = jnp.stack([piece(w1_rows), piece(fc2_weight)])
    gathered = lax.all_gather(mine, ("mp", "dp"))

    small, cuts = lines_of(after(rel_table.T, mine), fc1_bias[None], qv_bias, gate_scale[None])
    w0 = jnp.concatenate([qkv_weight.transpose(0, 2, 1).reshape(3 * width, feats), out_weight], axis=0)
    piece0 = jnp.concatenate([piece(w0, 2), cuts], axis=0)
    w0 = w0.reshape(2, 2 * width, feats)
    z0 = [rotate(piece0, r, n_mp) for r in range(1, n_mp)]
    buckets_t = buckets.T
    pos_own = bias_of(after(buckets_t, piece0), small[None], heads, size)
    z0, pos_own = lax.optimization_barrier((z0, pos_own))
    z0 = jnp.stack(z0)

    mid = 2 * width // n_dp
    got = z0[:, 2 * mid :].astype(f32)
    smalls = (got[:, 0:4] + got[:, 4:8]) + got[:, 8:12]
    own_sources = (w0, w0[1:], small[None], pos_own)
    spreads = [z0[:, :mid], z0[:, mid : 2 * mid]]
    routes = [plane[::-1], plane]
    covers = [lambda *deps: bias_of(after(buckets_t, *deps), smalls, heads, size), lambda *deps: attend(1, own_sources, *deps)]
    done = []
    for step in range(len(plane)):
        gots = [swap(v, route[step], n_dp) for v, route in zip(spreads, routes)]
        if step < len(covers):
            result = covers[step](*spreads)
            gots, result = lax.optimization_barrier((gots, result))
            done.append(result)
        spreads = [joined(v, g, route[step], dp, route[:step]) for v, g, route in zip(spreads, gots, routes)]
    for step in range(len(plane), len(covers)):
        done.append(covers[step]())
    pos_rest, front = done
    gots = [swap(v, 1, n_dp) for v in spreads]
    top, low = (joined(v, g, 1, dp, plane).reshape(others, 2 * width, feats) for v, g in zip(spreads, gots))
    rest_sources = (top, low, smalls, pos_rest)
    fronts = attend(others, rest_sources)
    gathered, fronts = lax.optimization_barrier((gathered, fronts))
    gathered = gathered.reshape(n_mp, n_dp, 2, units // n_dp, feats)
    if units // n_dp % 16:
        gathered = gathered.transpose(0, 2, 1, 3, 4).reshape(n_mp, 1, 2, units, feats)

    vec = jnp.concatenate([out_bias, ln1_gain, ln1_bias, fc2_bias, ln2_gain, ln2_bias]).reshape(6, feats)
    tile = 256

    def row(n):
        return pl.BlockSpec((tile, n), lambda i: (i, 0))

    outs = pl.pallas_call(
        layer_kernel,
        grid=(rows // tile,),
        in_specs=[pl.BlockSpec((n, tile, width), lambda i: (0, i, 0)) for n in (1, others)]
        + [row(feats), row(feats)]
        + [hbm] * 3
        + [full] * 2
        + [hbm] * 2
        + [full, smem],
        out_specs=[
            row(feats), row(feats), pl.BlockSpec((n_mp, 1, width, tile), lambda i: (0, i * tile // seq, 0, i % (seq // tile))),
            row(feats), row(feats), row(feats), row(units), row(units), pl.BlockSpec((8, feats), lambda i: (0, 0)),
        ],
        scratch_shapes=[
            pltpu.VMEM((n_mp * width, feats), bf), pltpu.VMEM((n_mp * units, feats), bf), pltpu.VMEM((n_mp * units, feats), bf),
            pltpu.VMEM((tile, n_mp * units), bf), pltpu.VMEM((tile, n_mp * units), f32), pltpu.VMEM((tile, n_mp * units), bf),
            pltpu.SemaphoreType.DMA((n_mp + 2 + 2 * others,)),
        ],
        out_shape=[
            sds((rows, feats), f32), sds((rows, feats), f32), sds((n_mp, seqs, width, seq), bf), sds((rows, feats), bf),
            sds((rows, feats), bf), sds((rows, feats), bf), sds((rows, units), bf), sds((rows, units), bf), sds((8, feats), f32),
        ],
        compiler_params=params(LIMIT),
        cost_estimate=pl.CostEstimate(flops=4 * COST, bytes_accessed=1 << 24, transcendentals=0),
        name="layer",
    )(
        front[1], fronts[1], tokens, grad_out, out_weight, low, w1_rows, small, smalls, fc2_weight, gathered, vec,
        order,
    )
    normed, grad_first = outs[:2]
    dctx = outs[2]
    hid_low, mix_low, first_low, act_own, pre_own, sums = outs[3:]

    def outer(a, b):
        return lax.dot_general(a, b, (((0,), (0,)), ((), ())), preferred_element_type=f32)

    big = jnp.concatenate([outer(front[1][0], first_low), outer(hid_low, pre_own), outer(act_own, mix_low)], axis=0).astype(bf)
    back, dw, tiny, acc = back_own(own_sources, front, dctx, grad_first, big)
    keep = lax.dynamic_slice_in_dim(big, core * (big.shape[0] // 2), big.shape[0] // 2, 0)
    give = lax.dynamic_slice_in_dim(big, (1 - core) * (big.shape[0] // 2), big.shape[0] // 2, 0)
    big = (keep.astype(f32) + swap(give, 1, n_dp).astype(f32)).astype(bf)
    same = [[d for d in range(n_dp) if d % 2 == c] for c in range(2)]
    big = lax.psum_scatter(big, "dp", scatter_dimension=0, tiled=True, axis_index_groups=same)

    shared = tiny[:3]
    turned = [rotate(shared, r, n_mp) for r in range(1, n_mp)]
    table = table_grad(after(buckets_t, shared), acc, size)
    table, turned, big = lax.optimization_barrier((table, turned, big))
    route = plane[::-1]
    turned = [shared] + list(turned)
    while len(turned) > 1:
        turned = [a + b for a, b in zip(turned[: len(turned) // 2], turned[len(turned) // 2 :])]
    table = jnp.pad(table, ((0, 0), (0, feats - table.shape[1])))
    extra = jnp.concatenate([sums, turned[0], tiny[3:], table], axis=0)
    count = extra.shape[0] // 2

    def parted(flip):
        def pick(v):
            v = v.reshape(2, -1, feats)
            return jnp.where((core == 1) != flip, v[1], v[0])

        return jnp.concatenate([pick(dw), pick(extra)])

    total = parted(False) + swap(parted(True), 1, n_dp)
    cut = dw.shape[0] // 2
    done = 0
    for step, bit in enumerate(plane):
        if step + 1 < len(plane):
            low_part = lax.reduce_precision(total[cut:], 8, 7)
            sent = jnp.concatenate([total[:cut], low_part, total[cut:] - low_part])
            sent = lax.reduce_precision(sent, 8, 7).astype(bf)
            n = 1
        else:
            sent = total
            n = others - done
        got = swap(sent, bit, n_dp)
        big_got = swap(big, route[step], n_dp)
        if done < others:
            back = back_rest(done, n, rest_sources, fronts, dctx, back, sent, big)
            got, big_got, back = lax.optimization_barrier((got, big_got, back))
            done += n
        big = joined(big[None], big_got[None], route[step], dp, route[:step])[0]
        both = sent.astype(f32) + got.astype(f32)
        if step + 1 < len(plane):
            both = jnp.concatenate([both[:cut], both[cut : cut + count] + both[cut + count :]])
        total = both
    got = swap(total, 1, n_dp)
    big = big.reshape(-1, feats)
    big_got = swap(big, 1, n_dp)
    outs = finish(
        heads, hd, gates, size, width, units, jnp.reshape(core, (1,)), total, got, big, big_got
    )
    dw, grad_ow, grad_fc1, grad_fc2, grad_table, grad_gate_weight, dqv_bias, grad_gate_bias, grad_gate_scale = outs[:9]
    sums = outs[9:]
    dw = dw.reshape(3, width, feats).transpose(0, 2, 1)
    grad_table = grad_table.T
    grad_gate_weight = grad_gate_weight.T
    input_grad = back
    return (
        normed, input_grad, dw, dqv_bias, grad_table, grad_gate_weight, grad_gate_bias, grad_gate_scale, grad_ow, sums[5],
        sums[3], sums[4], grad_fc1, sums[6], grad_fc2, sums[2], sums[0], sums[1],
    )


def solution(mesh):
    in_specs = (
        P("dp", None), P("dp", None), P(), P(None, None, "mp"), P(None, "mp"), P(None, "mp"), P(), P(), P("mp"),
        P("mp", None), P(), P(), P(), P(None, "mp"), P("mp"), P("mp", None), P(), P(), P(), P("dp", None),
    )
    out_specs = (
        P("dp", None), P("dp", None), P(None, None, "mp"), P(None, "mp"), P(None, "mp"), P(), P(), P("mp"),
        P("mp", None), P(), P(), P(), P(None, "mp"), P("mp"), P("mp", None), P(), P(), P(),
    )
    fn = functools.partial(body, mesh.shape["dp"], mesh.shape["mp"])
    return jax.shard_map(fn, mesh=mesh, in_specs=in_specs, out_specs=out_specs, check_vma=False)
```

```python
import functools

import jax
import jax.numpy as jnp
from jax import lax
from jax.experimental import pallas as pl
from jax.experimental.pallas import tpu as pltpu
from jax.sharding import PartitionSpec as P

norm_eps = 1e-05
deep_alpha = 24.0**0.25
masked_score = -1e30
bf = jnp.bfloat16
f32 = jnp.float32
LANES = 128
LIMIT = 60
COST = 3_000_000_000


def nn(a, b):
    return lax.dot_general(a, b, (((1,), (0,)), ((), ())), preferred_element_type=f32)


def nt(a, b):
    return lax.dot_general(a, b, (((1,), (1,)), ((), ())), preferred_element_type=f32)


def params(mib):
    return pltpu.CompilerParams(vmem_limit_bytes=mib * 1024 * 1024)


def lines_kernel(at_ref, table_ref, b1_ref, qv_ref, scale_ref, *refs):
    if len(refs) == 2:
        out_ref, cut_ref = refs
    else:
        w1_hbm, w2_hbm, out_ref, cut_ref, mine_ref, sem = refs
        per = mine_ref.shape[1]
        spot = pl.ds(pl.multiple_of(at_ref[0] * per, per), per)
        copies = [
            pltpu.make_async_copy(w.at[spot], mine_ref.at[i], sem.at[i]) for i, w in enumerate((w1_hbm, w2_hbm))
        ]
        for c in copies:
            c.start()
    heads, size = table_ref.shape
    feats = out_ref.shape[1]
    width = qv_ref.shape[1]
    out_ref[...] = jnp.zeros_like(out_ref)
    per = -(-size // LANES) * LANES
    for h in range(heads):
        out_ref[pl.ds(h * per // feats, 1), pl.ds(h * per % feats, size)] = table_ref[pl.ds(h, 1), :]
    out_ref[pl.ds(2, 1), :] = b1_ref[...].reshape(1, feats)
    out_ref[pl.ds(3, 1), pl.ds(0, width)] = qv_ref[pl.ds(0, 1), :]
    out_ref[pl.ds(3, 1), pl.ds(256, width)] = qv_ref[pl.ds(1, 1), :]
    out_ref[pl.ds(3, 1), pl.ds(512, heads)] = scale_ref[...].reshape(1, heads)
    rest = out_ref[...]
    cuts = []
    for _ in range(3):
        cut = rest.astype(bf).astype(f32)
        cuts.append(cut)
        rest = rest - cut
    cut_ref[...] = jnp.concatenate(cuts + [jnp.zeros_like(rest)], axis=0).astype(bf)
    if len(refs) > 2:
        for c in copies:
            c.wait()


def lines_of(at, table, b1, qv, scale, w1, w2, n):
    feats = b1.shape[0]
    per = w1.shape[0] // n
    fits = per % 16 == 0
    sds = jax.ShapeDtypeStruct
    hbm = [pl.BlockSpec(memory_space=pl.ANY)]
    outs = pl.pallas_call(
        lines_kernel,
        in_specs=[pl.BlockSpec(memory_space=pltpu.SMEM)] + [pl.BlockSpec()] * 4 + hbm * 2 * fits,
        out_specs=[pl.BlockSpec()] * (2 + fits),
        out_shape=[sds((4, feats), f32), sds((16, feats), bf)] + [sds((2, per, w1.shape[1]), bf)] * fits,
        scratch_shapes=[pltpu.SemaphoreType.DMA((2,))] * fits,
        compiler_params=params(LIMIT),
        name="lines",
    )(jnp.reshape(at, (1,)), table, b1, qv, scale, *((w1, w2) if fits else ()))
    if fits:
        return outs
    return *outs, jnp.stack([lax.dynamic_slice_in_dim(w, at * per, per, 0) for w in (w1, w2)])


def bias_kernel(heads, chunks, buckets_ref, small_ref, out_ref):
    rows, cols = buckets_ref.shape
    groups, _, feats = small_ref.shape
    for r in range(0, rows, 8):
        at = pl.ds(r, 8)
        for c in range(cols // LANES):
            lanes = pl.ds(c * LANES, LANES)
            idx = buckets_ref[at, lanes]
            low = idx & (LANES - 1)
            high = idx >> 7
            for h in range(heads):
                got = None
                for k in range(chunks):
                    spot = ((h % 3) * chunks + k) * LANES
                    line = jnp.broadcast_to(
                        small_ref[h // 3, pl.ds(spot // feats, 1), pl.ds(spot % feats, LANES)], (8, LANES)
                    )
                    part = jnp.take_along_axis(line, low, axis=1, mode="promise_in_bounds")
                    got = part if got is None else jnp.where(high == k, part, got)
                out_ref[h, at, lanes] = got


def bias_of(buckets_t, small, heads, size):
    groups, _, feats = small.shape
    seq = buckets_t.shape[0]
    rows = 64
    cost = pl.CostEstimate(flops=COST, bytes_accessed=1 << 20, transcendentals=0)
    return pl.pallas_call(
        functools.partial(bias_kernel, heads * groups, -(-size // LANES)),
        grid=(seq // rows,),
        in_specs=[
            pl.BlockSpec((rows, seq), lambda i: (i, 0)),
            pl.BlockSpec((groups, 4, feats), lambda i: (0, 0, 0)),
        ],
        out_specs=pl.BlockSpec((heads * groups, rows, seq), lambda i: (0, i, 0)),
        out_shape=jax.ShapeDtypeStruct((heads * groups, seq, seq), f32),
        compiler_params=params(LIMIT),
        cost_estimate=cost,
        name="pos_bias",
    )(buckets_t, small)


def tiled(v, lanes):
    while v.shape[1] < LANES:
        v = jnp.concatenate([v, v], axis=1)
    return jnp.concatenate([v] * (lanes // v.shape[1]), axis=1)


def head_lanes(shape, head, hd):
    return lax.broadcasted_iota(jnp.int32, shape, 1) // hd == head


def fill_mask(mask, seg_ref, row):
    seq = mask.shape[0]
    line = seg_ref[pl.ds(row, 1), :].astype(f32)
    column = jnp.broadcast_to(line, (8, seq)).T[:, :1]
    for c in range(0, seq, LANES):
        mask[:, pl.ds(c, LANES)] = jnp.where(column == line[:, c : c + LANES], 0.0, masked_score)


def attend_kernel(
    heads, hd, first, x_ref, wt_ref, wl_ref, pos_ref, gw_ref, small_ref, seg_ref, gbias_ref, at_ref,
    qkv_ref, ctx_ref, lse_ref, gate_ref, mask, sc, pr, ctx_t,
):
    group = pl.program_id(0)
    width = heads * hd
    seqs, seq = seg_ref.shape
    gates = gw_ref.shape[0]
    feats = x_ref.shape[1]
    half = gates // 2
    cut = wt_ref.shape[1]
    strips = [pl.ds(c, 2 * LANES) for c in range(0, seq, 2 * LANES)]

    def line(row):
        return pl.ds(row * seq, seq)

    cols = jnp.broadcast_to(small_ref[0, pl.ds(3, 1), pl.ds(0, 512)], (8, 512)).T[:, :1]
    gw = tiled(gw_ref[...].astype(f32), feats)
    mine = [jnp.where(head_lanes(gw.shape, at_ref[first + group] * heads + h, hd), gw, 0.0) for h in range(heads)]
    mine = jnp.concatenate(mine, axis=0).astype(bf)
    bias_a = gbias_ref[0] + gbias_ref[1] + gbias_ref[2] + gbias_ref[3]
    bias_b = gbias_ref[4] + gbias_ref[5] + gbias_ref[6] + gbias_ref[7]
    lins = {}

    def project(row):
        x = x_ref[line(row), :]
        upper = nt(wt_ref[0], x)
        lower = nt(wl_ref[0], x)
        qkv_ref[0, row, pl.ds(0, width), :] = (upper[:width] + cols[:width]).astype(bf) * bf(hd**-0.5)
        qkv_ref[0, row, pl.ds(width, width), :] = upper[width:cut].astype(bf)
        qkv_ref[0, row, pl.ds(2 * width, width), :] = (lower + cols[256 : 256 + width]).astype(bf)
        lins[row] = nt(mine, x)
        fill_mask(mask.at[row], seg_ref, row)

    def score(i):
        row, h = divmod(i, heads)
        k_t = qkv_ref[0, row, pl.ds(width + h * hd, hd), :]
        sc[i % 2] = nn(k_t.T, qkv_ref[0, row, pl.ds(h * hd, hd), :])

    def weigh(i):
        row, h = divmod(i, heads)
        lin = lins[row]
        first = jax.nn.sigmoid(jnp.sum(lin[h * gates : h * gates + half], axis=0, keepdims=True) + bias_a)
        second = jax.nn.sigmoid(jnp.sum(lin[h * gates + half : (h + 1) * gates], axis=0, keepdims=True) + bias_b)
        gate = first * (second * small_ref[0, pl.ds(3, 1), pl.ds(512 + h, 1)] - 1.0) + 2.0
        gate_ref[0, row, pl.ds(h, 1), :] = first
        gate_ref[0, row, pl.ds(heads + h, 1), :] = second
        for at in strips:
            s = sc[i % 2, :, at] + pos_ref[h, :, at] * gate[:, at.start : at.start + at.size] + mask[row, :, at]
            top = jnp.max(s, axis=0, keepdims=True)
            p = jnp.exp(s - top)
            total = jnp.sum(p, axis=0, keepdims=True)
            pr[i % 2, :, at] = (p * (1.0 / total)).astype(bf)
            lse_ref[0, row, pl.ds(h, 1), at] = top + jnp.log(total)

    def gather(i):
        row, h = divmod(i, heads)
        v_t = qkv_ref[0, row, pl.ds(2 * width + h * hd, hd), :]
        ctx_t[pl.ds(h * hd, hd), :] = nn(v_t, pr[i % 2])
        if h == heads - 1:
            ctx_ref[0, line(row), :] = ctx_t[...].T.astype(bf)

    count = seqs * heads
    project(0)
    score(0)
    for i in range(count):
        if i + 1 < count:
            if (i + 1) % heads == 0:
                project((i + 1) // heads)
            score(i + 1)
        weigh(i)
        if i:
            gather(i - 1)
    gather(count - 1)


def back_group(
    heads, hd, own, x_of, w_v, pos_of, gw_ref, small, seg_ref, head0, qkv_of, lse_of, gate_of, dctx_of, add,
    table_v, finish, mask, sc, dp, pr, ds, wide, ready,
):
    width = heads * hd
    seqs, seq = seg_ref.shape
    feats = w_v.shape[1]
    strips = [pl.ds(c, 2 * LANES) for c in range(0, seq, 2 * LANES)]
    gw = tiled(gw_ref[...].astype(f32), feats)
    half = gw.shape[0] // 2
    sums = [jnp.sum(gw[:half], axis=0, keepdims=True), jnp.sum(gw[half:], axis=0, keepdims=True)]
    lanes_of = [head_lanes((1, feats), head0 + h, hd) for h in range(heads)]
    gsum = [jnp.where(lanes_of[h], part, 0.0) for part in sums for h in range(heads)]
    w_v[pl.ds(3 * width, 16), :] = jnp.concatenate(gsum + [jnp.zeros((16 - 2 * heads, feats), f32)], axis=0).astype(bf)
    gate_parts = {}

    def score(i):
        row, h = divmod(i, heads)
        if h == 0:
            ready("row", row)
            fill_mask(mask.at[row], seg_ref, row)
        k_t = qkv_of(row, width + h * hd, hd)
        v_t = qkv_of(row, 2 * width + h * hd, hd)
        sc[i % 2] = nn(k_t.T, qkv_of(row, h * hd, hd))
        dp[i % 2] = nn(v_t.T, dctx_of(row, h * hd, hd))

    def weigh(i):
        row, h = divmod(i, heads)
        if row == 0:
            ready("pos", h)
        b = i % 2
        first = gate_of(row, h)
        second = gate_of(row, heads + h)
        scale = small[pl.ds(3, 1), pl.ds(512 + h, 1)]
        gate = first * (second * scale - 1.0) + 2.0
        lse = lse_of(row, h)
        sums_of = []
        for at in strips:
            here = slice(at.start, at.start + at.size)
            pos = pos_of(h, at)
            p = jnp.exp(sc[b, :, at] + (pos * gate[:, here] - lse[:, here]) + mask[row, :, at])
            pr[b, :, at] = p.astype(bf)
            g = dp[b, :, at]
            centre = jnp.sum(p * g, axis=0, keepdims=True)
            low = (p * (g - centre)).astype(bf)
            ds[b, :, at] = low
            d = low.astype(f32)
            sums_of.append(jnp.sum(d * pos, axis=0, keepdims=True))
            if own:
                tab = gate[:, here] * d
                if row == 0:
                    table_v[h, :, at] = tab
                else:
                    table_v[h, :, at] += tab
        if own and row == seqs - 1:
            finish("table", h)
        dgate = jnp.concatenate(sums_of, axis=1)
        dfirst = dgate * (second * scale - 1.0) * first * (1.0 - first)
        dsecond = dgate * first * scale * second * (1.0 - second)
        gate_parts[i] = (dfirst, dsecond, dgate * first * second)

    def gather(i):
        row, h = divmod(i, heads)
        b = i % 2
        q_t = qkv_of(row, h * hd, hd)
        k_t = qkv_of(row, width + h * hd, hd)
        g_t = dctx_of(row, h * hd, hd)
        for j, d in enumerate((nn(k_t, ds[b]) * hd**-0.5, nt(q_t, ds[b]), nt(g_t, pr[b]))):
            wide[row, pl.ds(j * width + h * hd, hd), :] = d.astype(bf)
        if h < heads - 1:
            return
        lines = [gate_parts[row * heads + j][k] for k in (0, 1) for j in range(heads)]
        low = jnp.concatenate(lines + [jnp.zeros((16 - 2 * heads, seq), f32)], axis=0).astype(bf)
        wide[row, pl.ds(3 * width, 16), :] = low
        if row == 0:
            ready("w", 0)
        add(row, nn(wide[row].T, w_v[...]))
        if not own:
            return
        ready("x", row)
        x = x_of(row)
        main = wide[row, pl.ds(0, 3 * width), :]
        dw_here = nn(main, x)
        rest = jnp.concatenate(lines, axis=0) - low[: 2 * heads].astype(f32)
        dgw = nn(low, x)[: 2 * heads] + nn(jnp.concatenate([rest.astype(bf)] * 3, axis=0)[:16], x)[: 2 * heads]
        one = sum(jnp.where(lanes_of[j], dgw[j : j + 1], 0.0) for j in range(heads))
        two = sum(jnp.where(lanes_of[j], dgw[heads + j : heads + j + 1], 0.0) for j in range(heads))
        qv = nt(jnp.ones((8, seq), bf), main)[:1]
        lane = lax.broadcasted_iota(jnp.int32, (1, feats), 1)

        def spot_of(k, v):
            return jnp.where(lane == k, jnp.sum(v, axis=1, keepdims=True), 0.0)

        biases = spot_of(0, sum(lines[:heads])) + spot_of(1, sum(lines[heads:]))
        gains = sum(spot_of(j, gate_parts[row * heads + j][2]) for j in range(heads))
        none = jnp.zeros((1, feats), f32)
        qv = jnp.concatenate([qv, none[:, : feats - qv.shape[1]]], axis=1)
        finish("row", row, dw_here, jnp.concatenate([one, two, biases, none, qv, gains, none, none], axis=0))

    count = seqs * heads
    score(0)
    for i in range(count):
        if i + 1 < count:
            score(i + 1)
        weigh(i)
        if i:
            gather(i - 1)
    gather(count - 1)


def back_own_kernel(
    heads, hd, wt_hbm, wl_hbm, pos_hbm, qkv_hbm, dctx_hbm, base_hbm, x_hbm,
    gw_ref, small_ref, seg_ref, at_ref, lse_ref, gate_ref,
    grad_hbm, dw_hbm, tiny_ref, table_hbm,
    w_v, pos_v, qkv_v, dctx_v, base_v, mask, sc, dp, pr, ds, wide, dw_v, x_v, table_v, sem,
):
    width = heads * hd
    seqs, seq = seg_ref.shape
    cut = wt_hbm.shape[1]
    count = iter(range(64))

    def line(row):
        return pl.ds(row * seq, seq)

    def copy(src, dst):
        return pltpu.make_async_copy(src, dst, sem.at[next(count)])

    w_in = [
        copy(wt_hbm.at[0], w_v.at[pl.ds(0, cut)]),
        copy(wl_hbm.at[1, pl.ds(0, 3 * width - cut)], w_v.at[pl.ds(cut, 3 * width - cut)]),
    ]
    pos_in = [copy(pos_hbm.at[h], pos_v.at[h]) for h in range(heads)]
    row_in = [[copy(qkv_hbm.at[0, r], qkv_v.at[r]), copy(dctx_hbm.at[0, r], dctx_v.at[r])] for r in range(seqs)]
    base_in = [copy(base_hbm.at[line(r)], base_v.at[r]) for r in range(seqs)]
    grad_out = [copy(base_v.at[r], grad_hbm.at[line(r)]) for r in range(seqs)]
    x_in = [copy(x_hbm.at[line(r)], x_v.at[r]) for r in range(seqs)]
    table_out = [copy(table_v.at[h], table_hbm.at[h]) for h in range(heads)]
    dw_out = copy(dw_v, dw_hbm)
    for c in row_in[0] + [pos_in[0]] + [c for r in row_in[1:] for c in r] + pos_in[1:] + w_in + base_in + x_in:
        c.start()

    def ready(what, i):
        for c in {"row": lambda: row_in[i], "pos": lambda: [pos_in[i]], "w": lambda: w_in, "x": lambda: [x_in[i]]}[what]():
            c.wait()

    def add(row, part):
        base_in[row].wait()
        base_v[row] = deep_alpha * base_v[row] + part
        grad_out[row].start()

    def finish(what, i, *values):
        if what == "table":
            table_out[i].start()
        elif i == 0:
            dw_v[...], tiny_ref[...] = values
        else:
            dw_v[...] += values[0]
            tiny_ref[...] += values[1]
            if i == seqs - 1:
                dw_out.start()

    back_group(
        heads, hd, True, lambda r: x_v[r], w_v, lambda h, at: pos_v[h, :, at], gw_ref, small_ref.at[0], seg_ref,
        at_ref[0] * heads, lambda r, i, n: qkv_v[r, pl.ds(i, n), :], lambda r, h: lse_ref[0, r, pl.ds(h, 1), :],
        lambda r, h: gate_ref[0, r, pl.ds(h, 1), :], lambda r, i, n: dctx_v[r, pl.ds(i, n), :], add, table_v, finish,
        mask, sc, dp, pr, ds, wide, ready,
    )
    for c in grad_out + table_out + [dw_out]:
        c.wait()


def back_rest_kernel(
    heads, hd, first, wt_ref, wl_ref, pos_ref, qkv_ref, dctx_ref, base_hbm,
    gw_ref, small_ref, seg_ref, at_ref, lse_ref, gate_ref,
    grad_hbm,
    w_v, base_v, mask, sc, dp, pr, ds, wide, sem,
):
    step = pl.program_id(0)
    last = pl.num_programs(0) - 1
    width = heads * hd
    seqs, seq = seg_ref.shape
    cut = wt_ref.shape[1]

    def line(row):
        return pl.ds(row * seq, seq)

    base_in = [pltpu.make_async_copy(base_hbm.at[line(r)], base_v.at[r], sem.at[r]) for r in range(seqs)]
    grad_out = [pltpu.make_async_copy(base_v.at[r], grad_hbm.at[line(r)], sem.at[seqs + r]) for r in range(seqs)]

    @pl.when(step == 0)
    def _():
        for c in base_in:
            c.start()

    w_v[pl.ds(0, cut), :] = wt_ref[0]
    w_v[pl.ds(cut, 3 * width - cut), :] = wl_ref[0]

    def add(row, part):
        @pl.when(step == 0)
        def _():
            base_in[row].wait()

        base_v[row] += part

        @pl.when(step == last)
        def _():
            grad_out[row].start()

    back_group(
        heads, hd, False, None, w_v, lambda h, at: pos_ref[h, :, at], gw_ref, small_ref.at[0], seg_ref,
        at_ref[1 + first + step] * heads, lambda r, i, n: qkv_ref[0, r, pl.ds(i, n), :], lambda r, h: lse_ref[0, r, pl.ds(h, 1), :],
        lambda r, h: gate_ref[0, r, pl.ds(h, 1), :], lambda r, i, n: dctx_ref[0, r, pl.ds(i, n), :], add, None, None,
        mask, sc, dp, pr, ds, wide, lambda what, i: None,
    )

    @pl.when(step == last)
    def _():
        for c in grad_out:
            c.wait()


def norm_stats(v):
    mean = jnp.mean(v, axis=-1, keepdims=True)
    cen = v - mean
    rs = lax.rsqrt(jnp.mean(cen * cen, axis=-1, keepdims=True) + norm_eps)
    return cen * rs, rs


def norm_back(g, n, rs, gain):
    gn = g * gain
    return rs * (gn - jnp.mean(gn, axis=-1, keepdims=True) - n * jnp.mean(gn * n, axis=-1, keepdims=True))


def gelu_pair(x):
    cdf = 0.5 + 0.5 * lax.erf(x * 0.5**0.5)
    return x * cdf, cdf + x * jnp.exp(x * x * -0.5) * 0.3989422804014327


def weave(*runs):
    runs = list(runs)
    while runs:
        runs = [r for r in runs if next(r, runs) is not runs]


def layer_kernel(
    ctx0_ref, ctx_ref, x_ref, go_ref, ow0_hbm, ow_hbm, w10_hbm, small_ref, smalls_ref,
    w20_hbm, all_hbm, out_bias_ref, gain1_ref, bias1_ref, bias2_ref, gain2_ref, beta2_ref, at_ref,
    out_ref, first_ref, dctx_ref, hid_low_ref, mix_low_ref, first_low_ref, act_ref, pre_low_ref, sums_ref,
    ow_v, w1_v, w2_v, act, slope, plow, wide, scale, acc, own_acc, sem,
):
    step = pl.program_id(0)
    ctxs = [ctx0_ref.at[0]] + [ctx_ref.at[i] for i in range(ctx_ref.shape[0])]
    width = ow0_hbm.shape[0]
    own = w20_hbm.shape[0]
    count = iter(range(128))
    _, pieces, _, per, feats = all_hbm.shape
    chains, rows = act.shape[:2]
    part = 64

    def copy(src, dst):
        return pltpu.make_async_copy(src, dst, sem.at[next(count)])

    ow_in = [copy(ow0_hbm, ow_v.at[pl.ds(0, width)])]
    for i in range(1, len(ctxs)):
        ow_in.append(copy(ow_hbm.at[i - 1, pl.ds(ow_hbm.shape[1] - width, width)], ow_v.at[pl.ds(i * width, width)]))
    w_in = []
    for k, (mine, all_v) in enumerate(((w10_hbm, w1_v), (w20_hbm, w2_v))):
        w_in.append([copy(mine, all_v.at[pl.ds(0, own)])])
        parted = all_v.reshape(len(ctxs) * pieces, per, feats)
        for i in range(1, len(ctxs)):
            w_in[k].append(copy(all_hbm.at[at_ref[i], :, k], parted.at[pl.ds(i * pieces, pieces)]))

    @pl.when(step == 0)
    def _():
        for c in ow_in + w_in[0] + w_in[1]:
            c.start()
        for c in ow_in:
            c.wait()
        acc[...] = jnp.zeros_like(acc)
        own_acc[...] = jnp.zeros_like(own_acc)

    vectors = (out_bias_ref, gain1_ref, bias1_ref, bias2_ref, gain2_ref, beta2_ref)
    out_bias, gain1, bias1, bias2, gain2, beta2 = (ref[...].reshape(1, feats) for ref in vectors)
    b1 = [small_ref[pl.ds(2, 1), :]] + [smalls_ref[i, pl.ds(2, 1), :] for i in range(len(ctxs) - 1)]
    b1 = jnp.concatenate(b1, axis=1)
    block = 256
    blocks = [pl.ds(u, block) for u in range(0, w2_v.shape[0], block)]
    cols = [pl.ds(u, block) for u in range(0, feats, block)]

    def lines(c):
        for r in range(0, rows, part):
            yield pl.ds(r, part), pl.ds(c * rows + r, part)

    def tally(i, v):
        acc[i] += jnp.sum(v.reshape(part // 8, 8, feats), axis=0)

    def enter(c):
        total = nn(ctxs[0][pl.ds(c * rows, rows), :], ow_v[pl.ds(0, width), :])
        for i in range(1, len(ctxs)):
            total = total + nn(ctxs[i][pl.ds(c * rows, rows), :], ow_v[pl.ds(i * width, width), :])
        wide[c, 2] = total
        yield
        for r, at in lines(c):
            n, rs = norm_stats(deep_alpha * x_ref[at, :].astype(f32) + out_bias + wide[c, 2, r, :])
            hidden = n * gain1 + bias1
            wide[c, 0, r, :] = n
            wide[c, 1, r, :] = hidden
            scale[c, r, :] = jnp.broadcast_to(rs, (part, LANES))
            hid_low_ref[at, :] = hidden.astype(bf)
            yield

    def up(c):
        at_rows = pl.ds(c * rows, rows)
        for at in blocks:
            group, inner = divmod(at.start, own)
            pre = nn(hid_low_ref[at_rows, :], w1_v[pl.ds(group * feats, feats), pl.ds(inner, block)])
            pre = pre + b1[:, at.start : at.start + block]
            a, s = gelu_pair(pre)
            act[c, :, at] = a.astype(bf)
            slope[c, :, at] = s
            yield
        act_ref[at_rows, :] = act[c, :, pl.ds(0, own)]

    def down(c):
        for at in cols:
            wide[c, 2, :, at] = nn(act[c], w2_v[:, at])
            yield

    def turn(c):
        for r, at in lines(c):
            n, rs = norm_stats(deep_alpha * wide[c, 1, r, :] + bias2 + wide[c, 2, r, :])
            out_ref[at, :] = n * gain2 + beta2
            g = go_ref[at, :].astype(f32)
            grad = norm_back(g, n, rs, gain2)
            wide[c, 1, r, :] = grad
            mix_low_ref[at, :] = grad.astype(bf)
            tally(0, g * n)
            tally(1, g)
            tally(2, grad)
            yield

    def back_down(c):
        at_rows = pl.ds(c * rows, rows)
        for at in blocks:
            d = nt(mix_low_ref[at_rows, :], w2_v[at, :]) * slope[c, :, at]
            if at.start < own:
                own_acc[:, at] += jnp.sum(d.reshape(rows // 8, 8, block), axis=0)
            plow[c, :, at] = d.astype(bf)
            yield
        pre_low_ref[at_rows, :] = plow[c, :, pl.ds(0, own)]

    def back_up(c):
        for at in cols:
            total = nt(plow[c, :, pl.ds(0, own)], w1_v[at, :])
            for i in range(1, len(ctxs)):
                total = total + nt(plow[c, :, pl.ds(i * own, own)], w1_v[pl.ds(i * feats + at.start, block), :])
            wide[c, 2, :, at] = total
            yield

    def leave(c):
        at_rows = pl.ds(c * rows, rows)
        for r, at in lines(c):
            n = wide[c, 0, r, :]
            grad = deep_alpha * wide[c, 1, r, :] + wide[c, 2, r, :]
            first = norm_back(grad, n, scale[c, r, :1], gain1)
            first_ref[at, :] = first
            first_low_ref[at, :] = first.astype(bf)
            tally(3, grad * n)
            tally(4, grad)
            tally(5, first)
            yield
        dctx = nt(ow_v[...], first_low_ref[at_rows, :]).astype(bf)
        for i in range(len(ctxs)):
            dctx_ref[i, 0, :, at_rows] = dctx[i * width : (i + 1) * width]
        yield

    def wait(which):
        @pl.when(step == 0)
        def _():
            for c in w_in[which]:
                c.wait()

    stages = (enter, up, down, turn, back_down, back_up, leave)
    for t in range(len(stages) + chains - 1):
        if t == 1:
            wait(0)
        if t == 2:
            wait(1)
        weave(*[stages[t - c](c) for c in range(chains) if 0 <= t - c < len(stages)])

    @pl.when(step == pl.num_programs(0) - 1)
    def _():
        rows_of = [jnp.sum(acc[i], axis=0, keepdims=True) for i in range(6)]
        rows_of.append(jnp.sum(own_acc[...], axis=0, keepdims=True))
        sums_ref[...] = jnp.concatenate(rows_of + [jnp.zeros_like(rows_of[0])], axis=0)


def table_kernel(heads, tops, lows, buckets_ref, val_ref, out_ref):
    rows, cols = buckets_ref.shape
    top_id = lax.broadcasted_iota(jnp.int32, (tops, cols), 0)
    low_id = lax.broadcasted_iota(jnp.int32, (lows, cols), 0)
    unroll = 64

    def group(g, acc):
        for u in range(0, unroll, 8):
            at = pl.ds(pl.multiple_of(g * unroll, unroll) + u, 8)
            idx = buckets_ref[at, :]
            high = idx >> 4
            low = idx & 15
            vals = [val_ref[h, at, :] for h in range(heads)]
            for i in range(8):
                a = jnp.where(high[i : i + 1] == top_id, 1.0, 0.0).astype(bf)
                hit = low[i : i + 1] == low_id
                b = jnp.concatenate([jnp.where(hit, v[i : i + 1], 0.0).astype(bf) for v in vals], axis=0)
                acc = acc + nt(a, b)
        return acc

    out_ref[...] = jnp.zeros_like(out_ref)
    out_ref[:, pl.ds(0, heads * lows)] = lax.fori_loop(
        0, rows // unroll, group, jnp.zeros((tops, heads * lows), f32)
    )


def table_grad(buckets_t, values, size, feats):
    heads, seq, _ = values.shape
    lows = 16
    tops = -(-size // lows // 8) * 8
    return pl.pallas_call(
        functools.partial(table_kernel, heads, tops, lows),
        out_shape=jax.ShapeDtypeStruct((tops, feats), f32),
        compiler_params=params(LIMIT),
        cost_estimate=pl.CostEstimate(flops=COST, bytes_accessed=1 << 20, transcendentals=0),
        name="table_grad",
    )(buckets_t, values)


def finish_kernel(
    heads, hd, size, core_ref, total_ref, got_ref, big_ref, big_got_ref,
    dw_ref, ow_ref, fc1_ref, fc2_ref, table_ref, gate_ref, qv_ref, gate_bias_ref, scale_ref, *sum_refs,
):
    later = core_ref[0] == 1
    total, got = total_ref[...], got_ref[...]
    first = jnp.where(later, got, total)
    second = jnp.where(later, total, got)
    cut = dw_ref.shape[0] // 2
    dw_ref[pl.ds(0, cut), :] = first[:cut]
    dw_ref[pl.ds(cut, cut), :] = second[:cut]
    extra = jnp.concatenate([first[cut:], second[cut:]], axis=0)
    feats = extra.shape[1]
    half = big_ref.shape[0]
    width, units = ow_ref.shape[0], fc2_ref.shape[0]
    inner = half - width
    for mine in (False, True):
        part = jnp.where(later == mine, big_ref[...], big_got_ref[...]).astype(f32)
        if not mine:
            ow_ref[...] = part[:width]
            fc1_ref[pl.ds(0, inner), :] = part[width:]
        else:
            fc1_ref[pl.ds(inner, feats - inner), :] = part[: feats - inner]
            fc2_ref[...] = part[feats - inner :]
    for i, ref in enumerate(sum_refs):
        ref[...] = extra[i]
    halves = sum(extra[8:10, c : c + LANES] for c in range(0, feats, LANES))
    halves = sum(halves[:, c : c + hd] for c in range(0, LANES, hd))
    gates = gate_ref.shape[0]
    gate_ref[...] = jnp.concatenate([halves[i : i + 1] for i in range(2) for _ in range(gates // 2)], axis=0)
    qv_ref[pl.ds(0, 1), :] = extra[12:13, :width]
    qv_ref[pl.ds(1, 1), :] = extra[12:13, 2 * width : 3 * width]
    lane = lax.broadcasted_iota(jnp.int32, (1, LANES), 1)
    pair = jnp.where(lane < gates // 2, extra[10:11, 0:1], extra[10:11, 1:2])
    gate_bias_ref[...] = pair[:, :gates]
    scale_ref[...] = extra[13:14, :heads]
    lows = 16
    tops = extra.shape[0] - 16
    wide = tops * lows
    spread = lax.broadcasted_iota(jnp.int32, (lows, wide), 1) % lows == lax.broadcasted_iota(jnp.int32, (lows, wide), 0)
    spread = jnp.where(spread, 1.0, 0.0).astype(bf)
    keep = lax.broadcasted_iota(jnp.int32, (tops, wide), 1) // lows == lax.broadcasted_iota(jnp.int32, (tops, wide), 0)
    for h in range(heads):
        rest = extra[16:, h * lows : (h + 1) * lows]
        line = jnp.zeros((tops, wide), f32)
        for _ in range(3):
            part = rest.astype(bf)
            line = line + nn(part, spread)
            rest = rest - part.astype(f32)
        line = jnp.sum(jnp.where(keep, line, 0.0), axis=0, keepdims=True)
        table_ref[pl.ds(h, 1), :] = line[:, :size]


def finish(heads, hd, gates, size, width, units, core, total, got, big, big_got):
    feats = total.shape[1]
    sds = jax.ShapeDtypeStruct
    vector = sds((feats,), f32)
    outs = pl.pallas_call(
        functools.partial(finish_kernel, heads, hd, size),
        in_specs=[pl.BlockSpec(memory_space=pltpu.SMEM)] + [pl.BlockSpec()] * 4,
        out_shape=[
            sds((3 * width, feats), f32), sds((width, feats), f32), sds((feats, units), f32), sds((units, feats), f32),
            sds((heads, size), f32), sds((gates, hd), f32), sds((2, width), f32), sds((1, gates), f32), sds((1, heads), f32),
        ]
        + [vector] * 7,
        compiler_params=params(LIMIT),
        name="finish",
    )(core, total, got, big, big_got)
    outs = list(outs)
    outs[7], outs[8] = outs[7][0], outs[8][0]
    return outs


def rotate(x, by, n):
    return lax.ppermute(x, "mp", [(i, (i + by) % n) for i in range(n)])


def swap(x, bit, n, axis="dp"):
    return lax.ppermute(x, axis, [(i, i ^ bit) for i in range(n)])


def after(x, *earlier):
    return lax.optimization_barrier((x,) + earlier)[0]


def joined(pieces, got, bit, index, have):
    at = 1 + sum(b > bit for b in have)
    mine = (index & bit) != 0
    return jnp.stack([jnp.where(mine, got, pieces), jnp.where(mine, pieces, got)], axis=at)


def body(
    n_dp, n_mp,
    tokens, segment_ids, buckets, qkv_weight, qv_bias, rel_table, gate_weight, gate_bias, gate_scale, out_weight,
    out_bias, ln1_gain, ln1_bias, fc1_weight, fc1_bias, fc2_weight, fc2_bias, ln2_gain, ln2_bias, grad_out,
):
    rows, feats = tokens.shape
    seqs, seq = segment_ids.shape
    size, heads = rel_table.shape
    hd, gates = gate_weight.shape
    width = heads * hd
    units = fc1_weight.shape[1]
    me = lax.axis_index("mp")
    dp = lax.axis_index("dp")
    order = ((me - jnp.arange(n_mp)) % n_mp).astype(jnp.int32)
    bits = [1 << i for i in range(n_dp.bit_length() - 1)]
    plane = bits[1:]
    others = n_mp - 1
    core = dp & 1
    sds = jax.ShapeDtypeStruct

    hbm = pl.BlockSpec(memory_space=pl.ANY)
    smem = pl.BlockSpec(memory_space=pltpu.SMEM)
    full = pl.BlockSpec()
    square = pltpu.VMEM((seqs, seq, seq), f32)
    pair = pltpu.VMEM((2, seq, seq), f32)
    low_pair = pltpu.VMEM((2, seq, seq), bf)
    gw = gate_weight.T
    lines_t = pltpu.VMEM((seqs, 3 * width, seq), bf)
    outs_t = pltpu.VMEM((seqs, width, seq), f32)
    tables_t = pltpu.VMEM((heads, seq, seq), f32)

    def one(*shape):
        return pl.BlockSpec((1,) + shape, lambda s: (s,) + (0,) * len(shape))

    def whole(*shape):
        return pl.BlockSpec(shape, lambda s: (0,) * len(shape))

    def attend(n, sources, *deps):
        wt, wl, sm, pos = sources
        return pl.pallas_call(
            functools.partial(attend_kernel, heads, hd, 0 if n == 1 else 1),
            grid=(n,),
            in_specs=[
                whole(rows, feats), one(2 * width, feats),
                pl.BlockSpec((1, width, feats), lambda s: (s + (n == 1), 0, 0)),
                pl.BlockSpec((heads, seq, seq), lambda s: (s, 0, 0)), whole(gates, hd), one(4, feats),
                whole(seqs, seq), smem, smem,
            ],
            out_specs=[one(seqs, 3 * width, seq), one(rows, width), one(seqs, 8, seq), one(seqs, 8, seq)],
            scratch_shapes=[square, pair, low_pair, pltpu.VMEM((width, seq), f32)],
            out_shape=[
                sds((n, seqs, 3 * width, seq), bf), sds((n, rows, width), bf), sds((n, seqs, 8, seq), f32),
                sds((n, seqs, 8, seq), f32),
            ],
            compiler_params=params(LIMIT),
            cost_estimate=pl.CostEstimate(flops=n * COST, bytes_accessed=1 << 20, transcendentals=0),
            name="attend",
        )(tokens, wt, wl, pos, gw, sm, segment_ids, gate_bias, after(order, *deps))

    back_scratch = [
        square, pair, pair, low_pair, low_pair, pltpu.VMEM((seqs, 3 * width + 16, seq), bf),
    ]
    w_t = pltpu.VMEM((3 * width + 16, feats), bf)
    base_t = pltpu.VMEM((seqs, seq, feats), f32)

    def back_own(sources, front, dctx, base, *deps):
        wt, wl, sm, pos = sources
        qkv_t, _, lse, gate = front
        return pl.pallas_call(
            functools.partial(back_own_kernel, heads, hd),
            in_specs=[hbm] * 7 + [full] * 3 + [smem] + [full] * 2,
            out_specs=[hbm, hbm, full, hbm],
            scratch_shapes=[w_t, tables_t, lines_t, pltpu.VMEM((seqs, width, seq), bf), base_t]
            + back_scratch
            + [
                pltpu.VMEM((3 * width, feats), f32), pltpu.VMEM((seqs, seq, feats), bf), tables_t,
                pltpu.SemaphoreType.DMA((3 + 2 * heads + 5 * seqs,)),
            ],
            out_shape=[
                sds((rows, feats), f32), sds((3 * width, feats), f32), sds((8, feats), f32), sds((heads, seq, seq), f32),
            ],
            compiler_params=params(LIMIT),
            cost_estimate=pl.CostEstimate(flops=COST, bytes_accessed=1 << 20, transcendentals=0),
            name="attend_back",
        )(wt, wl, pos, qkv_t, dctx, base, tokens, gw, sm, segment_ids, after(order, *deps), lse, gate)

    def back_rest(first, n, sources, front, dctx, base, *deps):
        wt, wl, sm, pos = sources
        qkv_t, _, lse, gate = front

        def off(by, *shape):
            return pl.BlockSpec((1,) + shape, lambda s: (s + by,) + (0,) * len(shape))

        return pl.pallas_call(
            functools.partial(back_rest_kernel, heads, hd, first),
            grid=(n,),
            in_specs=[
                off(first, 2 * width, feats), off(first, width, feats),
                pl.BlockSpec((heads, seq, seq), lambda s: (s + first, 0, 0)), off(first, seqs, 3 * width, seq),
                off(first + 1, seqs, width, seq), hbm, whole(gates, hd), off(first, 4, feats), whole(seqs, seq),
                smem, off(first, seqs, 8, seq), off(first, seqs, 8, seq),
            ],
            out_specs=hbm,
            scratch_shapes=[w_t, base_t] + back_scratch + [pltpu.SemaphoreType.DMA((2 * seqs,))],
            out_shape=sds((rows, feats), f32),
            compiler_params=params(LIMIT),
            cost_estimate=pl.CostEstimate(flops=n * COST, bytes_accessed=1 << 20, transcendentals=0),
            name="attend_back",
        )(wt, wl, pos, qkv_t, dctx, base, gw, sm, segment_ids, after(order, *deps), lse, gate)

    def piece(w, parts=1):
        per = w.shape[0] // n_dp // parts
        w = w.reshape(parts, n_dp, per, w.shape[1])
        return lax.dynamic_index_in_dim(w, dp, 1, False).reshape(parts * per, -1)

    small, cuts, mine = lines_of(dp, rel_table.T, fc1_bias, qv_bias, gate_scale, fc1_weight, fc2_weight, n_dp)
    gathered = lax.all_gather(mine, ("mp", "dp"))
    w0 = jnp.concatenate([qkv_weight.transpose(0, 2, 1).reshape(3 * width, feats), out_weight], axis=0)
    piece0 = jnp.concatenate([piece(w0, 2), cuts], axis=0)
    w0 = w0.reshape(2, 2 * width, feats)
    z0 = [rotate(piece0, r, n_mp) for r in range(1, n_mp)]
    buckets_t = buckets.T
    pos_own = bias_of(after(buckets_t, piece0), small[None], heads, size)
    z0, pos_own = lax.optimization_barrier((z0, pos_own))
    z0 = jnp.stack(z0)

    mid = 2 * width // n_dp
    got = z0[:, 2 * mid :].astype(f32)
    smalls = (got[:, 0:4] + got[:, 4:8]) + got[:, 8:12]
    own_sources = (w0, w0, small[None], pos_own)
    spreads = [z0[:, :mid], z0[:, mid : 2 * mid]]
    routes = [plane[::-1], plane]
    covers = [lambda *deps: bias_of(after(buckets_t, *deps), smalls, heads, size), lambda *deps: attend(1, own_sources, *deps)]
    done = []
    for step in range(len(plane)):
        gots = [swap(v, route[step], n_dp) for v, route in zip(spreads, routes)]
        if step < len(covers):
            result = covers[step](*spreads)
            gots, result = lax.optimization_barrier((gots, result))
            done.append(result)
        spreads = [joined(v, g, route[step], dp, route[:step]) for v, g, route in zip(spreads, gots, routes)]
    for step in range(len(plane), len(covers)):
        done.append(covers[step]())
    pos_rest, front = done
    gots = [swap(v, 1, n_dp) for v in spreads]
    top, low = (joined(v, g, 1, dp, plane).reshape(others, 2 * width, feats) for v, g in zip(spreads, gots))
    rest_sources = (top, low, smalls, pos_rest)
    fronts = attend(others, rest_sources)
    gathered, fronts = lax.optimization_barrier((gathered, fronts))
    gathered = gathered.reshape(n_mp, n_dp, 2, units // n_dp, feats)
    if units // n_dp % 16:
        gathered = gathered.transpose(0, 2, 1, 3, 4).reshape(n_mp, 1, 2, units, feats)

    tile = 512
    chains = 2

    def row(n):
        return pl.BlockSpec((tile, n), lambda i: (i, 0))

    outs = pl.pallas_call(
        layer_kernel,
        grid=(rows // tile,),
        in_specs=[pl.BlockSpec((n, tile, width), lambda i: (0, i, 0)) for n in (1, others)]
        + [row(feats), row(feats)]
        + [hbm] * 3
        + [full] * 2
        + [hbm] * 2
        + [full] * 6
        + [smem],
        out_specs=[
            row(feats), row(feats), pl.BlockSpec((n_mp, 1, width, tile), lambda i: (0, i * tile // seq, 0, i % (seq // tile))),
            row(feats), row(feats), row(feats), row(units), row(units), pl.BlockSpec((8, feats), lambda i: (0, 0)),
        ],
        scratch_shapes=[
            pltpu.VMEM((n_mp * width, feats), bf), pltpu.VMEM((n_mp * feats, units), bf), pltpu.VMEM((n_mp * units, feats), bf),
            pltpu.VMEM((chains, tile // chains, n_mp * units), bf), pltpu.VMEM((chains, tile // chains, n_mp * units), f32),
            pltpu.VMEM((chains, tile // chains, n_mp * units), bf), pltpu.VMEM((chains, 3, tile // chains, feats), f32),
            pltpu.VMEM((chains, tile // chains, LANES), f32), pltpu.VMEM((6, 8, feats), f32), pltpu.VMEM((8, units), f32),
            pltpu.SemaphoreType.DMA((n_mp + 2 + 2 * others,)),
        ],
        out_shape=[
            sds((rows, feats), f32), sds((rows, feats), f32), sds((n_mp, seqs, width, seq), bf), sds((rows, feats), bf),
            sds((rows, feats), bf), sds((rows, feats), bf), sds((rows, units), bf), sds((rows, units), bf), sds((8, feats), f32),
        ],
        compiler_params=params(LIMIT),
        cost_estimate=pl.CostEstimate(flops=4 * COST, bytes_accessed=1 << 24, transcendentals=0),
        name="layer",
    )(
        front[1], fronts[1], tokens, grad_out, out_weight, low, fc1_weight, small, smalls, fc2_weight, gathered, out_bias, ln1_gain, ln1_bias, fc2_bias, ln2_gain, ln2_bias,
        order,
    )
    normed, grad_first = outs[:2]
    dctx = outs[2]
    hid_low, mix_low, first_low, act_own, pre_own, sums = outs[3:]

    def outer(a, b):
        return lax.dot_general(a, b, (((0,), (0,)), ((), ())), preferred_element_type=f32)

    big = jnp.concatenate([outer(front[1][0], first_low), outer(hid_low, pre_own), outer(act_own, mix_low)], axis=0).astype(bf)
    back, dw, tiny, acc = back_own(own_sources, front, dctx, grad_first, big)
    keep = lax.dynamic_slice_in_dim(big, core * (big.shape[0] // 2), big.shape[0] // 2, 0)
    give = lax.dynamic_slice_in_dim(big, (1 - core) * (big.shape[0] // 2), big.shape[0] // 2, 0)
    big = (keep.astype(f32) + swap(give, 1, n_dp).astype(f32)).astype(bf)
    same = [[d for d in range(n_dp) if d % 2 == c] for c in range(2)]
    big = lax.psum_scatter(big, "dp", scatter_dimension=0, tiled=True, axis_index_groups=same)

    shared = tiny
    turned = [rotate(shared, r, n_mp) for r in range(1, n_mp)]
    table = table_grad(after(buckets_t, shared), acc, size, feats)
    table, turned, big = lax.optimization_barrier((table, turned, big))
    route = plane[::-1]
    turned = [shared] + list(turned)
    while len(turned) > 1:
        turned = [a + b for a, b in zip(turned[: len(turned) // 2], turned[len(turned) // 2 :])]
    extra = jnp.concatenate([sums, turned[0][:3], tiny[3:], table], axis=0)
    count = extra.shape[0] // 2

    def parted(flip):
        def pick(v):
            v = v.reshape(2, -1, feats)
            return jnp.where((core == 1) != flip, v[1], v[0])

        return jnp.concatenate([pick(dw), pick(extra)])

    total = parted(False) + swap(parted(True), 1, n_dp)
    cut = dw.shape[0] // 2
    done = 0
    for step, bit in enumerate(plane):
        if step + 1 < len(plane):
            low_part = lax.reduce_precision(total[cut:], 8, 7)
            sent = jnp.concatenate([total[:cut], low_part, total[cut:] - low_part])
            sent = lax.reduce_precision(sent, 8, 7).astype(bf)
            n = 1
        else:
            sent = total
            n = others - done
        got = swap(sent, bit, n_dp)
        big_got = swap(big, route[step], n_dp)
        if done < others:
            back = back_rest(done, n, rest_sources, fronts, dctx, back, sent, big)
            got, big_got, back = lax.optimization_barrier((got, big_got, back))
            done += n
        big = joined(big[None], big_got[None], route[step], dp, route[:step])[0]
        both = sent.astype(f32) + got.astype(f32)
        if step + 1 < len(plane):
            both = jnp.concatenate([both[:cut], both[cut : cut + count] + both[cut + count :]])
        total = both
    got = swap(total, 1, n_dp)
    big = big.reshape(-1, feats)
    big_got = swap(big, 1, n_dp)
    outs = finish(
        heads, hd, gates, size, width, units, jnp.reshape(core, (1,)), total, got, big, big_got
    )
    dw, grad_ow, grad_fc1, grad_fc2, grad_table, grad_gate_weight, dqv_bias, grad_gate_bias, grad_gate_scale = outs[:9]
    sums = outs[9:]
    dw = dw.reshape(3, width, feats).transpose(0, 2, 1)
    grad_table = grad_table.T
    grad_gate_weight = grad_gate_weight.T
    input_grad = back
    return (
        normed, input_grad, dw, dqv_bias, grad_table, grad_gate_weight, grad_gate_bias, grad_gate_scale, grad_ow, sums[5],
        sums[3], sums[4], grad_fc1, sums[6], grad_fc2, sums[2], sums[0], sums[1],
    )


def solution(mesh):
    in_specs = (
        P("dp", None), P("dp", None), P(), P(None, None, "mp"), P(None, "mp"), P(None, "mp"), P(), P(), P("mp"),
        P("mp", None), P(), P(), P(), P(None, "mp"), P("mp"), P("mp", None), P(), P(), P(), P("dp", None),
    )
    out_specs = (
        P("dp", None), P("dp", None), P(None, None, "mp"), P(None, "mp"), P(None, "mp"), P(), P(), P("mp"),
        P("mp", None), P(), P(), P(), P(None, "mp"), P("mp"), P("mp", None), P(), P(), P(),
    )
    fn = functools.partial(body, mesh.shape["dp"], mesh.shape["mp"])
    return jax.shard_map(fn, mesh=mesh, in_specs=in_specs, out_specs=out_specs, check_vma=False)
```

```python
import functools

import jax
import jax.numpy as jnp
from jax import lax
from jax.experimental import pallas as pl
from jax.experimental.pallas import tpu as pltpu
from jax.sharding import PartitionSpec as P

norm_eps = 1e-05
deep_alpha = 24.0**0.25
masked_score = -1e30
bf = jnp.bfloat16
f32 = jnp.float32
LANES = 128
LIMIT = 60
COST = 3_000_000_000


def nn(a, b):
    return lax.dot_general(a, b, (((1,), (0,)), ((), ())), preferred_element_type=f32)


def nt(a, b):
    return lax.dot_general(a, b, (((1,), (1,)), ((), ())), preferred_element_type=f32)


def params(mib):
    return pltpu.CompilerParams(vmem_limit_bytes=mib * 1024 * 1024)


def lines_kernel(at_ref, table_ref, b1_ref, qv_ref, scale_ref, *refs):
    if len(refs) == 2:
        out_ref, cut_ref = refs
    else:
        w1_hbm, w2_hbm, out_ref, cut_ref, mine_ref, sem = refs
        per = mine_ref.shape[1]
        spot = pl.ds(pl.multiple_of(at_ref[0] * per, per), per)
        copies = [
            pltpu.make_async_copy(w.at[spot], mine_ref.at[i], sem.at[i]) for i, w in enumerate((w1_hbm, w2_hbm))
        ]
        for c in copies:
            c.start()
    heads, size = table_ref.shape
    feats = out_ref.shape[1]
    width = qv_ref.shape[1]
    out_ref[...] = jnp.zeros_like(out_ref)
    per = -(-size // LANES) * LANES
    for h in range(heads):
        out_ref[pl.ds(h * per // feats, 1), pl.ds(h * per % feats, size)] = table_ref[pl.ds(h, 1), :]
    out_ref[pl.ds(2, 1), :] = b1_ref[...].reshape(1, feats)
    out_ref[pl.ds(3, 1), pl.ds(0, width)] = qv_ref[pl.ds(0, 1), :]
    out_ref[pl.ds(3, 1), pl.ds(256, width)] = qv_ref[pl.ds(1, 1), :]
    out_ref[pl.ds(3, 1), pl.ds(512, heads)] = scale_ref[...].reshape(1, heads)
    rest = out_ref[...]
    cuts = []
    for _ in range(3):
        cut = rest.astype(bf).astype(f32)
        cuts.append(cut)
        rest = rest - cut
    cut_ref[...] = jnp.concatenate(cuts + [jnp.zeros_like(rest)], axis=0).astype(bf)
    if len(refs) > 2:
        for c in copies:
            c.wait()


def lines_of(at, table, b1, qv, scale, w1, w2, n):
    feats = b1.shape[0]
    per = w1.shape[0] // n
    fits = per % 16 == 0
    sds = jax.ShapeDtypeStruct
    hbm = [pl.BlockSpec(memory_space=pl.ANY)]
    outs = pl.pallas_call(
        lines_kernel,
        in_specs=[pl.BlockSpec(memory_space=pltpu.SMEM)] + [pl.BlockSpec()] * 4 + hbm * 2 * fits,
        out_specs=[pl.BlockSpec()] * (2 + fits),
        out_shape=[sds((4, feats), f32), sds((16, feats), bf)] + [sds((2, per, w1.shape[1]), bf)] * fits,
        scratch_shapes=[pltpu.SemaphoreType.DMA((2,))] * fits,
        compiler_params=params(LIMIT),
        name="lines",
    )(jnp.reshape(at, (1,)), table, b1, qv, scale, *((w1, w2) if fits else ()))
    if fits:
        return outs
    return *outs, jnp.stack([lax.dynamic_slice_in_dim(w, at * per, per, 0) for w in (w1, w2)])


def bias_kernel(heads, chunks, buckets_ref, small_ref, out_ref):
    rows, cols = buckets_ref.shape
    groups, _, feats = small_ref.shape
    for r in range(0, rows, 8):
        at = pl.ds(r, 8)
        for c in range(cols // LANES):
            lanes = pl.ds(c * LANES, LANES)
            idx = buckets_ref[at, lanes]
            low = idx & (LANES - 1)
            high = idx >> 7
            for h in range(heads):
                got = None
                for k in range(chunks):
                    spot = ((h % 3) * chunks + k) * LANES
                    line = jnp.broadcast_to(
                        small_ref[h // 3, pl.ds(spot // feats, 1), pl.ds(spot % feats, LANES)], (8, LANES)
                    )
                    part = jnp.take_along_axis(line, low, axis=1, mode="promise_in_bounds")
                    got = part if got is None else jnp.where(high == k, part, got)
                out_ref[h, at, lanes] = got


def bias_of(buckets_t, small, heads, size):
    groups, _, feats = small.shape
    seq = buckets_t.shape[0]
    rows = 64
    cost = pl.CostEstimate(flops=COST, bytes_accessed=1 << 20, transcendentals=0)
    return pl.pallas_call(
        functools.partial(bias_kernel, heads * groups, -(-size // LANES)),
        grid=(seq // rows,),
        in_specs=[
            pl.BlockSpec((rows, seq), lambda i: (i, 0)),
            pl.BlockSpec((groups, 4, feats), lambda i: (0, 0, 0)),
        ],
        out_specs=pl.BlockSpec((heads * groups, rows, seq), lambda i: (0, i, 0)),
        out_shape=jax.ShapeDtypeStruct((heads * groups, seq, seq), f32),
        compiler_params=params(30),
        cost_estimate=cost,
        name="pos_bias",
    )(buckets_t, small)


def tiled(v, lanes):
    while v.shape[1] < LANES:
        v = jnp.concatenate([v, v], axis=1)
    return jnp.concatenate([v] * (lanes // v.shape[1]), axis=1)


def head_lanes(shape, head, hd):
    return lax.broadcasted_iota(jnp.int32, shape, 1) // hd == head


def fill_mask(mask, seg_ref, row):
    seq = mask.shape[0]
    line = seg_ref[pl.ds(row, 1), :].astype(f32)
    column = jnp.broadcast_to(line, (8, seq)).T[:, :1]
    for c in range(0, seq, LANES):
        mask[:, pl.ds(c, LANES)] = jnp.where(column == line[:, c : c + LANES], 0.0, masked_score)


def attend_kernel(
    heads, hd, first, x_ref, wt_ref, wl_ref, pos_ref, gw_ref, small_ref, seg_ref, gbias_ref, at_ref,
    qkv_ref, ctx_ref, prob_ref, gate_ref, mask, sc, pr, ctx_t,
):
    group = pl.program_id(0)
    width = heads * hd
    seqs, seq = seg_ref.shape
    gates = gw_ref.shape[0]
    feats = x_ref.shape[1]
    half = gates // 2
    cut = wt_ref.shape[1]
    strips = [pl.ds(c, 2 * LANES) for c in range(0, seq, 2 * LANES)]

    def line(row):
        return pl.ds(row * seq, seq)

    cols = jnp.broadcast_to(small_ref[0, pl.ds(3, 1), pl.ds(0, 512)], (8, 512)).T[:, :1]
    gw = tiled(gw_ref[...].astype(f32), feats)
    mine = [jnp.where(head_lanes(gw.shape, at_ref[first + group] * heads + h, hd), gw, 0.0) for h in range(heads)]
    mine = jnp.concatenate(mine, axis=0).astype(bf)
    bias_a = gbias_ref[0] + gbias_ref[1] + gbias_ref[2] + gbias_ref[3]
    bias_b = gbias_ref[4] + gbias_ref[5] + gbias_ref[6] + gbias_ref[7]
    lins = {}

    def project(row):
        x = x_ref[line(row), :]
        upper = nt(wt_ref[0], x)
        lower = nt(wl_ref[0], x)
        qkv_ref[0, row, pl.ds(0, width), :] = (upper[:width] + cols[:width]).astype(bf) * bf(hd**-0.5)
        qkv_ref[0, row, pl.ds(width, width), :] = upper[width:cut].astype(bf)
        qkv_ref[0, row, pl.ds(2 * width, width), :] = (lower + cols[256 : 256 + width]).astype(bf)
        lins[row] = nt(mine, x)
        fill_mask(mask.at[row], seg_ref, row)

    def score(i):
        row, h = divmod(i, heads)
        k_t = qkv_ref[0, row, pl.ds(width + h * hd, hd), :]
        sc[i % 2] = nn(k_t.T, qkv_ref[0, row, pl.ds(h * hd, hd), :])

    def weigh(i):
        row, h = divmod(i, heads)
        lin = lins[row]
        first = jax.nn.sigmoid(jnp.sum(lin[h * gates : h * gates + half], axis=0, keepdims=True) + bias_a)
        second = jax.nn.sigmoid(jnp.sum(lin[h * gates + half : (h + 1) * gates], axis=0, keepdims=True) + bias_b)
        gate = first * (second * small_ref[0, pl.ds(3, 1), pl.ds(512 + h, 1)] - 1.0) + 2.0
        gate_ref[0, row, pl.ds(h, 1), :] = first
        gate_ref[0, row, pl.ds(heads + h, 1), :] = second
        for at in strips:
            s = sc[i % 2, :, at] + pos_ref[h, :, at] * gate[:, at.start : at.start + at.size] + mask[row, :, at]
            top = jnp.max(s, axis=0, keepdims=True)
            p = jnp.exp(s - top)
            p = p * (1.0 / jnp.sum(p, axis=0, keepdims=True))
            prob_ref[0, row, h, :, at] = p
            pr[i % 2, :, at] = p.astype(bf)

    def gather(i):
        row, h = divmod(i, heads)
        v_t = qkv_ref[0, row, pl.ds(2 * width + h * hd, hd), :]
        ctx_t[pl.ds(h * hd, hd), :] = nn(v_t, pr[i % 2])
        if h == heads - 1:
            ctx_ref[0, line(row), :] = ctx_t[...].T.astype(bf)

    count = seqs * heads
    project(0)
    score(0)
    for i in range(count):
        if i + 1 < count:
            if (i + 1) % heads == 0:
                project((i + 1) // heads)
            score(i + 1)
        weigh(i)
        if i:
            gather(i - 1)
    gather(count - 1)


def back_group(
    heads, hd, own, x_of, w_v, pos_of, gw_ref, small, seqs, seq, head0, qkv_of, prob_of, gate_of, dctx_of, add,
    table_v, finish, dp, pr, ds, wide, ready,
):
    width = heads * hd
    feats = w_v.shape[1]
    strips = [pl.ds(c, 2 * LANES) for c in range(0, seq, 2 * LANES)]
    gw = tiled(gw_ref[...].astype(f32), feats)
    half = gw.shape[0] // 2
    sums = [jnp.sum(gw[:half], axis=0, keepdims=True), jnp.sum(gw[half:], axis=0, keepdims=True)]
    lanes_of = [head_lanes((1, feats), head0 + h, hd) for h in range(heads)]
    gsum = [jnp.where(lanes_of[h], part, 0.0) for part in sums for h in range(heads)]
    w_v[pl.ds(3 * width, 16), :] = jnp.concatenate(gsum + [jnp.zeros((16 - 2 * heads, feats), f32)], axis=0).astype(bf)
    gate_parts = {}

    def score(i):
        row, h = divmod(i, heads)
        if h == 0:
            ready("row", row)
        v_t = qkv_of(row, 2 * width + h * hd, hd)
        dp[i % 2] = nn(v_t.T, dctx_of(row, h * hd, hd))

    def weigh(i):
        row, h = divmod(i, heads)
        if row == 0:
            ready("pos", h)
        ready("prob", i)
        b = i % 2
        first = gate_of(row, h)
        second = gate_of(row, heads + h)
        scale = small[pl.ds(3, 1), pl.ds(512 + h, 1)]
        gate = first * (second * scale - 1.0) + 2.0
        sums_of = []
        for at in strips:
            here = slice(at.start, at.start + at.size)
            pos = pos_of(h, at)
            p = prob_of(row, h, at)
            pr[b, :, at] = p.astype(bf)
            g = dp[b, :, at]
            centre = jnp.sum(p * g, axis=0, keepdims=True)
            low = (p * (g - centre)).astype(bf)
            ds[b, :, at] = low
            d = low.astype(f32)
            sums_of.append(jnp.sum(d * pos, axis=0, keepdims=True))
            if own:
                tab = gate[:, here] * d
                if row == 0:
                    table_v[h, :, at] = tab
                else:
                    table_v[h, :, at] += tab
        if own and row == seqs - 1:
            finish("table", h)
        dgate = jnp.concatenate(sums_of, axis=1)
        dfirst = dgate * (second * scale - 1.0) * first * (1.0 - first)
        dsecond = dgate * first * scale * second * (1.0 - second)
        gate_parts[i] = (dfirst, dsecond, dgate * first * second)

    def gather(i):
        row, h = divmod(i, heads)
        b = i % 2
        q_t = qkv_of(row, h * hd, hd)
        k_t = qkv_of(row, width + h * hd, hd)
        g_t = dctx_of(row, h * hd, hd)
        for j, d in enumerate((nn(k_t, ds[b]) * hd**-0.5, nt(q_t, ds[b]), nt(g_t, pr[b]))):
            wide[row, pl.ds(j * width + h * hd, hd), :] = d.astype(bf)
        if h < heads - 1:
            return
        lines = [gate_parts[row * heads + j][k] for k in (0, 1) for j in range(heads)]
        low = jnp.concatenate(lines + [jnp.zeros((16 - 2 * heads, seq), f32)], axis=0).astype(bf)
        wide[row, pl.ds(3 * width, 16), :] = low
        if row == 0:
            ready("w", 0)
        add(row, nn(wide[row].T, w_v[...]))
        if not own:
            return
        ready("x", row)
        x = x_of(row)
        main = wide[row, pl.ds(0, 3 * width), :]
        dw_here = nn(main, x)
        rest = jnp.concatenate(lines, axis=0) - low[: 2 * heads].astype(f32)
        dgw = nn(low, x)[: 2 * heads] + nn(jnp.concatenate([rest.astype(bf)] * 3, axis=0)[:16], x)[: 2 * heads]
        one = sum(jnp.where(lanes_of[j], dgw[j : j + 1], 0.0) for j in range(heads))
        two = sum(jnp.where(lanes_of[j], dgw[heads + j : heads + j + 1], 0.0) for j in range(heads))
        qv = nt(jnp.ones((8, seq), bf), main)[:1]
        lane = lax.broadcasted_iota(jnp.int32, (1, feats), 1)

        def spot_of(k, v):
            return jnp.where(lane == k, jnp.sum(v, axis=1, keepdims=True), 0.0)

        biases = spot_of(0, sum(lines[:heads])) + spot_of(1, sum(lines[heads:]))
        gains = sum(spot_of(j, gate_parts[row * heads + j][2]) for j in range(heads))
        none = jnp.zeros((1, feats), f32)
        qv = jnp.concatenate([qv, none[:, : feats - qv.shape[1]]], axis=1)
        finish("row", row, dw_here, jnp.concatenate([one, two, biases, none, qv, gains, none, none], axis=0))

    count = seqs * heads
    score(0)
    for i in range(count):
        if i + 1 < count:
            score(i + 1)
        weigh(i)
        if i:
            gather(i - 1)
    gather(count - 1)


def back_own_kernel(
    heads, hd, wt_hbm, wl_hbm, pos_hbm, qkv_hbm, dctx_hbm, base_hbm, x_hbm, prob_hbm,
    gw_ref, small_ref, at_ref, gate_ref,
    grad_hbm, dw_hbm, tiny_ref, table_hbm,
    w_v, pos_v, qkv_v, dctx_v, base_v, dp, pr, ds, wide, dw_v, x_v, table_v, prob_v, sem,
):
    width = heads * hd
    seqs, seq, _ = base_v.shape
    cut = wt_hbm.shape[1]
    count = iter(range(64))

    def line(row):
        return pl.ds(row * seq, seq)

    def copy(src, dst):
        return pltpu.make_async_copy(src, dst, sem.at[next(count)])

    w_in = [
        copy(wt_hbm.at[0], w_v.at[pl.ds(0, cut)]),
        copy(wl_hbm.at[1, pl.ds(0, 3 * width - cut)], w_v.at[pl.ds(cut, 3 * width - cut)]),
    ]
    pos_in = [copy(pos_hbm.at[h], pos_v.at[h]) for h in range(heads)]
    row_in = [[copy(qkv_hbm.at[0, r], qkv_v.at[r]), copy(dctx_hbm.at[0, r], dctx_v.at[r])] for r in range(seqs)]
    prob_in = [copy(prob_hbm.at[0, r, h], prob_v.at[r, h]) for r in range(seqs) for h in range(heads)]
    base_in = [copy(base_hbm.at[line(r)], base_v.at[r]) for r in range(seqs)]
    grad_out = [copy(base_v.at[r], grad_hbm.at[line(r)]) for r in range(seqs)]
    x_in = [copy(x_hbm.at[line(r)], x_v.at[r]) for r in range(seqs)]
    table_out = [copy(table_v.at[h], table_hbm.at[h]) for h in range(heads)]
    dw_out = copy(dw_v, dw_hbm)
    for c in row_in[0] + [prob_in[0], pos_in[0]] + prob_in[1:heads] + pos_in[1:] + row_in[1] + w_in + prob_in[heads:] + base_in + x_in:
        c.start()

    def ready(what, i):
        for c in {"row": lambda: row_in[i], "pos": lambda: [pos_in[i]], "w": lambda: w_in, "x": lambda: [x_in[i]], "prob": lambda: [prob_in[i]]}[what]():
            c.wait()

    def add(row, part):
        base_in[row].wait()
        base_v[row] = deep_alpha * base_v[row] + part
        grad_out[row].start()

    def finish(what, i, *values):
        if what == "table":
            table_out[i].start()
        elif i == 0:
            dw_v[...], tiny_ref[...] = values
        else:
            dw_v[...] += values[0]
            tiny_ref[...] += values[1]
            if i == seqs - 1:
                dw_out.start()

    back_group(
        heads, hd, True, lambda r: x_v[r], w_v, lambda h, at: pos_v[h, :, at], gw_ref, small_ref.at[0], seqs, seq,
        at_ref[0] * heads, lambda r, i, n: qkv_v[r, pl.ds(i, n), :], lambda r, h, at: prob_v[r, h, :, at],
        lambda r, h: gate_ref[0, r, pl.ds(h, 1), :], lambda r, i, n: dctx_v[r, pl.ds(i, n), :], add, table_v, finish,
        dp, pr, ds, wide, ready,
    )
    for c in grad_out + table_out + [dw_out]:
        c.wait()


def back_rest_kernel(
    heads, hd, first, wt_ref, wl_ref, pos_ref, qkv_ref, dctx_ref, base_hbm,
    prob_hbm, gw_ref, small_ref, at_ref, gate_ref,
    grad_hbm,
    w_v, base_v, dp, pr, ds, wide, prob_v, sem, prob_sem,
):
    step = pl.program_id(0)
    last = pl.num_programs(0) - 1
    width = heads * hd
    seqs, seq, _ = base_v.shape
    slot = lax.rem(step, 2)
    cut = wt_ref.shape[1]

    def line(row):
        return pl.ds(row * seq, seq)

    base_in = [pltpu.make_async_copy(base_hbm.at[line(r)], base_v.at[r], sem.at[r]) for r in range(seqs)]
    grad_out = [pltpu.make_async_copy(base_v.at[r], grad_hbm.at[line(r)], sem.at[seqs + r]) for r in range(seqs)]

    def prob_in(at, to, i):
        r, h = divmod(i, heads)
        return pltpu.make_async_copy(prob_hbm.at[first + at, r, h], prob_v.at[to, i], prob_sem.at[to, i])

    @pl.when(step == 0)
    def _():
        for i in range(seqs * heads):
            prob_in(step, slot, i).start()
        for c in base_in:
            c.start()

    @pl.when(step < last)
    def _():
        for i in range(seqs * heads):
            prob_in(step + 1, 1 - slot, i).start()

    def ready(what, i):
        if what == "prob":
            prob_in(step, slot, i).wait()

    w_v[pl.ds(0, cut), :] = wt_ref[0]
    w_v[pl.ds(cut, 3 * width - cut), :] = wl_ref[0]

    def add(row, part):
        @pl.when(step == 0)
        def _():
            base_in[row].wait()

        base_v[row] += part

        @pl.when(step == last)
        def _():
            grad_out[row].start()

    back_group(
        heads, hd, False, None, w_v, lambda h, at: pos_ref[h, :, at], gw_ref, small_ref.at[0], seqs, seq,
        at_ref[1 + first + step] * heads, lambda r, i, n: qkv_ref[0, r, pl.ds(i, n), :],
        lambda r, h, at: prob_v[slot, r * heads + h, :, at],
        lambda r, h: gate_ref[0, r, pl.ds(h, 1), :], lambda r, i, n: dctx_ref[0, r, pl.ds(i, n), :], add, None, None,
        dp, pr, ds, wide, ready,
    )

    @pl.when(step == last)
    def _():
        for c in grad_out:
            c.wait()


def norm_stats(v):
    mean = jnp.mean(v, axis=-1, keepdims=True)
    cen = v - mean
    rs = lax.rsqrt(jnp.mean(cen * cen, axis=-1, keepdims=True) + norm_eps)
    return cen * rs, rs


def norm_back(g, n, rs, gain):
    gn = g * gain
    return rs * (gn - jnp.mean(gn, axis=-1, keepdims=True) - n * jnp.mean(gn * n, axis=-1, keepdims=True))


def gelu_pair(x):
    cdf = 0.5 + 0.5 * lax.erf(x * 0.5**0.5)
    return x * cdf, cdf + x * jnp.exp(x * x * -0.5) * 0.3989422804014327


def weave(*runs):
    runs = list(runs)
    while runs:
        runs = [r for r in runs if next(r, runs) is not runs]


def layer_kernel(
    ctx0_ref, ctx_ref, x_ref, go_ref, ow0_hbm, ow_hbm, w10_hbm, small_ref, smalls_ref,
    w20_hbm, all_hbm, out_bias_ref, gain1_ref, bias1_ref, bias2_ref, gain2_ref, beta2_ref, at_ref,
    out_ref, first_ref, dctx_ref, hid_low_ref, mix_low_ref, first_low_ref, act_ref, pre_low_ref, sums_ref,
    ow_v, w1_v, w2_v, act, slope, plow, wide, scale, acc, own_acc, sem,
):
    step = pl.program_id(0)
    ctxs = [ctx0_ref.at[0]] + [ctx_ref.at[i] for i in range(ctx_ref.shape[0])]
    width = ow0_hbm.shape[0]
    own = w20_hbm.shape[0]
    count = iter(range(128))
    _, pieces, _, per, feats = all_hbm.shape
    chains, rows = act.shape[:2]
    part = 64

    def copy(src, dst):
        return pltpu.make_async_copy(src, dst, sem.at[next(count)])

    ow_in = [copy(ow0_hbm, ow_v.at[pl.ds(0, width)])]
    for i in range(1, len(ctxs)):
        ow_in.append(copy(ow_hbm.at[i - 1, pl.ds(ow_hbm.shape[1] - width, width)], ow_v.at[pl.ds(i * width, width)]))
    w_in = []
    for k, (mine, all_v) in enumerate(((w10_hbm, w1_v), (w20_hbm, w2_v))):
        w_in.append([copy(mine, all_v.at[pl.ds(0, own)])])
        parted = all_v.reshape(len(ctxs) * pieces, per, feats)
        for i in range(1, len(ctxs)):
            w_in[k].append(copy(all_hbm.at[at_ref[i], :, k], parted.at[pl.ds(i * pieces, pieces)]))

    @pl.when(step == 0)
    def _():
        for c in ow_in + w_in[0] + w_in[1]:
            c.start()
        for c in ow_in:
            c.wait()
        acc[...] = jnp.zeros_like(acc)
        own_acc[...] = jnp.zeros_like(own_acc)

    vectors = (out_bias_ref, gain1_ref, bias1_ref, bias2_ref, gain2_ref, beta2_ref)
    out_bias, gain1, bias1, bias2, gain2, beta2 = (ref[...].reshape(1, feats) for ref in vectors)
    b1 = [small_ref[pl.ds(2, 1), :]] + [smalls_ref[i, pl.ds(2, 1), :] for i in range(len(ctxs) - 1)]
    b1 = jnp.concatenate(b1, axis=1)
    block = 256
    blocks = [pl.ds(u, block) for u in range(0, w2_v.shape[0], block)]
    cols = [pl.ds(u, block) for u in range(0, feats, block)]

    def lines(c):
        for r in range(0, rows, part):
            yield pl.ds(r, part), pl.ds(c * rows + r, part)

    def tally(i, v):
        acc[i] += jnp.sum(v.reshape(part // 8, 8, feats), axis=0)

    def enter(c):
        total = nn(ctxs[0][pl.ds(c * rows, rows), :], ow_v[pl.ds(0, width), :])
        for i in range(1, len(ctxs)):
            total = total + nn(ctxs[i][pl.ds(c * rows, rows), :], ow_v[pl.ds(i * width, width), :])
        wide[c, 2] = total
        yield
        for r, at in lines(c):
            n, rs = norm_stats(deep_alpha * x_ref[at, :].astype(f32) + out_bias + wide[c, 2, r, :])
            hidden = n * gain1 + bias1
            wide[c, 0, r, :] = n
            wide[c, 1, r, :] = hidden
            scale[c, r, :] = jnp.broadcast_to(rs, (part, LANES))
            hid_low_ref[at, :] = hidden.astype(bf)
            yield

    def up(c):
        at_rows = pl.ds(c * rows, rows)
        for at in blocks:
            group, inner = divmod(at.start, own)
            pre = nn(hid_low_ref[at_rows, :], w1_v[pl.ds(group * feats, feats), pl.ds(inner, block)])
            pre = pre + b1[:, at.start : at.start + block]
            a, s = gelu_pair(pre)
            act[c, :, at] = a.astype(bf)
            slope[c, :, at] = s
            yield
        act_ref[at_rows, :] = act[c, :, pl.ds(0, own)]

    def down(c):
        for at in cols:
            wide[c, 2, :, at] = nn(act[c], w2_v[:, at])
            yield

    def turn(c):
        for r, at in lines(c):
            n, rs = norm_stats(deep_alpha * wide[c, 1, r, :] + bias2 + wide[c, 2, r, :])
            out_ref[at, :] = n * gain2 + beta2
            g = go_ref[at, :].astype(f32)
            grad = norm_back(g, n, rs, gain2)
            wide[c, 1, r, :] = grad
            mix_low_ref[at, :] = grad.astype(bf)
            tally(0, g * n)
            tally(1, g)
            tally(2, grad)
            yield

    def back_down(c):
        at_rows = pl.ds(c * rows, rows)
        for at in blocks:
            d = nt(mix_low_ref[at_rows, :], w2_v[at, :]) * slope[c, :, at]
            if at.start < own:
                own_acc[:, at] += jnp.sum(d.reshape(rows // 8, 8, block), axis=0)
            plow[c, :, at] = d.astype(bf)
            yield
        pre_low_ref[at_rows, :] = plow[c, :, pl.ds(0, own)]

    def back_up(c):
        for at in cols:
            total = nt(plow[c, :, pl.ds(0, own)], w1_v[at, :])
            for i in range(1, len(ctxs)):
                total = total + nt(plow[c, :, pl.ds(i * own, own)], w1_v[pl.ds(i * feats + at.start, block), :])
            wide[c, 2, :, at] = total
            yield

    def leave(c):
        at_rows = pl.ds(c * rows, rows)
        for r, at in lines(c):
            n = wide[c, 0, r, :]
            grad = deep_alpha * wide[c, 1, r, :] + wide[c, 2, r, :]
            first = norm_back(grad, n, scale[c, r, :1], gain1)
            first_ref[at, :] = first
            first_low_ref[at, :] = first.astype(bf)
            tally(3, grad * n)
            tally(4, grad)
            tally(5, first)
            yield
        dctx = nt(ow_v[...], first_low_ref[at_rows, :]).astype(bf)
        for i in range(len(ctxs)):
            dctx_ref[i, 0, :, at_rows] = dctx[i * width : (i + 1) * width]
        yield

    def wait(which):
        @pl.when(step == 0)
        def _():
            for c in w_in[which]:
                c.wait()

    stages = (enter, up, down, turn, back_down, back_up, leave)
    for t in range(len(stages) + chains - 1):
        if t == 1:
            wait(0)
        if t == 2:
            wait(1)
        weave(*[stages[t - c](c) for c in range(chains) if 0 <= t - c < len(stages)])

    @pl.when(step == pl.num_programs(0) - 1)
    def _():
        rows_of = [jnp.sum(acc[i], axis=0, keepdims=True) for i in range(6)]
        rows_of.append(jnp.sum(own_acc[...], axis=0, keepdims=True))
        sums_ref[...] = jnp.concatenate(rows_of + [jnp.zeros_like(rows_of[0])], axis=0)


def table_kernel(heads, tops, lows, buckets_ref, val_ref, out_ref):
    rows, cols = buckets_ref.shape
    top_id = lax.broadcasted_iota(jnp.int32, (tops, cols), 0)
    low_id = lax.broadcasted_iota(jnp.int32, (lows, cols), 0)
    unroll = 128

    def group(g, acc):
        for u in range(0, unroll, 8):
            at = pl.ds(pl.multiple_of(g * unroll, unroll) + u, 8)
            idx = buckets_ref[at, :]
            high = idx >> 4
            low = idx & 15
            vals = [val_ref[h, at, :] for h in range(heads)]
            for i in range(8):
                a = jnp.where(high[i : i + 1] == top_id, 1.0, 0.0).astype(bf)
                hit = low[i : i + 1] == low_id
                b = jnp.concatenate([jnp.where(hit, v[i : i + 1], 0.0).astype(bf) for v in vals], axis=0)
                acc = acc + nt(a, b)
        return acc

    out_ref[...] = jnp.zeros_like(out_ref)
    out_ref[:, pl.ds(0, heads * lows)] = lax.fori_loop(
        0, rows // unroll, group, jnp.zeros((tops, heads * lows), f32)
    )


def table_grad(buckets_t, values, size, feats):
    heads, seq, _ = values.shape
    lows = 16
    tops = -(-size // lows // 8) * 8
    return pl.pallas_call(
        functools.partial(table_kernel, heads, tops, lows),
        out_shape=jax.ShapeDtypeStruct((tops, feats), f32),
        compiler_params=params(24),
        cost_estimate=pl.CostEstimate(flops=COST, bytes_accessed=1 << 20, transcendentals=0),
        name="table_grad",
    )(buckets_t, values)


def finish_kernel(
    heads, hd, size, core_ref, total_ref, got_ref, big_ref, big_got_ref,
    dw_ref, ow_ref, fc1_ref, fc2_ref, table_ref, gate_ref, qv_ref, gate_bias_ref, scale_ref, *sum_refs,
):
    later = core_ref[0] == 1
    total, got = total_ref[...], got_ref[...]
    first = jnp.where(later, got, total)
    second = jnp.where(later, total, got)
    cut = dw_ref.shape[0] // 2
    dw_ref[pl.ds(0, cut), :] = first[:cut]
    dw_ref[pl.ds(cut, cut), :] = second[:cut]
    extra = jnp.concatenate([first[cut:], second[cut:]], axis=0)
    feats = extra.shape[1]
    width = ow_ref.shape[0]
    for mine in (False, True):
        part = jnp.where(later == mine, big_ref[...], big_got_ref[...]).astype(f32)
        ow_ref[pl.ds(width // 2 * mine, width // 2), :] = part[feats:]
        (fc2_ref if mine else fc1_ref)[...] = part[:feats]
    for i, ref in enumerate(sum_refs):
        ref[...] = extra[i]
    halves = sum(extra[8:10, c : c + LANES] for c in range(0, feats, LANES))
    halves = sum(halves[:, c : c + hd] for c in range(0, LANES, hd))
    gates = gate_ref.shape[0]
    gate_ref[...] = jnp.concatenate([halves[i : i + 1] for i in range(2) for _ in range(gates // 2)], axis=0)
    qv_ref[pl.ds(0, 1), :] = extra[12:13, :width]
    qv_ref[pl.ds(1, 1), :] = extra[12:13, 2 * width : 3 * width]
    lane = lax.broadcasted_iota(jnp.int32, (1, LANES), 1)
    pair = jnp.where(lane < gates // 2, extra[10:11, 0:1], extra[10:11, 1:2])
    gate_bias_ref[...] = pair[:, :gates]
    scale_ref[...] = extra[13:14, :heads]
    lows = 16
    tops = extra.shape[0] - 16
    wide = tops * lows
    spread = lax.broadcasted_iota(jnp.int32, (lows, wide), 1) % lows == lax.broadcasted_iota(jnp.int32, (lows, wide), 0)
    spread = jnp.where(spread, 1.0, 0.0).astype(bf)
    keep = lax.broadcasted_iota(jnp.int32, (tops, wide), 1) // lows == lax.broadcasted_iota(jnp.int32, (tops, wide), 0)
    for h in range(heads):
        rest = extra[16:, h * lows : (h + 1) * lows]
        line = jnp.zeros((tops, wide), f32)
        for _ in range(3):
            part = rest.astype(bf)
            line = line + nn(part, spread)
            rest = rest - part.astype(f32)
        line = jnp.sum(jnp.where(keep, line, 0.0), axis=0, keepdims=True)
        table_ref[pl.ds(h, 1), :] = line[:, :size]


def finish(heads, hd, gates, size, width, units, core, total, got, big, big_got):
    feats = total.shape[1]
    sds = jax.ShapeDtypeStruct
    vector = sds((feats,), f32)
    outs = pl.pallas_call(
        functools.partial(finish_kernel, heads, hd, size),
        in_specs=[pl.BlockSpec(memory_space=pltpu.SMEM)] + [pl.BlockSpec()] * 4,
        out_shape=[
            sds((3 * width, feats), f32), sds((width, feats), f32), sds((feats, units), f32), sds((units, feats), f32),
            sds((heads, size), f32), sds((gates, hd), f32), sds((2, width), f32), sds((1, gates), f32), sds((1, heads), f32),
        ]
        + [vector] * 7,
        compiler_params=params(24),
        name="finish",
    )(core, total, got, big, big_got)
    outs = list(outs)
    outs[7], outs[8] = outs[7][0], outs[8][0]
    return outs


def rotate(x, by, n):
    return lax.ppermute(x, "mp", [(i, (i + by) % n) for i in range(n)])


def swap(x, bit, n, axis="dp"):
    return lax.ppermute(x, axis, [(i, i ^ bit) for i in range(n)])


def after(x, *earlier):
    return lax.optimization_barrier((x,) + earlier)[0]


def joined(pieces, got, bit, index, have):
    at = 1 + sum(b > bit for b in have)
    mine = (index & bit) != 0
    return jnp.stack([jnp.where(mine, got, pieces), jnp.where(mine, pieces, got)], axis=at)


def body(
    n_dp, n_mp,
    tokens, segment_ids, buckets, qkv_weight, qv_bias, rel_table, gate_weight, gate_bias, gate_scale, out_weight,
    out_bias, ln1_gain, ln1_bias, fc1_weight, fc1_bias, fc2_weight, fc2_bias, ln2_gain, ln2_bias, grad_out,
):
    rows, feats = tokens.shape
    seqs, seq = segment_ids.shape
    size, heads = rel_table.shape
    hd, gates = gate_weight.shape
    width = heads * hd
    units = fc1_weight.shape[1]
    me = lax.axis_index("mp")
    dp = lax.axis_index("dp")
    order = ((me - jnp.arange(n_mp)) % n_mp).astype(jnp.int32)
    bits = [1 << i for i in range(n_dp.bit_length() - 1)]
    plane = bits[1:]
    others = n_mp - 1
    core = dp & 1
    sds = jax.ShapeDtypeStruct

    hbm = pl.BlockSpec(memory_space=pl.ANY)
    smem = pl.BlockSpec(memory_space=pltpu.SMEM)
    full = pl.BlockSpec()
    square = pltpu.VMEM((seqs, seq, seq), f32)
    pair = pltpu.VMEM((2, seq, seq), f32)
    low_pair = pltpu.VMEM((2, seq, seq), bf)
    gw = gate_weight.T
    lines_t = pltpu.VMEM((seqs, 3 * width, seq), bf)
    outs_t = pltpu.VMEM((seqs, width, seq), f32)
    tables_t = pltpu.VMEM((heads, seq, seq), f32)

    def one(*shape):
        return pl.BlockSpec((1,) + shape, lambda s: (s,) + (0,) * len(shape))

    def whole(*shape):
        return pl.BlockSpec(shape, lambda s: (0,) * len(shape))

    def attend(n, sources, *deps):
        wt, wl, sm, pos = sources
        return pl.pallas_call(
            functools.partial(attend_kernel, heads, hd, 0 if n == 1 else 1),
            grid=(n,),
            in_specs=[
                whole(rows, feats), one(2 * width, feats),
                pl.BlockSpec((1, width, feats), lambda s: (s + (n == 1), 0, 0)),
                pl.BlockSpec((heads, seq, seq), lambda s: (s, 0, 0)), whole(gates, hd), one(4, feats),
                whole(seqs, seq), smem, smem,
            ],
            out_specs=[one(seqs, 3 * width, seq), one(rows, width), one(seqs, heads, seq, seq), one(seqs, 8, seq)],
            scratch_shapes=[square, pair, low_pair, pltpu.VMEM((width, seq), f32)],
            out_shape=[
                sds((n, seqs, 3 * width, seq), bf), sds((n, rows, width), bf), sds((n, seqs, heads, seq, seq), f32),
                sds((n, seqs, 8, seq), f32),
            ],
            compiler_params=params(LIMIT),
            cost_estimate=pl.CostEstimate(flops=n * COST, bytes_accessed=1 << 20, transcendentals=0),
            name="attend",
        )(tokens, wt, wl, pos, gw, sm, segment_ids, gate_bias, after(order, *deps))

    back_scratch = [pair, low_pair, low_pair, pltpu.VMEM((seqs, 3 * width + 16, seq), bf)]
    w_t = pltpu.VMEM((3 * width + 16, feats), bf)
    base_t = pltpu.VMEM((seqs, seq, feats), f32)

    def back_own(sources, front, dctx, base, *deps):
        wt, wl, sm, pos = sources
        qkv_t, _, prob, gate = front
        return pl.pallas_call(
            functools.partial(back_own_kernel, heads, hd),
            in_specs=[hbm] * 8 + [full] * 2 + [smem, full],
            out_specs=[hbm, hbm, full, hbm],
            scratch_shapes=[w_t, tables_t, lines_t, pltpu.VMEM((seqs, width, seq), bf), base_t]
            + back_scratch
            + [
                pltpu.VMEM((3 * width, feats), f32), pltpu.VMEM((seqs, seq, feats), bf), tables_t,
                pltpu.VMEM((seqs, heads, seq, seq), f32), pltpu.SemaphoreType.DMA((3 + 2 * heads + (5 + heads) * seqs,)),
            ],
            out_shape=[
                sds((rows, feats), f32), sds((3 * width, feats), f32), sds((8, feats), f32), sds((heads, seq, seq), f32),
            ],
            compiler_params=params(LIMIT),
            cost_estimate=pl.CostEstimate(flops=COST, bytes_accessed=1 << 20, transcendentals=0),
            name="attend_back",
        )(wt, wl, pos, qkv_t, dctx, base, tokens, prob, gw, sm, after(order, *deps), gate)

    def back_rest(first, n, sources, front, dctx, base, *deps):
        wt, wl, sm, pos = sources
        qkv_t, _, prob, gate = front

        def off(by, *shape):
            return pl.BlockSpec((1,) + shape, lambda s: (s + by,) + (0,) * len(shape))

        return pl.pallas_call(
            functools.partial(back_rest_kernel, heads, hd, first),
            grid=(n,),
            in_specs=[
                off(first, 2 * width, feats), off(first, width, feats),
                pl.BlockSpec((heads, seq, seq), lambda s: (s + first, 0, 0)), off(first, seqs, 3 * width, seq),
                off(first + 1, seqs, width, seq), hbm, hbm, whole(gates, hd), off(first, 4, feats), smem,
                off(first, seqs, 8, seq),
            ],
            out_specs=hbm,
            scratch_shapes=[w_t, base_t]
            + back_scratch
            + [
                pltpu.VMEM((2, seqs * heads, seq, seq), f32), pltpu.SemaphoreType.DMA((2 * seqs,)),
                pltpu.SemaphoreType.DMA((2, seqs * heads)),
            ],
            out_shape=sds((rows, feats), f32),
            compiler_params=params(LIMIT),
            cost_estimate=pl.CostEstimate(flops=n * COST, bytes_accessed=1 << 20, transcendentals=0),
            name="attend_back",
        )(wt, wl, pos, qkv_t, dctx, base, prob, gw, sm, after(order, *deps), gate)

    def piece(w, parts=1):
        per = w.shape[0] // n_dp // parts
        w = w.reshape(parts, n_dp, per, w.shape[1])
        return lax.dynamic_index_in_dim(w, dp, 1, False).reshape(parts * per, -1)

    small, cuts, mine = lines_of(dp, rel_table.T, fc1_bias, qv_bias, gate_scale, fc1_weight, fc2_weight, n_dp)
    gathered = lax.all_gather(mine, ("mp", "dp"))
    w0 = jnp.concatenate([qkv_weight.transpose(0, 2, 1).reshape(3 * width, feats), out_weight], axis=0)
    piece0 = jnp.concatenate([piece(w0, 2), cuts], axis=0)
    w0 = w0.reshape(2, 2 * width, feats)
    z0 = [rotate(piece0, r, n_mp) for r in range(1, n_mp)]
    buckets_t = buckets.T
    pos_own = bias_of(after(buckets_t, piece0), small[None], heads, size)
    z0, pos_own = lax.optimization_barrier((z0, pos_own))
    z0 = jnp.stack(z0)

    mid = 2 * width // n_dp
    got = z0[:, 2 * mid :].astype(f32)
    smalls = (got[:, 0:4] + got[:, 4:8]) + got[:, 8:12]
    own_sources = (w0, w0, small[None], pos_own)
    spreads = [z0[:, :mid], z0[:, mid : 2 * mid]]
    routes = [plane[::-1], plane]
    covers = [lambda *deps: bias_of(after(buckets_t, *deps), smalls, heads, size), lambda *deps: attend(1, own_sources, *deps)]
    done = []
    for step in range(len(plane)):
        gots = [swap(v, route[step], n_dp) for v, route in zip(spreads, routes)]
        if step < len(covers):
            result = covers[step](*spreads)
            gots, result = lax.optimization_barrier((gots, result))
            done.append(result)
        spreads = [joined(v, g, route[step], dp, route[:step]) for v, g, route in zip(spreads, gots, routes)]
    for step in range(len(plane), len(covers)):
        done.append(covers[step]())
    pos_rest, front = done
    gots = [swap(v, 1, n_dp) for v in spreads]
    top, low = (joined(v, g, 1, dp, plane).reshape(others, 2 * width, feats) for v, g in zip(spreads, gots))
    rest_sources = (top, low, smalls, pos_rest)
    fronts = attend(others, rest_sources)
    gathered, fronts = lax.optimization_barrier((gathered, fronts))
    gathered = gathered.reshape(n_mp, n_dp, 2, units // n_dp, feats)
    if units // n_dp % 16:
        gathered = gathered.transpose(0, 2, 1, 3, 4).reshape(n_mp, 1, 2, units, feats)

    tile = 512
    chains = 2

    def row(n):
        return pl.BlockSpec((tile, n), lambda i: (i, 0))

    outs = pl.pallas_call(
        layer_kernel,
        grid=(rows // tile,),
        in_specs=[pl.BlockSpec((n, tile, width), lambda i: (0, i, 0)) for n in (1, others)]
        + [row(feats), row(feats)]
        + [hbm] * 3
        + [full] * 2
        + [hbm] * 2
        + [full] * 6
        + [smem],
        out_specs=[
            row(feats), row(feats), pl.BlockSpec((n_mp, 1, width, tile), lambda i: (0, i * tile // seq, 0, i % (seq // tile))),
            row(feats), row(feats), row(feats), row(units), row(units), pl.BlockSpec((8, feats), lambda i: (0, 0)),
        ],
        scratch_shapes=[
            pltpu.VMEM((n_mp * width, feats), bf), pltpu.VMEM((n_mp * feats, units), bf), pltpu.VMEM((n_mp * units, feats), bf),
            pltpu.VMEM((chains, tile // chains, n_mp * units), bf), pltpu.VMEM((chains, tile // chains, n_mp * units), f32),
            pltpu.VMEM((chains, tile // chains, n_mp * units), bf), pltpu.VMEM((chains, 3, tile // chains, feats), f32),
            pltpu.VMEM((chains, tile // chains, LANES), f32), pltpu.VMEM((6, 8, feats), f32), pltpu.VMEM((8, units), f32),
            pltpu.SemaphoreType.DMA((n_mp + 2 + 2 * others,)),
        ],
        out_shape=[
            sds((rows, feats), f32), sds((rows, feats), f32), sds((n_mp, seqs, width, seq), bf), sds((rows, feats), bf),
            sds((rows, feats), bf), sds((rows, feats), bf), sds((rows, units), bf), sds((rows, units), bf), sds((8, feats), f32),
        ],
        compiler_params=params(LIMIT),
        cost_estimate=pl.CostEstimate(flops=4 * COST, bytes_accessed=1 << 24, transcendentals=0),
        name="layer",
    )(
        front[1], fronts[1], tokens, grad_out, out_weight, low, fc1_weight, small, smalls, fc2_weight, gathered, out_bias, ln1_gain, ln1_bias, fc2_bias, ln2_gain, ln2_bias,
        order,
    )
    normed, grad_first = outs[:2]
    dctx = outs[2]
    hid_low, mix_low, first_low, act_own, pre_own, sums = outs[3:]

    def outer(a, b):
        return lax.dot_general(a, b, (((0,), (0,)), ((), ())), preferred_element_type=f32)

    fc1_part, fc2_part = (outer(a, b).astype(bf) for a, b in ((hid_low, pre_own), (act_own, mix_low)))
    ow_part = outer(front[1][0], first_low).astype(bf).reshape(2, width // 2, feats)
    later = core == 1
    give = [jnp.where(later, fc1_part, fc2_part), jnp.where(later, ow_part[0], ow_part[1])]
    keep = [jnp.where(later, fc2_part, fc1_part), jnp.where(later, ow_part[1], ow_part[0])]
    give, keep = jnp.concatenate(give), jnp.concatenate(keep)
    back, dw, tiny, acc = back_own(own_sources, front, dctx, grad_first, give, keep)
    big = (keep.astype(f32) + swap(give, 1, n_dp).astype(f32)).astype(bf)
    same = [[d for d in range(n_dp) if d % 2 == c] for c in range(2)]
    big = lax.psum_scatter(big, "dp", scatter_dimension=0, tiled=True, axis_index_groups=same)

    shared = tiny
    turned = [rotate(shared, r, n_mp) for r in range(1, n_mp)]
    table = table_grad(after(buckets_t, shared), acc, size, feats)
    table, turned, big = lax.optimization_barrier((table, turned, big))
    route = plane[::-1]
    turned = [shared] + list(turned)
    while len(turned) > 1:
        turned = [a + b for a, b in zip(turned[: len(turned) // 2], turned[len(turned) // 2 :])]
    extra = jnp.concatenate([sums, turned[0][:3], tiny[3:], table], axis=0)
    count = extra.shape[0] // 2

    def parted(flip):
        def pick(v):
            v = v.reshape(2, -1, feats)
            return jnp.where((core == 1) != flip, v[1], v[0])

        return jnp.concatenate([pick(dw), pick(extra)])

    total = parted(False) + swap(parted(True), 1, n_dp)
    cut = dw.shape[0] // 2
    done = 0
    for step, bit in enumerate(plane):
        if step + 1 < len(plane):
            low_part = lax.reduce_precision(total[cut:], 8, 7)
            sent = jnp.concatenate([total[:cut], low_part, total[cut:] - low_part])
            sent = lax.reduce_precision(sent, 8, 7).astype(bf)
            n = 1
        else:
            sent = total
            n = others - done
        got = swap(sent, bit, n_dp)
        big_got = swap(big, route[step], n_dp)
        if done < others:
            back = back_rest(done, n, rest_sources, fronts, dctx, back, sent, big)
            got, big_got, back = lax.optimization_barrier((got, big_got, back))
            done += n
        big = joined(big[None], big_got[None], route[step], dp, route[:step])[0]
        both = sent.astype(f32) + got.astype(f32)
        if step + 1 < len(plane):
            both = jnp.concatenate([both[:cut], both[cut : cut + count] + both[cut + count :]])
        total = both
    got = swap(total, 1, n_dp)
    big = big.reshape(-1, feats)
    big_got = swap(big, 1, n_dp)
    outs = finish(
        heads, hd, gates, size, width, units, jnp.reshape(core, (1,)), total, got, big, big_got
    )
    dw, grad_ow, grad_fc1, grad_fc2, grad_table, grad_gate_weight, dqv_bias, grad_gate_bias, grad_gate_scale = outs[:9]
    sums = outs[9:]
    dw = dw.reshape(3, width, feats).transpose(0, 2, 1)
    grad_table = grad_table.T
    grad_gate_weight = grad_gate_weight.T
    input_grad = back
    return (
        normed, input_grad, dw, dqv_bias, grad_table, grad_gate_weight, grad_gate_bias, grad_gate_scale, grad_ow, sums[5],
        sums[3], sums[4], grad_fc1, sums[6], grad_fc2, sums[2], sums[0], sums[1],
    )


def solution(mesh):
    in_specs = (
        P("dp", None), P("dp", None), P(), P(None, None, "mp"), P(None, "mp"), P(None, "mp"), P(), P(), P("mp"),
        P("mp", None), P(), P(), P(), P(None, "mp"), P("mp"), P("mp", None), P(), P(), P(), P("dp", None),
    )
    out_specs = (
        P("dp", None), P("dp", None), P(None, None, "mp"), P(None, "mp"), P(None, "mp"), P(), P(), P("mp"),
        P("mp", None), P(), P(), P(), P(None, "mp"), P("mp"), P("mp", None), P(), P(), P(),
    )
    fn = functools.partial(body, mesh.shape["dp"], mesh.shape["mp"])
    return jax.shard_map(fn, mesh=mesh, in_specs=in_specs, out_specs=out_specs, check_vma=False)
```

```python
import functools

import jax
import jax.numpy as jnp
from jax import lax
from jax.experimental import pallas as pl
from jax.experimental.pallas import tpu as pltpu
from jax.sharding import PartitionSpec as P

norm_eps = 1e-05
deep_alpha = 24.0**0.25
masked_score = -1e30
bf = jnp.bfloat16
f32 = jnp.float32
LANES = 128
LIMIT = 60
COST = 3_000_000_000


def nn(a, b):
    return lax.dot_general(a, b, (((1,), (0,)), ((), ())), preferred_element_type=f32)


def nt(a, b):
    return lax.dot_general(a, b, (((1,), (1,)), ((), ())), preferred_element_type=f32)


def params(mib):
    return pltpu.CompilerParams(vmem_limit_bytes=mib * 1024 * 1024)


def lines_kernel(at_ref, table_ref, b1_ref, qv_ref, scale_ref, *refs):
    if len(refs) == 2:
        out_ref, cut_ref = refs
    else:
        w1_hbm, w2_hbm, out_ref, cut_ref, mine_ref, sem = refs
        per = mine_ref.shape[1]
        spot = pl.ds(pl.multiple_of(at_ref[0] * per, per), per)
        copies = [
            pltpu.make_async_copy(w.at[spot], mine_ref.at[i], sem.at[i]) for i, w in enumerate((w1_hbm, w2_hbm))
        ]
        for c in copies:
            c.start()
    heads, size = table_ref.shape
    feats = out_ref.shape[1]
    width = qv_ref.shape[1]
    out_ref[...] = jnp.zeros_like(out_ref)
    per = -(-size // LANES) * LANES
    for h in range(heads):
        out_ref[pl.ds(h * per // feats, 1), pl.ds(h * per % feats, size)] = table_ref[pl.ds(h, 1), :]
    out_ref[pl.ds(2, 1), :] = b1_ref[...].reshape(1, feats)
    out_ref[pl.ds(3, 1), pl.ds(0, width)] = qv_ref[pl.ds(0, 1), :]
    out_ref[pl.ds(3, 1), pl.ds(256, width)] = qv_ref[pl.ds(1, 1), :]
    out_ref[pl.ds(3, 1), pl.ds(512, heads)] = scale_ref[...].reshape(1, heads)
    rest = out_ref[...]
    cuts = []
    for _ in range(3):
        cut = rest.astype(bf).astype(f32)
        cuts.append(cut)
        rest = rest - cut
    cut_ref[...] = jnp.concatenate(cuts + [jnp.zeros_like(rest)], axis=0).astype(bf)
    if len(refs) > 2:
        for c in copies:
            c.wait()


def lines_of(at, table, b1, qv, scale, w1, w2, n):
    feats = b1.shape[0]
    per = w1.shape[0] // n
    fits = per % 16 == 0
    sds = jax.ShapeDtypeStruct
    hbm = [pl.BlockSpec(memory_space=pl.ANY)]
    outs = pl.pallas_call(
        lines_kernel,
        in_specs=[pl.BlockSpec(memory_space=pltpu.SMEM)] + [pl.BlockSpec()] * 4 + hbm * 2 * fits,
        out_specs=[pl.BlockSpec()] * (2 + fits),
        out_shape=[sds((4, feats), f32), sds((16, feats), bf)] + [sds((2, per, w1.shape[1]), bf)] * fits,
        scratch_shapes=[pltpu.SemaphoreType.DMA((2,))] * fits,
        compiler_params=params(LIMIT),
        name="lines",
    )(jnp.reshape(at, (1,)), table, b1, qv, scale, *((w1, w2) if fits else ()))
    if fits:
        return outs
    return *outs, jnp.stack([lax.dynamic_slice_in_dim(w, at * per, per, 0) for w in (w1, w2)])


def bias_kernel(heads, chunks, buckets_ref, small_ref, out_ref):
    rows, cols = buckets_ref.shape
    groups, _, feats = small_ref.shape
    for r in range(0, rows, 8):
        at = pl.ds(r, 8)
        for c in range(cols // LANES):
            lanes = pl.ds(c * LANES, LANES)
            idx = buckets_ref[at, lanes]
            low = idx & (LANES - 1)
            high = idx >> 7
            for h in range(heads):
                got = None
                for k in range(chunks):
                    spot = ((h % 3) * chunks + k) * LANES
                    line = jnp.broadcast_to(
                        small_ref[h // 3, pl.ds(spot // feats, 1), pl.ds(spot % feats, LANES)], (8, LANES)
                    )
                    part = jnp.take_along_axis(line, low, axis=1, mode="promise_in_bounds")
                    got = part if got is None else jnp.where(high == k, part, got)
                out_ref[h, at, lanes] = got


def bias_of(buckets_t, small, heads, size):
    groups, _, feats = small.shape
    seq = buckets_t.shape[0]
    rows = 64
    cost = pl.CostEstimate(flops=COST, bytes_accessed=1 << 20, transcendentals=0)
    return pl.pallas_call(
        functools.partial(bias_kernel, heads * groups, -(-size // LANES)),
        grid=(seq // rows,),
        in_specs=[
            pl.BlockSpec((rows, seq), lambda i: (i, 0)),
            pl.BlockSpec((groups, 4, feats), lambda i: (0, 0, 0)),
        ],
        out_specs=pl.BlockSpec((heads * groups, rows, seq), lambda i: (0, i, 0)),
        out_shape=jax.ShapeDtypeStruct((heads * groups, seq, seq), f32),
        compiler_params=params(30),
        cost_estimate=cost,
        name="pos_bias",
    )(buckets_t, small)


def tiled(v, lanes):
    while v.shape[1] < LANES:
        v = jnp.concatenate([v, v], axis=1)
    return jnp.concatenate([v] * (lanes // v.shape[1]), axis=1)


def head_lanes(shape, head, hd):
    return lax.broadcasted_iota(jnp.int32, shape, 1) // hd == head


def fill_mask(mask, seg_ref, row):
    seq = mask.shape[0]
    line = seg_ref[pl.ds(row, 1), :].astype(f32)
    column = jnp.broadcast_to(line, (8, seq)).T[:, :1]
    for c in range(0, seq, LANES):
        mask[:, pl.ds(c, LANES)] = jnp.where(column == line[:, c : c + LANES], 0.0, masked_score)


def attend_kernel(
    heads, hd, first, x_ref, wt_ref, wl_ref, pos_ref, gw_ref, small_ref, seg_ref, gbias_ref, at_ref,
    qkv_ref, ctx_ref, prob_ref, gate_ref, mask, sc, pr, ctx_t,
):
    group = pl.program_id(0)
    width = heads * hd
    seqs, seq = seg_ref.shape
    gates = gw_ref.shape[0]
    feats = x_ref.shape[1]
    half = gates // 2
    cut = wt_ref.shape[1]
    strips = [pl.ds(c, 2 * LANES) for c in range(0, seq, 2 * LANES)]

    def line(row):
        return pl.ds(row * seq, seq)

    cols = jnp.broadcast_to(small_ref[0, pl.ds(3, 1), pl.ds(0, 512)], (8, 512)).T[:, :1]
    gw = tiled(gw_ref[...].astype(f32), feats)
    mine = [jnp.where(head_lanes(gw.shape, at_ref[first + group] * heads + h, hd), gw, 0.0) for h in range(heads)]
    mine = jnp.concatenate(mine, axis=0).astype(bf)
    bias_a = gbias_ref[0] + gbias_ref[1] + gbias_ref[2] + gbias_ref[3]
    bias_b = gbias_ref[4] + gbias_ref[5] + gbias_ref[6] + gbias_ref[7]
    lins = {}

    def project(row):
        x = x_ref[line(row), :]
        upper = nt(wt_ref[0], x)
        lower = nt(wl_ref[0], x)
        qkv_ref[0, row, pl.ds(0, width), :] = (upper[:width] + cols[:width]).astype(bf) * bf(hd**-0.5)
        qkv_ref[0, row, pl.ds(width, width), :] = upper[width:cut].astype(bf)
        qkv_ref[0, row, pl.ds(2 * width, width), :] = (lower + cols[256 : 256 + width]).astype(bf)
        lins[row] = nt(mine, x)
        fill_mask(mask.at[row], seg_ref, row)

    def score(i):
        row, h = divmod(i, heads)
        k_t = qkv_ref[0, row, pl.ds(width + h * hd, hd), :]
        sc[i % 2] = nn(k_t.T, qkv_ref[0, row, pl.ds(h * hd, hd), :])

    def weigh(i):
        row, h = divmod(i, heads)
        lin = lins[row]
        first = jax.nn.sigmoid(jnp.sum(lin[h * gates : h * gates + half], axis=0, keepdims=True) + bias_a)
        second = jax.nn.sigmoid(jnp.sum(lin[h * gates + half : (h + 1) * gates], axis=0, keepdims=True) + bias_b)
        gate = first * (second * small_ref[0, pl.ds(3, 1), pl.ds(512 + h, 1)] - 1.0) + 2.0
        gate_ref[0, row, pl.ds(h, 1), :] = first
        gate_ref[0, row, pl.ds(heads + h, 1), :] = second
        for at in strips:
            s = sc[i % 2, :, at] + pos_ref[h, :, at] * gate[:, at.start : at.start + at.size] + mask[row, :, at]
            top = jnp.max(s, axis=0, keepdims=True)
            p = jnp.exp(s - top)
            p = p * (1.0 / jnp.sum(p, axis=0, keepdims=True))
            prob_ref[0, row, h, :, at] = p
            pr[i % 2, :, at] = p.astype(bf)

    def gather(i):
        row, h = divmod(i, heads)
        v_t = qkv_ref[0, row, pl.ds(2 * width + h * hd, hd), :]
        ctx_t[pl.ds(h * hd, hd), :] = nn(v_t, pr[i % 2])
        if h == heads - 1:
            ctx_ref[0, line(row), :] = ctx_t[...].T.astype(bf)

    count = seqs * heads
    project(0)
    score(0)
    for i in range(count):
        if i + 1 < count:
            if (i + 1) % heads == 0:
                project((i + 1) // heads)
            score(i + 1)
        weigh(i)
        if i:
            gather(i - 1)
    gather(count - 1)


def back_group(
    heads, hd, own, x_of, w_v, pos_of, gw_ref, small, seqs, seq, head0, qkv_of, prob_of, gate_of, dctx_of, add,
    table_v, finish, dp, pr, ds, wide, ready,
):
    width = heads * hd
    feats = w_v.shape[1]
    strips = [pl.ds(c, 2 * LANES) for c in range(0, seq, 2 * LANES)]
    gw = tiled(gw_ref[...].astype(f32), feats)
    half = gw.shape[0] // 2
    sums = [jnp.sum(gw[:half], axis=0, keepdims=True), jnp.sum(gw[half:], axis=0, keepdims=True)]
    lanes_of = [head_lanes((1, feats), head0 + h, hd) for h in range(heads)]
    gsum = [jnp.where(lanes_of[h], part, 0.0) for part in sums for h in range(heads)]
    w_v[pl.ds(3 * width, 16), :] = jnp.concatenate(gsum + [jnp.zeros((16 - 2 * heads, feats), f32)], axis=0).astype(bf)
    gate_parts = {}

    def score(i):
        row, h = divmod(i, heads)
        if h == 0:
            ready("row", row)
        v_t = qkv_of(row, 2 * width + h * hd, hd)
        dp[i % 2] = nn(v_t.T, dctx_of(row, h * hd, hd))

    def weigh(i):
        row, h = divmod(i, heads)
        if row == 0:
            ready("pos", h)
        ready("prob", i)
        b = i % 2
        first = gate_of(row, h)
        second = gate_of(row, heads + h)
        scale = small[pl.ds(3, 1), pl.ds(512 + h, 1)]
        gate = first * (second * scale - 1.0) + 2.0
        sums_of = []
        for at in strips:
            here = slice(at.start, at.start + at.size)
            pos = pos_of(h, at)
            p = prob_of(row, h, at)
            pr[b, :, at] = p.astype(bf)
            g = dp[b, :, at]
            centre = jnp.sum(p * g, axis=0, keepdims=True)
            low = (p * (g - centre)).astype(bf)
            ds[b, :, at] = low
            d = low.astype(f32)
            sums_of.append(jnp.sum(d * pos, axis=0, keepdims=True))
            if own:
                tab = gate[:, here] * d
                if row == 0:
                    table_v[h, :, at] = tab
                else:
                    table_v[h, :, at] += tab
        if own and row == seqs - 1:
            finish("table", h)
        dgate = jnp.concatenate(sums_of, axis=1)
        dfirst = dgate * (second * scale - 1.0) * first * (1.0 - first)
        dsecond = dgate * first * scale * second * (1.0 - second)
        gate_parts[i] = (dfirst, dsecond, dgate * first * second)

    def gather(i):
        row, h = divmod(i, heads)
        b = i % 2
        q_t = qkv_of(row, h * hd, hd)
        k_t = qkv_of(row, width + h * hd, hd)
        g_t = dctx_of(row, h * hd, hd)
        for j, d in enumerate((nn(k_t, ds[b]) * hd**-0.5, nt(q_t, ds[b]), nt(g_t, pr[b]))):
            wide[row, pl.ds(j * width + h * hd, hd), :] = d.astype(bf)
        if h < heads - 1:
            return
        lines = [gate_parts[row * heads + j][k] for k in (0, 1) for j in range(heads)]
        low = jnp.concatenate(lines + [jnp.zeros((16 - 2 * heads, seq), f32)], axis=0).astype(bf)
        wide[row, pl.ds(3 * width, 16), :] = low
        if row == 0:
            ready("w", 0)
        add(row, nn(wide[row].T, w_v[...]))
        if not own:
            return
        ready("x", row)
        x = x_of(row)
        main = wide[row, pl.ds(0, 3 * width), :]
        dw_here = nn(main, x)
        rest = jnp.concatenate(lines, axis=0) - low[: 2 * heads].astype(f32)
        dgw = nn(low, x)[: 2 * heads] + nn(jnp.concatenate([rest.astype(bf)] * 3, axis=0)[:16], x)[: 2 * heads]
        one = sum(jnp.where(lanes_of[j], dgw[j : j + 1], 0.0) for j in range(heads))
        two = sum(jnp.where(lanes_of[j], dgw[heads + j : heads + j + 1], 0.0) for j in range(heads))
        qv = nt(jnp.ones((8, seq), bf), main)[:1]
        lane = lax.broadcasted_iota(jnp.int32, (1, feats), 1)

        def spot_of(k, v):
            return jnp.where(lane == k, jnp.sum(v, axis=1, keepdims=True), 0.0)

        biases = spot_of(0, sum(lines[:heads])) + spot_of(1, sum(lines[heads:]))
        gains = sum(spot_of(j, gate_parts[row * heads + j][2]) for j in range(heads))
        none = jnp.zeros((1, feats), f32)
        qv = jnp.concatenate([qv, none[:, : feats - qv.shape[1]]], axis=1)
        finish("row", row, dw_here, jnp.concatenate([one, two, biases, none, qv, gains, none, none], axis=0))

    count = seqs * heads
    score(0)
    for i in range(count):
        if i + 1 < count:
            score(i + 1)
        weigh(i)
        if i:
            gather(i - 1)
    gather(count - 1)


def back_own_kernel(
    heads, hd, wt_hbm, wl_hbm, pos_hbm, qkv_hbm, dctx_hbm, base_hbm, x_hbm, prob_hbm,
    gw_ref, small_ref, at_ref, gate_ref,
    grad_hbm, dw_hbm, tiny_ref, table_hbm,
    w_v, pos_v, qkv_v, dctx_v, base_v, dp, pr, ds, wide, dw_v, x_v, table_v, prob_v, sem,
):
    width = heads * hd
    seqs, seq, _ = base_v.shape
    cut = wt_hbm.shape[1]
    count = iter(range(64))

    def line(row):
        return pl.ds(row * seq, seq)

    def copy(src, dst):
        return pltpu.make_async_copy(src, dst, sem.at[next(count)])

    w_in = [
        copy(wt_hbm.at[0], w_v.at[pl.ds(0, cut)]),
        copy(wl_hbm.at[1, pl.ds(0, 3 * width - cut)], w_v.at[pl.ds(cut, 3 * width - cut)]),
    ]
    pos_in = [copy(pos_hbm.at[h], pos_v.at[h]) for h in range(heads)]
    row_in = [[copy(qkv_hbm.at[0, r], qkv_v.at[r]), copy(dctx_hbm.at[0, r], dctx_v.at[r])] for r in range(seqs)]
    prob_in = [copy(prob_hbm.at[0, r, h], prob_v.at[r, h]) for r in range(seqs) for h in range(heads)]
    base_in = [copy(base_hbm.at[line(r)], base_v.at[r]) for r in range(seqs)]
    grad_out = [copy(base_v.at[r], grad_hbm.at[line(r)]) for r in range(seqs)]
    x_in = [copy(x_hbm.at[line(r)], x_v.at[r]) for r in range(seqs)]
    table_out = [copy(table_v.at[h], table_hbm.at[h]) for h in range(heads)]
    dw_out = copy(dw_v, dw_hbm)
    for c in row_in[0] + [prob_in[0], pos_in[0]] + prob_in[1:heads] + pos_in[1:] + row_in[1] + w_in + prob_in[heads:] + base_in + x_in:
        c.start()

    def ready(what, i):
        for c in {"row": lambda: row_in[i], "pos": lambda: [pos_in[i]], "w": lambda: w_in, "x": lambda: [x_in[i]], "prob": lambda: [prob_in[i]]}[what]():
            c.wait()

    def add(row, part):
        base_in[row].wait()
        base_v[row] = deep_alpha * base_v[row] + part
        grad_out[row].start()

    def finish(what, i, *values):
        if what == "table":
            table_out[i].start()
        elif i == 0:
            dw_v[...], tiny_ref[...] = values
        else:
            dw_v[...] += values[0]
            tiny_ref[...] += values[1]
            if i == seqs - 1:
                dw_out.start()

    back_group(
        heads, hd, True, lambda r: x_v[r], w_v, lambda h, at: pos_v[h, :, at], gw_ref, small_ref.at[0], seqs, seq,
        at_ref[0] * heads, lambda r, i, n: qkv_v[r, pl.ds(i, n), :], lambda r, h, at: prob_v[r, h, :, at],
        lambda r, h: gate_ref[0, r, pl.ds(h, 1), :], lambda r, i, n: dctx_v[r, pl.ds(i, n), :], add, table_v, finish,
        dp, pr, ds, wide, ready,
    )
    for c in grad_out + table_out + [dw_out]:
        c.wait()


def back_rest_kernel(
    heads, hd, first, wt_ref, wl_ref, pos_ref, qkv_ref, dctx_ref, base_hbm,
    prob_hbm, gw_ref, small_ref, at_ref, gate_ref,
    grad_hbm,
    w_v, base_v, dp, pr, ds, wide, prob_v, sem, prob_sem,
):
    step = pl.program_id(0)
    last = pl.num_programs(0) - 1
    width = heads * hd
    seqs, seq, _ = base_v.shape
    slot = lax.rem(step, 2)
    cut = wt_ref.shape[1]

    def line(row):
        return pl.ds(row * seq, seq)

    base_in = [pltpu.make_async_copy(base_hbm.at[line(r)], base_v.at[r], sem.at[r]) for r in range(seqs)]
    grad_out = [pltpu.make_async_copy(base_v.at[r], grad_hbm.at[line(r)], sem.at[seqs + r]) for r in range(seqs)]

    def prob_in(at, to, i):
        r, h = divmod(i, heads)
        return pltpu.make_async_copy(prob_hbm.at[first + at, r, h], prob_v.at[to, i], prob_sem.at[to, i])

    @pl.when(step == 0)
    def _():
        for i in range(seqs * heads):
            prob_in(step, slot, i).start()
        for c in base_in:
            c.start()

    @pl.when(step < last)
    def _():
        for i in range(seqs * heads):
            prob_in(step + 1, 1 - slot, i).start()

    def ready(what, i):
        if what == "prob":
            prob_in(step, slot, i).wait()

    w_v[pl.ds(0, cut), :] = wt_ref[0]
    w_v[pl.ds(cut, 3 * width - cut), :] = wl_ref[0]

    def add(row, part):
        @pl.when(step == 0)
        def _():
            base_in[row].wait()

        base_v[row] += part

        @pl.when(step == last)
        def _():
            grad_out[row].start()

    back_group(
        heads, hd, False, None, w_v, lambda h, at: pos_ref[h, :, at], gw_ref, small_ref.at[0], seqs, seq,
        at_ref[1 + first + step] * heads, lambda r, i, n: qkv_ref[0, r, pl.ds(i, n), :],
        lambda r, h, at: prob_v[slot, r * heads + h, :, at],
        lambda r, h: gate_ref[0, r, pl.ds(h, 1), :], lambda r, i, n: dctx_ref[0, r, pl.ds(i, n), :], add, None, None,
        dp, pr, ds, wide, ready,
    )

    @pl.when(step == last)
    def _():
        for c in grad_out:
            c.wait()


def norm_stats(v):
    mean = jnp.mean(v, axis=-1, keepdims=True)
    cen = v - mean
    rs = lax.rsqrt(jnp.mean(cen * cen, axis=-1, keepdims=True) + norm_eps)
    return cen * rs, rs


def norm_back(g, n, rs, gain):
    gn = g * gain
    return rs * (gn - jnp.mean(gn, axis=-1, keepdims=True) - n * jnp.mean(gn * n, axis=-1, keepdims=True))


def gelu_pair(x):
    cdf = 0.5 + 0.5 * lax.erf(x * 0.5**0.5)
    return x * cdf, cdf + x * jnp.exp(x * x * -0.5) * 0.3989422804014327


def weave(*runs):
    runs = list(runs)
    while runs:
        runs = [r for r in runs if next(r, runs) is not runs]


def layer_kernel(
    ctx0_ref, ctx_ref, x_ref, go_ref, ow0_hbm, ow_hbm, w10_hbm, small_ref, smalls_ref,
    w20_hbm, all_hbm, out_bias_ref, gain1_ref, bias1_ref, bias2_ref, gain2_ref, beta2_ref, at_ref,
    out_ref, first_ref, dctx_ref, hid_low_ref, mix_low_ref, first_low_ref, act_ref, pre_low_ref, sums_ref,
    ow_v, w1_v, w2_v, act, slope, plow, wide, scale, acc, own_acc, sem,
):
    step = pl.program_id(0)
    ctxs = [ctx0_ref.at[0]] + [ctx_ref.at[i] for i in range(ctx_ref.shape[0])]
    width = ow0_hbm.shape[0]
    own = w20_hbm.shape[0]
    count = iter(range(128))
    _, pieces, _, per, feats = all_hbm.shape
    chains, rows = act.shape[:2]
    part = 64

    def copy(src, dst):
        return pltpu.make_async_copy(src, dst, sem.at[next(count)])

    ow_in = [copy(ow0_hbm, ow_v.at[pl.ds(0, width)])]
    for i in range(1, len(ctxs)):
        ow_in.append(copy(ow_hbm.at[i - 1, pl.ds(ow_hbm.shape[1] - width, width)], ow_v.at[pl.ds(i * width, width)]))
    w_in = []
    for k, (mine, all_v) in enumerate(((w10_hbm, w1_v), (w20_hbm, w2_v))):
        w_in.append([copy(mine, all_v.at[pl.ds(0, own)])])
        parted = all_v.reshape(len(ctxs) * pieces, per, feats)
        for i in range(1, len(ctxs)):
            w_in[k].append(copy(all_hbm.at[at_ref[i], :, k], parted.at[pl.ds(i * pieces, pieces)]))

    @pl.when(step == 0)
    def _():
        for c in ow_in + w_in[0] + w_in[1]:
            c.start()
        for c in ow_in:
            c.wait()
        acc[...] = jnp.zeros_like(acc)
        own_acc[...] = jnp.zeros_like(own_acc)

    vectors = (out_bias_ref, gain1_ref, bias1_ref, bias2_ref, gain2_ref, beta2_ref)
    out_bias, gain1, bias1, bias2, gain2, beta2 = (ref[...].reshape(1, feats) for ref in vectors)
    b1 = [small_ref[pl.ds(2, 1), :]] + [smalls_ref[i, pl.ds(2, 1), :] for i in range(len(ctxs) - 1)]
    b1 = jnp.concatenate(b1, axis=1)
    block = 256
    blocks = [pl.ds(u, block) for u in range(0, w2_v.shape[0], block)]
    cols = [pl.ds(u, block) for u in range(0, feats, block)]

    def lines(c):
        for r in range(0, rows, part):
            yield pl.ds(r, part), pl.ds(c * rows + r, part)

    def tally(i, v):
        acc[i] += jnp.sum(v.reshape(part // 8, 8, feats), axis=0)

    def enter(c):
        total = nn(ctxs[0][pl.ds(c * rows, rows), :], ow_v[pl.ds(0, width), :])
        for i in range(1, len(ctxs)):
            total = total + nn(ctxs[i][pl.ds(c * rows, rows), :], ow_v[pl.ds(i * width, width), :])
        wide[c, 2] = total
        yield
        for r, at in lines(c):
            n, rs = norm_stats(deep_alpha * x_ref[at, :].astype(f32) + out_bias + wide[c, 2, r, :])
            hidden = n * gain1 + bias1
            wide[c, 0, r, :] = n
            wide[c, 1, r, :] = hidden
            scale[c, r, :] = jnp.broadcast_to(rs, (part, LANES))
            hid_low_ref[at, :] = hidden.astype(bf)
            yield

    def up(c):
        at_rows = pl.ds(c * rows, rows)
        for at in blocks:
            group, inner = divmod(at.start, own)
            pre = nn(hid_low_ref[at_rows, :], w1_v[pl.ds(group * feats, feats), pl.ds(inner, block)])
            pre = pre + b1[:, at.start : at.start + block]
            a, s = gelu_pair(pre)
            act[c, :, at] = a.astype(bf)
            slope[c, :, at] = s
            yield
        act_ref[at_rows, :] = act[c, :, pl.ds(0, own)]

    def down(c):
        for at in cols:
            wide[c, 2, :, at] = nn(act[c], w2_v[:, at])
            yield

    def turn(c):
        for r, at in lines(c):
            n, rs = norm_stats(deep_alpha * wide[c, 1, r, :] + bias2 + wide[c, 2, r, :])
            out_ref[at, :] = n * gain2 + beta2
            g = go_ref[at, :].astype(f32)
            grad = norm_back(g, n, rs, gain2)
            wide[c, 1, r, :] = grad
            mix_low_ref[at, :] = grad.astype(bf)
            tally(0, g * n)
            tally(1, g)
            tally(2, grad)
            yield

    def back_down(c):
        at_rows = pl.ds(c * rows, rows)
        for at in blocks:
            d = nt(mix_low_ref[at_rows, :], w2_v[at, :]) * slope[c, :, at]
            if at.start < own:
                own_acc[:, at] += jnp.sum(d.reshape(rows // 8, 8, block), axis=0)
            plow[c, :, at] = d.astype(bf)
            yield
        pre_low_ref[at_rows, :] = plow[c, :, pl.ds(0, own)]

    def back_up(c):
        for at in cols:
            total = nt(plow[c, :, pl.ds(0, own)], w1_v[at, :])
            for i in range(1, len(ctxs)):
                total = total + nt(plow[c, :, pl.ds(i * own, own)], w1_v[pl.ds(i * feats + at.start, block), :])
            wide[c, 2, :, at] = total
            yield

    def leave(c):
        at_rows = pl.ds(c * rows, rows)
        for r, at in lines(c):
            n = wide[c, 0, r, :]
            grad = deep_alpha * wide[c, 1, r, :] + wide[c, 2, r, :]
            first = norm_back(grad, n, scale[c, r, :1], gain1)
            first_ref[at, :] = first
            first_low_ref[at, :] = first.astype(bf)
            tally(3, grad * n)
            tally(4, grad)
            tally(5, first)
            yield
        dctx = nt(ow_v[...], first_low_ref[at_rows, :]).astype(bf)
        for i in range(len(ctxs)):
            dctx_ref[i, 0, :, at_rows] = dctx[i * width : (i + 1) * width]
        yield

    def wait(which):
        @pl.when(step == 0)
        def _():
            for c in w_in[which]:
                c.wait()

    stages = (enter, up, down, turn, back_down, back_up, leave)
    for t in range(len(stages) + chains - 1):
        if t == 1:
            wait(0)
        if t == 2:
            wait(1)
        weave(*[stages[t - c](c) for c in range(chains) if 0 <= t - c < len(stages)])

    @pl.when(step == pl.num_programs(0) - 1)
    def _():
        rows_of = [jnp.sum(acc[i], axis=0, keepdims=True) for i in range(6)]
        rows_of.append(jnp.sum(own_acc[...], axis=0, keepdims=True))
        sums_ref[...] = jnp.concatenate(rows_of + [jnp.zeros_like(rows_of[0])], axis=0)


def table_kernel(heads, tops, lows, buckets_ref, val_ref, out_ref):
    rows, cols = buckets_ref.shape
    top_id = lax.broadcasted_iota(jnp.int32, (tops, cols), 0)
    low_id = lax.broadcasted_iota(jnp.int32, (lows, cols), 0)
    unroll = 128

    def group(g, acc):
        for u in range(0, unroll, 8):
            at = pl.ds(pl.multiple_of(g * unroll, unroll) + u, 8)
            idx = buckets_ref[at, :]
            high = idx >> 4
            low = idx & 15
            vals = [val_ref[h, at, :] for h in range(heads)]
            for i in range(8):
                a = jnp.where(high[i : i + 1] == top_id, 1.0, 0.0).astype(bf)
                hit = low[i : i + 1] == low_id
                b = jnp.concatenate([jnp.where(hit, v[i : i + 1], 0.0).astype(bf) for v in vals], axis=0)
                acc = acc + nt(a, b)
        return acc

    out_ref[...] = jnp.zeros_like(out_ref)
    out_ref[:, pl.ds(0, heads * lows)] = lax.fori_loop(
        0, rows // unroll, group, jnp.zeros((tops, heads * lows), f32)
    )


def table_grad(buckets_t, values, size, feats):
    heads, seq, _ = values.shape
    lows = 16
    tops = -(-size // lows // 8) * 8
    return pl.pallas_call(
        functools.partial(table_kernel, heads, tops, lows),
        out_shape=jax.ShapeDtypeStruct((tops, feats), f32),
        compiler_params=params(24),
        cost_estimate=pl.CostEstimate(flops=COST, bytes_accessed=1 << 20, transcendentals=0),
        name="table_grad",
    )(buckets_t, values)


def finish_kernel(
    heads, hd, size, core_ref, total_ref, got_ref, big_ref, big_got_ref,
    dw_ref, ow_ref, fc1_ref, fc2_ref, table_ref, gate_ref, qv_ref, gate_bias_ref, scale_ref, *sum_refs,
):
    later = core_ref[0] == 1
    total, got = total_ref[...], got_ref[...]
    first = jnp.where(later, got, total)
    second = jnp.where(later, total, got)
    cut = dw_ref.shape[0] // 2
    dw_ref[pl.ds(0, cut), :] = first[:cut]
    dw_ref[pl.ds(cut, cut), :] = second[:cut]
    extra = jnp.concatenate([first[cut:], second[cut:]], axis=0)
    feats = extra.shape[1]
    width = ow_ref.shape[0]
    for mine in (False, True):
        part = jnp.where(later == mine, big_ref[...], big_got_ref[...]).astype(f32)
        ow_ref[pl.ds(width // 2 * mine, width // 2), :] = part[feats:]
        (fc2_ref if mine else fc1_ref)[...] = part[:feats]
    for i, ref in enumerate(sum_refs):
        ref[...] = extra[i]
    halves = sum(extra[8:10, c : c + LANES] for c in range(0, feats, LANES))
    halves = sum(halves[:, c : c + hd] for c in range(0, LANES, hd))
    gates = gate_ref.shape[0]
    gate_ref[...] = jnp.concatenate([halves[i : i + 1] for i in range(2) for _ in range(gates // 2)], axis=0)
    qv_ref[pl.ds(0, 1), :] = extra[12:13, :width]
    qv_ref[pl.ds(1, 1), :] = extra[12:13, 2 * width : 3 * width]
    lane = lax.broadcasted_iota(jnp.int32, (1, LANES), 1)
    pair = jnp.where(lane < gates // 2, extra[10:11, 0:1], extra[10:11, 1:2])
    gate_bias_ref[...] = pair[:, :gates]
    scale_ref[...] = extra[13:14, :heads]
    lows = 16
    tops = extra.shape[0] - 16
    wide = tops * lows
    spread = lax.broadcasted_iota(jnp.int32, (lows, wide), 1) % lows == lax.broadcasted_iota(jnp.int32, (lows, wide), 0)
    spread = jnp.where(spread, 1.0, 0.0).astype(bf)
    keep = lax.broadcasted_iota(jnp.int32, (tops, wide), 1) // lows == lax.broadcasted_iota(jnp.int32, (tops, wide), 0)
    for h in range(heads):
        rest = extra[16:, h * lows : (h + 1) * lows]
        line = jnp.zeros((tops, wide), f32)
        for _ in range(3):
            part = rest.astype(bf)
            line = line + nn(part, spread)
            rest = rest - part.astype(f32)
        line = jnp.sum(jnp.where(keep, line, 0.0), axis=0, keepdims=True)
        table_ref[pl.ds(h, 1), :] = line[:, :size]


def finish(heads, hd, gates, size, width, units, core, total, got, big, big_got):
    feats = total.shape[1]
    sds = jax.ShapeDtypeStruct
    vector = sds((feats,), f32)
    outs = pl.pallas_call(
        functools.partial(finish_kernel, heads, hd, size),
        in_specs=[pl.BlockSpec(memory_space=pltpu.SMEM)] + [pl.BlockSpec()] * 4,
        out_shape=[
            sds((3 * width, feats), f32), sds((width, feats), f32), sds((feats, units), f32), sds((units, feats), f32),
            sds((heads, size), f32), sds((gates, hd), f32), sds((2, width), f32), sds((1, gates), f32), sds((1, heads), f32),
        ]
        + [vector] * 7,
        compiler_params=params(24),
        name="finish",
    )(core, total, got, big, big_got)
    outs = list(outs)
    outs[7], outs[8] = outs[7][0], outs[8][0]
    return outs


def rotate(x, by, n):
    return lax.ppermute(x, "mp", [(i, (i + by) % n) for i in range(n)])


def swap(x, bit, n, axis="dp"):
    return lax.ppermute(x, axis, [(i, i ^ bit) for i in range(n)])


def after(x, *earlier):
    return lax.optimization_barrier((x,) + earlier)[0]


def joined(pieces, got, bit, index, have):
    at = 1 + sum(b > bit for b in have)
    mine = (index & bit) != 0
    return jnp.stack([jnp.where(mine, got, pieces), jnp.where(mine, pieces, got)], axis=at)


def body(
    n_dp, n_mp,
    tokens, segment_ids, buckets, qkv_weight, qv_bias, rel_table, gate_weight, gate_bias, gate_scale, out_weight,
    out_bias, ln1_gain, ln1_bias, fc1_weight, fc1_bias, fc2_weight, fc2_bias, ln2_gain, ln2_bias, grad_out,
):
    rows, feats = tokens.shape
    seqs, seq = segment_ids.shape
    size, heads = rel_table.shape
    hd, gates = gate_weight.shape
    width = heads * hd
    units = fc1_weight.shape[1]
    me = lax.axis_index("mp")
    dp = lax.axis_index("dp")
    order = ((me - jnp.arange(n_mp)) % n_mp).astype(jnp.int32)
    bits = [1 << i for i in range(n_dp.bit_length() - 1)]
    plane = bits[1:]
    others = n_mp - 1
    core = dp & 1
    sds = jax.ShapeDtypeStruct

    hbm = pl.BlockSpec(memory_space=pl.ANY)
    smem = pl.BlockSpec(memory_space=pltpu.SMEM)
    full = pl.BlockSpec()
    square = pltpu.VMEM((seqs, seq, seq), f32)
    pair = pltpu.VMEM((2, seq, seq), f32)
    low_pair = pltpu.VMEM((2, seq, seq), bf)
    gw = gate_weight.T
    lines_t = pltpu.VMEM((seqs, 3 * width, seq), bf)
    outs_t = pltpu.VMEM((seqs, width, seq), f32)
    tables_t = pltpu.VMEM((heads, seq, seq), f32)

    def one(*shape):
        return pl.BlockSpec((1,) + shape, lambda s: (s,) + (0,) * len(shape))

    def whole(*shape):
        return pl.BlockSpec(shape, lambda s: (0,) * len(shape))

    def attend(n, sources, *deps):
        wt, wl, sm, pos = sources
        return pl.pallas_call(
            functools.partial(attend_kernel, heads, hd, 0 if n == 1 else 1),
            grid=(n,),
            in_specs=[
                whole(rows, feats), one(2 * width, feats),
                pl.BlockSpec((1, width, feats), lambda s: (s + (n == 1), 0, 0)),
                pl.BlockSpec((heads, seq, seq), lambda s: (s, 0, 0)), whole(gates, hd), one(4, feats),
                whole(seqs, seq), smem, smem,
            ],
            out_specs=[one(seqs, 3 * width, seq), one(rows, width), one(seqs, heads, seq, seq), one(seqs, 8, seq)],
            scratch_shapes=[square, pair, low_pair, pltpu.VMEM((width, seq), f32)],
            out_shape=[
                sds((n, seqs, 3 * width, seq), bf), sds((n, rows, width), bf), sds((n, seqs, heads, seq, seq), f32),
                sds((n, seqs, 8, seq), f32),
            ],
            compiler_params=params(LIMIT),
            cost_estimate=pl.CostEstimate(flops=n * COST, bytes_accessed=1 << 20, transcendentals=0),
            name="attend",
        )(tokens, wt, wl, pos, gw, sm, segment_ids, gate_bias, after(order, *deps))

    back_scratch = [pair, low_pair, low_pair, pltpu.VMEM((seqs, 3 * width + 16, seq), bf)]
    w_t = pltpu.VMEM((3 * width + 16, feats), bf)
    base_t = pltpu.VMEM((seqs, seq, feats), f32)

    def back_own(sources, front, dctx, base, *deps):
        wt, wl, sm, pos = sources
        qkv_t, _, prob, gate = front
        return pl.pallas_call(
            functools.partial(back_own_kernel, heads, hd),
            in_specs=[hbm] * 8 + [full] * 2 + [smem, full],
            out_specs=[hbm, hbm, full, hbm],
            scratch_shapes=[w_t, tables_t, lines_t, pltpu.VMEM((seqs, width, seq), bf), base_t]
            + back_scratch
            + [
                pltpu.VMEM((3 * width, feats), f32), pltpu.VMEM((seqs, seq, feats), bf), tables_t,
                pltpu.VMEM((seqs, heads, seq, seq), f32), pltpu.SemaphoreType.DMA((3 + 2 * heads + (5 + heads) * seqs,)),
            ],
            out_shape=[
                sds((rows, feats), f32), sds((3 * width, feats), f32), sds((8, feats), f32), sds((heads, seq, seq), f32),
            ],
            compiler_params=params(LIMIT),
            cost_estimate=pl.CostEstimate(flops=COST, bytes_accessed=1 << 20, transcendentals=0),
            name="attend_back",
        )(wt, wl, pos, qkv_t, dctx, base, tokens, prob, gw, sm, after(order, *deps), gate)

    def back_rest(first, n, sources, front, dctx, base, *deps):
        wt, wl, sm, pos = sources
        qkv_t, _, prob, gate = front

        def off(by, *shape):
            return pl.BlockSpec((1,) + shape, lambda s: (s + by,) + (0,) * len(shape))

        return pl.pallas_call(
            functools.partial(back_rest_kernel, heads, hd, first),
            grid=(n,),
            in_specs=[
                off(first, 2 * width, feats), off(first, width, feats),
                pl.BlockSpec((heads, seq, seq), lambda s: (s + first, 0, 0)), off(first, seqs, 3 * width, seq),
                off(first + 1, seqs, width, seq), hbm, hbm, whole(gates, hd), off(first, 4, feats), smem,
                off(first, seqs, 8, seq),
            ],
            out_specs=hbm,
            scratch_shapes=[w_t, base_t]
            + back_scratch
            + [
                pltpu.VMEM((2, seqs * heads, seq, seq), f32), pltpu.SemaphoreType.DMA((2 * seqs,)),
                pltpu.SemaphoreType.DMA((2, seqs * heads)),
            ],
            out_shape=sds((rows, feats), f32),
            compiler_params=params(48),
            cost_estimate=pl.CostEstimate(flops=n * COST, bytes_accessed=1 << 20, transcendentals=0),
            name="attend_back",
        )(wt, wl, pos, qkv_t, dctx, base, prob, gw, sm, after(order, *deps), gate)

    def piece(w, parts=1):
        per = w.shape[0] // n_dp // parts
        w = w.reshape(parts, n_dp, per, w.shape[1])
        return lax.dynamic_index_in_dim(w, dp, 1, False).reshape(parts * per, -1)

    small, cuts, mine = lines_of(dp, rel_table.T, fc1_bias, qv_bias, gate_scale, fc1_weight, fc2_weight, n_dp)
    gathered = lax.all_gather(mine, ("mp", "dp"))
    w0 = jnp.concatenate([qkv_weight.transpose(0, 2, 1).reshape(3 * width, feats), out_weight], axis=0)
    piece0 = jnp.concatenate([piece(w0, 2), cuts], axis=0)
    w0 = w0.reshape(2, 2 * width, feats)
    z0 = [rotate(piece0, r, n_mp) for r in range(1, n_mp)]
    buckets_t = buckets.T
    pos_own = bias_of(after(buckets_t, piece0), small[None], heads, size)
    z0, pos_own = lax.optimization_barrier((z0, pos_own))
    z0 = jnp.stack(z0)

    mid = 2 * width // n_dp
    got = z0[:, 2 * mid :].astype(f32)
    smalls = (got[:, 0:4] + got[:, 4:8]) + got[:, 8:12]
    own_sources = (w0, w0, small[None], pos_own)
    spreads = [z0[:, :mid], z0[:, mid : 2 * mid]]
    routes = [plane[::-1], plane]
    covers = [lambda *deps: bias_of(after(buckets_t, *deps), smalls, heads, size), lambda *deps: attend(1, own_sources, *deps)]
    done = []
    for step in range(len(plane)):
        gots = [swap(v, route[step], n_dp) for v, route in zip(spreads, routes)]
        if step < len(covers):
            result = covers[step](*spreads)
            gots, result = lax.optimization_barrier((gots, result))
            done.append(result)
        spreads = [joined(v, g, route[step], dp, route[:step]) for v, g, route in zip(spreads, gots, routes)]
    for step in range(len(plane), len(covers)):
        done.append(covers[step]())
    pos_rest, front = done
    gots = [swap(v, 1, n_dp) for v in spreads]
    top, low = (joined(v, g, 1, dp, plane).reshape(others, 2 * width, feats) for v, g in zip(spreads, gots))
    rest_sources = (top, low, smalls, pos_rest)
    fronts = attend(others, rest_sources)
    gathered, fronts = lax.optimization_barrier((gathered, fronts))
    gathered = gathered.reshape(n_mp, n_dp, 2, units // n_dp, feats)
    if units // n_dp % 16:
        gathered = gathered.transpose(0, 2, 1, 3, 4).reshape(n_mp, 1, 2, units, feats)

    tile = 512
    chains = 2

    def row(n):
        return pl.BlockSpec((tile, n), lambda i: (i, 0))

    outs = pl.pallas_call(
        layer_kernel,
        grid=(rows // tile,),
        in_specs=[pl.BlockSpec((n, tile, width), lambda i: (0, i, 0)) for n in (1, others)]
        + [row(feats), row(feats)]
        + [hbm] * 3
        + [full] * 2
        + [hbm] * 2
        + [full] * 6
        + [smem],
        out_specs=[
            row(feats), row(feats), pl.BlockSpec((n_mp, 1, width, tile), lambda i: (0, i * tile // seq, 0, i % (seq // tile))),
            row(feats), row(feats), row(feats), row(units), row(units), pl.BlockSpec((8, feats), lambda i: (0, 0)),
        ],
        scratch_shapes=[
            pltpu.VMEM((n_mp * width, feats), bf), pltpu.VMEM((n_mp * feats, units), bf), pltpu.VMEM((n_mp * units, feats), bf),
            pltpu.VMEM((chains, tile // chains, n_mp * units), bf), pltpu.VMEM((chains, tile // chains, n_mp * units), f32),
            pltpu.VMEM((chains, tile // chains, n_mp * units), bf), pltpu.VMEM((chains, 3, tile // chains, feats), f32),
            pltpu.VMEM((chains, tile // chains, LANES), f32), pltpu.VMEM((6, 8, feats), f32), pltpu.VMEM((8, units), f32),
            pltpu.SemaphoreType.DMA((n_mp + 2 + 2 * others,)),
        ],
        out_shape=[
            sds((rows, feats), f32), sds((rows, feats), f32), sds((n_mp, seqs, width, seq), bf), sds((rows, feats), bf),
            sds((rows, feats), bf), sds((rows, feats), bf), sds((rows, units), bf), sds((rows, units), bf), sds((8, feats), f32),
        ],
        compiler_params=params(LIMIT),
        cost_estimate=pl.CostEstimate(flops=4 * COST, bytes_accessed=1 << 24, transcendentals=0),
        name="layer",
    )(
        front[1], fronts[1], tokens, grad_out, out_weight, low, fc1_weight, small, smalls, fc2_weight, gathered, out_bias, ln1_gain, ln1_bias, fc2_bias, ln2_gain, ln2_bias,
        order,
    )
    normed, grad_first = outs[:2]
    dctx = outs[2]
    hid_low, mix_low, first_low, act_own, pre_own, sums = outs[3:]

    def outer(a, b):
        return lax.dot_general(a, b, (((0,), (0,)), ((), ())), preferred_element_type=f32)

    fc1_part, fc2_part = (outer(a, b).astype(bf) for a, b in ((hid_low, pre_own), (act_own, mix_low)))
    ow_part = outer(front[1][0], first_low).astype(bf).reshape(2, width // 2, feats)
    later = core == 1
    give = [jnp.where(later, fc1_part, fc2_part), jnp.where(later, ow_part[0], ow_part[1])]
    keep = [jnp.where(later, fc2_part, fc1_part), jnp.where(later, ow_part[1], ow_part[0])]
    give, keep = jnp.concatenate(give), jnp.concatenate(keep)
    back, dw, tiny, acc = back_own(own_sources, front, dctx, grad_first, give, keep)
    big = (keep.astype(f32) + swap(give, 1, n_dp).astype(f32)).astype(bf)
    same = [[d for d in range(n_dp) if d % 2 == c] for c in range(2)]
    big = lax.psum_scatter(big, "dp", scatter_dimension=0, tiled=True, axis_index_groups=same)

    shared = tiny
    turned = [rotate(shared, r, n_mp) for r in range(1, n_mp)]
    table = table_grad(after(buckets_t, shared), acc, size, feats)
    table, turned, big = lax.optimization_barrier((table, turned, big))
    route = plane[::-1]
    turned = [shared] + list(turned)
    while len(turned) > 1:
        turned = [a + b for a, b in zip(turned[: len(turned) // 2], turned[len(turned) // 2 :])]
    extra = jnp.concatenate([sums, turned[0][:3], tiny[3:], table], axis=0)
    count = extra.shape[0] // 2

    def parted(flip):
        def pick(v):
            v = v.reshape(2, -1, feats)
            return jnp.where((core == 1) != flip, v[1], v[0])

        return jnp.concatenate([pick(dw), pick(extra)])

    total = parted(False) + swap(parted(True), 1, n_dp)
    cut = dw.shape[0] // 2
    done = 0
    for step, bit in enumerate(plane):
        if step + 1 < len(plane):
            low_part = lax.reduce_precision(total[cut:], 8, 7)
            sent = jnp.concatenate([total[:cut], low_part, total[cut:] - low_part])
            sent = lax.reduce_precision(sent, 8, 7).astype(bf)
            n = 1
        else:
            sent = total
            n = others - done
        got = swap(sent, bit, n_dp)
        big_got = swap(big, route[step], n_dp)
        if done < others:
            back = back_rest(done, n, rest_sources, fronts, dctx, back, sent, big)
            got, big_got, back = lax.optimization_barrier((got, big_got, back))
            done += n
        big = joined(big[None], big_got[None], route[step], dp, route[:step])[0]
        both = sent.astype(f32) + got.astype(f32)
        if step + 1 < len(plane):
            both = jnp.concatenate([both[:cut], both[cut : cut + count] + both[cut + count :]])
        total = both
    got = swap(total, 1, n_dp)
    big = big.reshape(-1, feats)
    big_got = swap(big, 1, n_dp)
    outs = finish(
        heads, hd, gates, size, width, units, jnp.reshape(core, (1,)), total, got, big, big_got
    )
    dw, grad_ow, grad_fc1, grad_fc2, grad_table, grad_gate_weight, dqv_bias, grad_gate_bias, grad_gate_scale = outs[:9]
    sums = outs[9:]
    dw = dw.reshape(3, width, feats).transpose(0, 2, 1)
    grad_table = grad_table.T
    grad_gate_weight = grad_gate_weight.T
    input_grad = back
    return (
        normed, input_grad, dw, dqv_bias, grad_table, grad_gate_weight, grad_gate_bias, grad_gate_scale, grad_ow, sums[5],
        sums[3], sums[4], grad_fc1, sums[6], grad_fc2, sums[2], sums[0], sums[1],
    )


def solution(mesh):
    in_specs = (
        P("dp", None), P("dp", None), P(), P(None, None, "mp"), P(None, "mp"), P(None, "mp"), P(), P(), P("mp"),
        P("mp", None), P(), P(), P(), P(None, "mp"), P("mp"), P("mp", None), P(), P(), P(), P("dp", None),
    )
    out_specs = (
        P("dp", None), P("dp", None), P(None, None, "mp"), P(None, "mp"), P(None, "mp"), P(), P(), P("mp"),
        P("mp", None), P(), P(), P(), P(None, "mp"), P("mp"), P("mp", None), P(), P(), P(),
    )
    fn = functools.partial(body, mesh.shape["dp"], mesh.shape["mp"])
    return jax.shard_map(fn, mesh=mesh, in_specs=in_specs, out_specs=out_specs, check_vma=False)
```
